128 devices in a mesh: space: 16 (over z_lo, y, core), own: 8 (over z_hi, x).
Axes of the slice: x: 4, y: 4, z: 4 (z_hi: 2, z_lo: 2; z = z_hi * 2 + z_lo), core: 2. Of those that a mesh axis runs over, the one named last changes fastest.
Arguments:
- acts: bfloat16 [64, 32, 32, 256], P(None, 'space', 'own'), may hold values from -12 to 12
- cotangents: bfloat16 [64, 32, 32, 256], P(None, 'space', 'own'), may hold values from -12 to 12
- weight_grad: float32 [64, 1728], P(None, 'own'), may hold values from -6 to 6
Outputs:
- preconditioned: float32 [64, 1728], P('own', 'space')
The draws below stay inside these ranges and needn't reach their ends.
All inputs are finite; a program needn't handle non-finite values.
Results may differ from the reference program's by a relative error of at most 0.009.
Values may be sent and summed in bfloat16 or wider, within the bound.
A program may use at most 128 MiB of HBM per device.

```python
import math
import jax
import jax.numpy as jnp
from jax import lax

C_IN = 64
C_OUT = 64
NZ = 256
ITERS = 8
FACTOR = 1728
NX = 32
NY = 32


def scaled_field(key, chans):
    key_scale = jax.random.fold_in(key, 0)
    key_base = jax.random.fold_in(key, 1)
    key_perm = jax.random.fold_in(key, 2)
    key_plane = jax.random.fold_in(key, 5)
    key_phase = jax.random.fold_in(key, 6)
    shape = (chans, NX, NY, NZ)
    scales = jnp.exp(jax.random.uniform(key_scale, (chans, 1, 1, 1), jnp.float32, math.log(0.45), math.log(2.2)))
    low_plane = jnp.exp(jax.random.uniform(key_plane, (1, NX, 1, 1), jnp.float32, math.log(0.35), math.log(0.75)))
    high_plane = jnp.exp(jax.random.uniform(jax.random.fold_in(key_plane, 1), (1, NX, 1, 1), jnp.float32, math.log(1.6), math.log(2.8)))
    phase = jax.random.randint(key_phase, (), 0, 2)
    parity = ((jnp.arange(NX, dtype=jnp.int32) + phase) % 2).reshape(1, NX, 1, 1)
    planes = jnp.where(parity == 1, high_plane, low_plane)
    base = jax.random.truncated_normal(key_base, -4.0, 4.0, shape, jnp.float32)
    smooth = base + 0.8 * jnp.roll(base, 1, 3) + 0.6 * jnp.roll(base, 1, 2) + 0.5 * jnp.roll(base, 1, 1)
    smooth = smooth / 1.5
    order = jax.random.permutation(key_perm, chans)
    mixed = (smooth + 0.5 * smooth[order]) / 1.118
    field = mixed * scales * planes
    return jnp.clip(field, -11.9, 11.9).astype(jnp.bfloat16)


def draw_acts(key, part):
    key = jax.random.fold_in(key, 11)
    return scaled_field(key, C_IN)


def draw_cotangents(key, part):
    key = jax.random.fold_in(key, 23)
    return scaled_field(key, C_OUT)


def level_of(key, dims, cuts, low, high):
    def one(position, blocks):
        heights = jax.random.uniform(jax.random.fold_in(jax.random.fold_in(key, 6), position), (blocks,), jnp.float32, low / len(cuts), high / len(cuts))
        return jnp.repeat(jnp.exp(heights), dims[position] // blocks).reshape((-1,) + (1,) * (len(dims) - position - 1))

    level = one(*cuts[0])
    for cut in cuts[1:]:
        level = level * one(*cut)
    return level


def centred(stream_key, shape, scale, limit, cuts=(), kind=jnp.bfloat16):
    values = jax.random.normal(stream_key, shape, jnp.float32) * scale
    if len(cuts) > 0:
        values = level_of(stream_key, shape, cuts, -0.22, 0.18) * values
    return jnp.clip(values, min=-limit, max=limit).astype(kind)


def setup_inputs(seed: int = 0) -> dict:
    key_list = jax.random.split(jax.random.key(seed), 4)
    return {
        "acts": draw_acts(jax.random.fold_in(key_list[3], 71), 0),
        "cotangents": draw_cotangents(jax.random.fold_in(key_list[3], 71), 0),
        "weight_grad": centred(key_list[2], (C_OUT, FACTOR), 1.0, 6.0, ((1, 8),), jnp.float32),
    }


def patch_plane(padded, xpos, depth_y, depth_z):
    chans = padded.shape[0]
    plane = lax.dynamic_slice_in_dim(padded, xpos, 3, 1)
    pieces = []
    for shift_x in range(3):
        for shift_y in range(3):
            for shift_z in range(3):
                piece = plane[:, shift_x, shift_y:shift_y + depth_y, shift_z:shift_z + depth_z]
                pieces.append(piece.reshape(chans, depth_y * depth_z))
    return jnp.concatenate(pieces, 0)

def reference(acts, cotangents, weight_grad):
    chans, size_x, size_y, size_z = acts.shape
    width = 27 * chans
    c_out = cotangents.shape[0]
    inv_cells = 1.0 / (size_x * size_y * size_z)
    padded = jnp.pad(acts.astype(jnp.float32), ((0, 0), (1, 1), (1, 1), (1, 1)))

    def add_plane(total, xpos):
        block = patch_plane(padded, xpos, size_y, size_z)
        return (total + jnp.dot(block, block.T, precision=lax.Precision.HIGHEST), None)
    gram, _ = lax.scan(add_plane, jnp.zeros((width, width), jnp.float32), jnp.arange(size_x, dtype=jnp.int32))
    a_factor = gram * inv_cells + 0.05 * jnp.eye(width, dtype=jnp.float32)
    frob = jnp.sqrt(jnp.sum(a_factor * a_factor))
    g_flat = cotangents.astype(jnp.float32).reshape(c_out, -1)
    g_factor = jnp.dot(g_flat, g_flat.T, precision=lax.Precision.HIGHEST) * inv_cells + 0.05 * jnp.eye(c_out, dtype=jnp.float32)
    iterate = jnp.eye(width, dtype=jnp.float32) / frob
    for step in range(ITERS):
        image = jnp.dot(a_factor, iterate, precision=lax.Precision.HIGHEST)
        iterate = 2.0 * iterate - jnp.dot(image, iterate, precision=lax.Precision.HIGHEST)
    lower = jnp.linalg.cholesky(g_factor)
    half = lax.linalg.triangular_solve(lower, weight_grad, left_side=True, lower=True)
    solved = lax.linalg.triangular_solve(lower, half, left_side=True, lower=True, transpose_a=True)
    return jnp.dot(solved, iterate, precision=lax.Precision.HIGHEST)
```

```python
import functools

import jax
import jax.numpy as jnp
from jax import lax
from jax.experimental import pallas as pl
from jax.experimental.pallas import tpu as pltpu
from jax.sharding import PartitionSpec as P

SQUARINGS = 4
TILE = 256
damping = 0.05


def padded_2(block, sides, width):
    for axis, dim in sides:
        count = lax.axis_size(axis)
        forward = [(i, i + 1) for i in range(count - 1)]
        backward = [(target, source) for source, target in forward]
        low = lax.ppermute(
            lax.slice_in_dim(block, block.shape[dim] - width, None, axis=dim), axis, forward
        )
        high = lax.ppermute(lax.slice_in_dim(block, 0, width, axis=dim), axis, backward)
        block = jnp.concatenate([low, block, high], axis=dim)
    return block


def patch_slab(padded, xpos, ypos, depth_y, depth_z):
    chans = padded.shape[0]
    zero = jnp.zeros((), jnp.int32)
    slab = lax.dynamic_slice(padded, (zero, xpos, ypos, zero), (chans, 3, depth_y + 2, depth_z + 2))
    pieces = []
    for shift_x in range(3):
        for shift_y in range(3):
            for shift_z in range(3):
                piece = slab[:, shift_x, shift_y : shift_y + depth_y, shift_z : shift_z + depth_z]
                pieces.append(piece.reshape(chans, depth_y * depth_z))
    return jnp.concatenate(pieces, 0)


def gram_block(padded, count, planes, slabs, depth_y, scale):
    width = 27 * padded.shape[0]
    depth_z = padded.shape[3] - 2

    def add_slab(index, total):
        xpos = index // slabs
        ypos = index % slabs * depth_y
        block = patch_slab(padded, xpos, ypos, depth_y, depth_z)
        picked = lax.slice_in_dim(block, 0, count, axis=0)
        return total + lax.dot_general(
            picked, block, (((1,), (1,)), ((), ())), preferred_element_type=jnp.float32
        )

    total = lax.fori_loop(0, planes * slabs, add_slab, jnp.zeros((count, width), jnp.float32))
    return total * scale


def times_factor(factor, row):
    size = factor.shape[0]
    parts = []
    for base in range(0, size, 128):
        rows = factor[pl.ds(base, 128), :].reshape(16, 8, size)
        total = jnp.zeros((16, 8, 128), jnp.float32)
        for lane in range(0, size, 128):
            total = total + rows[:, :, lane : lane + 128] * row[None, :, lane : lane + 128]
        flipped = total.reshape(128, 128).T
        parts.append(jnp.broadcast_to(jnp.sum(flipped, axis=0, keepdims=True), (8, 128)))
    return jnp.concatenate(parts, axis=1)


def halves(value):
    high = value.astype(jnp.bfloat16)
    return high, (value - high.astype(jnp.float32)).astype(jnp.bfloat16)


def poly_kernel(a_hbm, row_ref, out_ref, factor, high, low, sem):
    size = factor.shape[0]
    tiles = size // TILE
    copy = pltpu.make_async_copy(a_hbm, factor, sem)
    copy.start()
    copy.wait()

    def sum_squares(index, total):
        block = factor[pl.ds(pl.multiple_of(index * 32, 32), 32), :]
        return total + jnp.sum((block * block).reshape(4, 8, size), axis=0)

    squares = lax.fori_loop(0, size // 32, sum_squares, jnp.zeros((8, size), jnp.float32))
    inverse = 1.0 / jnp.sqrt(jnp.sum(squares, keepdims=True))

    def scale(index, carry):
        here = pl.ds(pl.multiple_of(index * 32, 32), 32)
        block = factor[here, :] * inverse
        factor[here, :] = block
        high[0, here, :], low[0, here, :] = halves(block)
        return carry

    lax.fori_loop(0, size // 32, scale, 0)
    row = jnp.broadcast_to(row_ref[...], (8, size)) * inverse
    for step in range(SQUARINGS):
        now, later = step % 2, 1 - step % 2
        row = 2.0 * row - times_factor(factor, row)

        def row_tile(i, carry, now=now, later=later, last=step == SQUARINGS - 1):
            rows = pl.ds(pl.multiple_of(i * TILE, TILE), TILE)
            left_high, left_low = high[now, rows, :], low[now, rows, :]
            for apart in range((tiles + 1) // 2):
                j = lax.rem(i + apart, tiles)
                cols = pl.ds(pl.multiple_of(j * TILE, TILE), TILE)
                right_high, right_low = high[now, :, cols], low[now, :, cols]
                dot = functools.partial(jnp.dot, preferred_element_type=jnp.float32)
                square = dot(left_high, right_high) + (dot(left_high, right_low) + dot(left_low, right_high))
                fresh = 2.0 * factor[rows, cols] - square
                factor[rows, cols] = fresh
                flipped = fresh.T
                if apart:
                    factor[cols, rows] = flipped
                if not last:
                    high[later, rows, cols], low[later, rows, cols] = halves(fresh)
                    if apart:
                        high[later, cols, rows], low[later, cols, rows] = halves(flipped)
            return carry

        lax.fori_loop(0, tiles, row_tile, 0)

    def horner(index, value):
        return row + (value - times_factor(factor, value))

    value = lax.fori_loop(0, 2 ** (8 - SQUARINGS) - 1, horner, row)
    out_ref[...] = value[:1]


def polynomial(a_padded, row):
    size = a_padded.shape[0]
    return pl.pallas_call(
        poly_kernel,
        out_shape=jax.ShapeDtypeStruct((1, size), jnp.float32),
        in_specs=[pl.BlockSpec(memory_space=pl.ANY), pl.BlockSpec(memory_space=pltpu.VMEM)],
        out_specs=pl.BlockSpec(memory_space=pltpu.VMEM),
        scratch_shapes=[
            pltpu.VMEM((size, size), jnp.float32),
            pltpu.VMEM((2, size, size), jnp.bfloat16),
            pltpu.VMEM((2, size, size), jnp.bfloat16),
            pltpu.SemaphoreType.DMA,
        ],
        compiler_params=pltpu.CompilerParams(vmem_limit_bytes=56 * 2**20),
    )(a_padded, row)


def body(acts, cotangents, weight_grad):
    chans, block_x, block_y, depth_z = acts.shape
    c_out = cotangents.shape[0]
    width = 27 * chans
    n_space = lax.axis_size("space")
    n_own = lax.axis_size("own")
    row_len = width // n_own
    col_len = width // n_space
    own_idx = lax.axis_index("own")
    space_idx = lax.axis_index("space")
    inv_cells = 1.0 / (block_x * n_space * block_y * n_own * depth_z)
    framed_x = padded_2(acts, (("space", 1),), 1)
    framed = padded_2(framed_x, (("own", 2),), 1)
    padded = jnp.pad(framed, ((0, 0), (0, 0), (0, 0), (1, 1)))
    owned = lax.psum_scatter(
        gram_block(padded, width, block_x, 1, block_y, inv_cells),
        "own",
        scatter_dimension=0,
        tiled=True,
    )
    factor_rows = lax.psum(owned, "space")
    factor = lax.all_gather(factor_rows, "own", axis=0, tiled=True)
    factor = factor + damping * jnp.eye(width, dtype=jnp.float32)
    size = -(-width // TILE) * TILE
    factor = jnp.pad(factor, ((0, size - width), (0, size - width)))
    g_flat = cotangents.reshape(c_out, -1)
    g_part = (
        lax.dot_general(
            g_flat, g_flat, (((1,), (1,)), ((), ())), preferred_element_type=jnp.float32
        )
        * inv_cells
    )
    g_total = lax.psum(g_part, ("space", "own"))
    g_factor = g_total + damping * jnp.eye(c_out, dtype=jnp.float32)
    grads = lax.all_gather(weight_grad, "own", axis=1, tiled=True)
    lower = jnp.linalg.cholesky(g_factor)
    half = lax.linalg.triangular_solve(lower, grads, left_side=True, lower=True)
    solved = lax.linalg.triangular_solve(lower, half, left_side=True, lower=True, transpose_a=True)
    rows = c_out // n_own
    sharing = n_space // rows
    mine = own_idx * rows + space_idx // sharing
    row = lax.dynamic_slice_in_dim(solved, mine, 1, 0)
    row = jnp.pad(row, ((0, 0), (0, size - width)))
    done = polynomial(factor, row)[:, :width].reshape(n_space, col_len)
    spread = lax.all_to_all(done, "space", split_axis=0, concat_axis=0, tiled=True)
    return spread.reshape(rows, sharing, col_len)[:, 0]


def solution(mesh):
    in_specs = (P(None, "space", "own", None), P(None, "space", "own", None), P(None, "own"))
    out_specs = P("own", "space")
    return jax.shard_map(body, mesh=mesh, in_specs=in_specs, out_specs=out_specs, check_vma=False)
```

```python
import functools

import jax
import jax.numpy as jnp
from jax import lax
from jax.experimental import pallas as pl
from jax.experimental.pallas import tpu as pltpu
from jax.sharding import PartitionSpec as P

SQUARINGS = 3
TILE = 256
CH = 64
NZ = 256
damping = 0.05
MESH = pl.DeviceIdType.MESH
SAME = ((0, 0), (1, 1), (2, 2))
UP = ((0, 1), (0, 2))
DOWN = ((1, 0), (2, 0))


def pair_type(first, second):
    if first == second:
        return (first, second)
    apart = second - first
    return (0, apart) if apart > 0 else (-apart, 0)


def distinct_pairs():
    pairs = []
    for x_pair in SAME + UP:
        for y_pair in SAME + UP + (DOWN if x_pair in UP else ()):
            full = x_pair in UP or y_pair in UP
            pairs.append((x_pair, y_pair, SAME + UP + (DOWN if full else ())))
    return pairs


PAIRS = distinct_pairs()
SLOTS = {}
for _x_pair, _y_pair, _z_pairs in PAIRS:
    for _z_pair in _z_pairs:
        SLOTS[(_x_pair, _y_pair, _z_pair)] = len(SLOTS)
G_SLOT = len(SLOTS)
N_SLOTS = 192
ROWS = N_SLOTS // 2 * CH


def slot_place(slot):
    return slice(slot // 2 * CH, slot // 2 * CH + CH), slice(slot % 2 * CH, slot % 2 * CH + CH)


def block_slot(row, col):
    return SLOTS[
        tuple(
            pair_type(row // unit % 3, col // unit % 3) for unit in (9, 3, 1)
        )
    ]


def meet(peers):
    barrier = pltpu.get_barrier_semaphore()
    for peer in peers:
        pl.semaphore_signal(barrier, inc=1, device_id=peer, device_id_type=MESH)
    pl.semaphore_wait(barrier, len(peers))


def halo_kernel(base, ext, send_sem, recv_sem):
    space, own = lax.axis_index("space"), lax.axis_index("own")
    n_space, n_own = lax.axis_size("space"), lax.axis_size("own")
    planes, lines = base.shape[0], base.shape[1]
    ext[1 : 1 + planes, 1 : 1 + lines] = base[...]
    steps = [(dx, dy) for dx in (-1, 0, 1) for dy in (-1, 0, 1) if dx or dy]
    peers = [
        {"space": lax.rem(space + dx + n_space, n_space), "own": lax.rem(own + dy + n_own, n_own)}
        for dx, dy in steps
    ]
    meet(peers)

    def ends(step, count):
        if step == 0:
            return pl.ds(1, count), pl.ds(1, count)
        return (pl.ds(count, 1), pl.ds(0, 1)) if step > 0 else (pl.ds(1, 1), pl.ds(count + 1, 1))

    copies = []
    for index, (dx, dy) in enumerate(steps):
        from_x, to_x = ends(dx, planes)
        from_y, to_y = ends(dy, lines)
        copy = pltpu.make_async_remote_copy(
            src_ref=ext.at[from_x, from_y],
            dst_ref=ext.at[to_x, to_y],
            send_sem=send_sem.at[index],
            recv_sem=recv_sem.at[index],
            device_id=peers[index],
            device_id_type=MESH,
        )
        copy.start()
        copies.append(copy)
    for copy in copies:
        copy.wait()

    @pl.when(space == 0)
    def _():
        ext[0] = jnp.zeros_like(ext[0])

    @pl.when(space == n_space - 1)
    def _():
        ext[planes + 1] = jnp.zeros_like(ext[0])

    @pl.when(own == 0)
    def _():
        ext[:, 0] = jnp.zeros_like(ext[:, 0])

    @pl.when(own == n_own - 1)
    def _():
        ext[:, lines + 1] = jnp.zeros_like(ext[:, 0])


def with_halo(base):
    planes, lines, chans, depth = base.shape
    return pl.pallas_call(
        halo_kernel,
        out_shape=jax.ShapeDtypeStruct((planes + 2, lines + 2, chans, depth), base.dtype),
        in_specs=[pl.BlockSpec(memory_space=pltpu.VMEM)],
        out_specs=pl.BlockSpec(memory_space=pltpu.VMEM),
        scratch_shapes=[pltpu.SemaphoreType.DMA((8,)), pltpu.SemaphoreType.DMA((8,))],
        compiler_params=pltpu.CompilerParams(
            collective_id=0, has_side_effects=True, vmem_limit_bytes=32 * 2**20
        ),
    )(base)


def gram_kernel(ext, cots, out, left, right):
    planes, lines, chans, depth = ext.shape
    lane = lax.broadcasted_iota(jnp.int32, (chans, depth), 1)

    def shift_plane(xpos, carry):
        for ypos in range(lines):
            here = ext[xpos, ypos].astype(jnp.float32)
            before = jnp.where(lane == 0, 0.0, pltpu.roll(here, 1, 1))
            after = jnp.where(lane == depth - 1, 0.0, pltpu.roll(here, depth - 1, 1))
            stack = jnp.concatenate([before, here, after], axis=0)
            across = slice(ypos * depth, (ypos + 1) * depth)
            left[xpos, :, across] = stack.astype(left.dtype)
            right[xpos, across, :] = stack.T.astype(right.dtype)
        return carry

    lax.fori_loop(0, planes, shift_plane, 0)
    run = (lines - 2) * depth
    for x_pair, y_pair, z_pairs in PAIRS:
        total = None
        for xpos in range(planes - 2):
            term = jnp.dot(
                left[xpos + x_pair[0], :, y_pair[0] * depth : y_pair[0] * depth + run],
                right[xpos + x_pair[1], y_pair[1] * depth : y_pair[1] * depth + run, :],
                preferred_element_type=jnp.float32,
            )
            total = term if total is None else total + term
        for z_pair in z_pairs:
            block = total[z_pair[0] * chans : (z_pair[0] + 1) * chans, z_pair[1] * chans : (z_pair[1] + 1) * chans]
            out[slot_place(SLOTS[(x_pair, y_pair, z_pair)])] = block
    out[slot_place(G_SLOT)] = lax.dot_general(
        cots[...], cots[...], (((1,), (1,)), ((), ())), preferred_element_type=jnp.float32
    )
    for slot in range(G_SLOT + 1, N_SLOTS):
        out[slot_place(slot)] = jnp.zeros((chans, chans), jnp.float32)


def gram_terms(ext, cots):
    planes, lines, chans, depth = ext.shape
    vmem = pl.BlockSpec(memory_space=pltpu.VMEM)
    return pl.pallas_call(
        gram_kernel,
        out_shape=jax.ShapeDtypeStruct((ROWS, 2 * CH), jnp.float32),
        in_specs=[vmem, vmem],
        out_specs=vmem,
        scratch_shapes=[
            pltpu.VMEM((planes, 3 * chans, lines * depth), jnp.bfloat16),
            pltpu.VMEM((planes, lines * depth, 3 * chans), jnp.bfloat16),
        ],
        compiler_params=pltpu.CompilerParams(vmem_limit_bytes=48 * 2**20),
    )(ext, cots)


HALF = ROWS // 2
PART = HALF // 3
SIZES = (PART // 4, PART // 16, PART // 64)


def reduce_kernel(
    terms, full, half, from_core, sums_1, sums_2, sums_3, came_1, came_2, came_3,
    core_send, core_recv, ring_send, ring_recv, back_send, back_recv, last_send, last_recv,
):
    space, own = lax.axis_index("space"), lax.axis_index("own")
    core, ypos, z_lo = lax.rem(space, 2), lax.rem(space // 2, 4), space // 8
    xpos, z_hi = lax.rem(own, 4), own // 4
    coords = (xpos, ypos, z_hi * 2 + z_lo)

    def peer(axis, coord):
        if axis == 0:
            return {"space": space, "own": own - xpos + coord}
        if axis == 1:
            return {"space": space + 2 * (coord - ypos), "own": own}
        return {"space": space + 8 * (lax.rem(coord, 2) - z_lo), "own": coord // 2 * 4 + xpos}

    partner = {"space": space + 1 - 2 * core, "own": own}
    ring = {
        (axis, step): peer(axis, lax.rem(coords[axis] + step, 4)) for axis in range(3) for step in (1, 2, 3)
    }
    meet([partner] + list(ring.values()))

    def rows(start, count):
        return pl.ds(pl.multiple_of(start, 8), count)

    def send(src, dst, send_sem, recv_sem, device):
        copy = pltpu.make_async_remote_copy(
            src_ref=src, dst_ref=dst, send_sem=send_sem, recv_sem=recv_sem, device_id=device, device_id_type=MESH
        )
        copy.start()
        return copy

    waiting = []
    to_core = [
        send(
            terms.at[rows((1 - core) * HALF + part * PART, PART)],
            from_core.at[rows(part * PART, PART)],
            core_send.at[part], core_recv.at[part], partner,
        )
        for part in range(3)
    ]
    waiting += to_core
    levels = (half, sums_1, sums_2, sums_3)
    came = (came_1, came_2, came_3)
    flights = {}

    def scatter(level, part):
        axis, count = (part + level) % 3, SIZES[level]
        for step in (1, 2, 3):
            target = lax.rem(coords[axis] + step, 4)
            slot = part * 3 + step - 1
            flights[(level, part, step)] = send(
                levels[level].at[rows(part * count * 4 + target * count, count)],
                came[level].at[rows(slot * count, count)],
                ring_send.at[level * 9 + slot], ring_recv.at[level * 9 + slot], ring[(axis, step)],
            )
            waiting.append(flights[(level, part, step)])

    def collect(level, part):
        axis, count = (part + level) % 3, SIZES[level]
        total = levels[level][rows(part * count * 4 + coords[axis] * count, count), :]
        for step in (1, 2, 3):
            flights[(level, part, step)].wait_recv()
            total = total + came[level][rows((part * 3 + step - 1) * count, count), :]
        levels[level + 1][rows(part * count, count), :] = total

    for part in range(3):
        to_core[part].wait_recv()
        here = rows(part * PART, PART)
        half[here, :] = terms[rows(core * HALF + part * PART, PART), :] + from_core[here, :]
        scatter(0, part)
    for level in range(3):
        for part in range(3):
            collect(level, part)
            if level < 2:
                scatter(level + 1, part)

    def base(level, part):
        start = core * HALF + part * PART
        for outer in range(level):
            start = start + coords[(part + outer) % 3] * SIZES[outer]
        return start

    back = {}

    def spread(level, part):
        axis, count = (part + level) % 3, SIZES[level]
        here = rows(base(level, part) + coords[axis] * count, count)
        for step in (1, 2, 3):
            slot = level * 9 + part * 3 + step - 1
            back[(level, part, step)] = send(
                full.at[here], full.at[here], back_send.at[slot], back_recv.at[slot], ring[(axis, step)]
            )
            waiting.append(back[(level, part, step)])

    for part in range(3):
        here = rows(base(3, part), SIZES[2])
        full[here, :] = sums_3[rows(part * SIZES[2], SIZES[2]), :]
        spread(2, part)
    for level in (2, 1, 0):
        for part in range(3):
            for step in (1, 2, 3):
                back[(level, part, step)].wait_recv()
            if level:
                spread(level - 1, part)
            else:
                here = rows(core * HALF + part * PART, PART)
                back[(part,)] = send(full.at[here], full.at[here], last_send.at[part], last_recv.at[part], partner)
                waiting.append(back[(part,)])
    for part in range(3):
        back[(part,)].wait_recv()
    for copy in waiting:
        copy.wait_send()


def reduced(terms):
    vmem = pl.BlockSpec(memory_space=pltpu.VMEM)
    lanes = terms.shape[1]
    buffers = [HALF, HALF] + [3 * count for count in SIZES] + [9 * count for count in SIZES]
    dma = pltpu.SemaphoreType.DMA
    return pl.pallas_call(
        reduce_kernel,
        out_shape=jax.ShapeDtypeStruct(terms.shape, terms.dtype),
        in_specs=[vmem],
        out_specs=vmem,
        scratch_shapes=[pltpu.VMEM((count, lanes), terms.dtype) for count in buffers]
        + [dma((count,)) for count in (3, 3, 27, 27, 27, 27, 3, 3)],
        compiler_params=pltpu.CompilerParams(
            collective_id=1, has_side_effects=True, vmem_limit_bytes=48 * 2**20
        ),
    )(terms)


def times_factor(factor, row):
    size = factor.shape[0]
    parts = []
    for base in range(0, size, 128):
        rows = factor[pl.ds(base, 128), :].reshape(16, 8, size)
        total = jnp.zeros((16, 8, 128), jnp.float32)
        for lane in range(0, size, 128):
            total = total + rows[:, :, lane : lane + 128] * row[None, :, lane : lane + 128]
        flipped = total.reshape(128, 128).T
        parts.append(jnp.broadcast_to(jnp.sum(flipped, axis=0, keepdims=True), (8, 128)))
    return jnp.concatenate(parts, axis=1)


def halves(value):
    high = value.astype(jnp.bfloat16)
    return high, (value - high.astype(jnp.float32)).astype(jnp.bfloat16)


def assemble(full, factor, inv_cells):
    size = factor.shape[0]
    blocks = 27
    factor[blocks * CH :, :] = jnp.zeros((size - blocks * CH, size), jnp.float32)
    factor[:, blocks * CH :] = jnp.zeros((size, size - blocks * CH), jnp.float32)
    eye = jnp.where(
        lax.broadcasted_iota(jnp.int32, (CH, CH), 0) == lax.broadcasted_iota(jnp.int32, (CH, CH), 1), damping, 0.0
    )
    for row in range(blocks):
        for col in range(row, blocks):
            block = full[slot_place(block_slot(row, col))] * inv_cells
            if row == col:
                block = block + eye
            factor[row * CH : (row + 1) * CH, col * CH : (col + 1) * CH] = block
            if row != col and row * CH // TILE == col * CH // TILE:
                factor[col * CH : (col + 1) * CH, row * CH : (row + 1) * CH] = block.T
    tiles = size // TILE
    for row in range(tiles):
        for col in range(row + 1, tiles):
            rows, cols = slice(row * TILE, (row + 1) * TILE), slice(col * TILE, (col + 1) * TILE)
            factor[cols, rows] = factor[rows, cols].T


def poly_kernel(inv_cells, full, row_ref, out_ref, factor, high_a, low_a, high_b, low_b):
    size = factor.shape[0]
    tiles = size // TILE
    assemble(full, factor, inv_cells)

    def sum_squares(index, total):
        block = factor[pl.ds(pl.multiple_of(index * 32, 32), 32), :]
        return total + jnp.sum((block * block).reshape(4, 8, size), axis=0)

    squares = lax.fori_loop(0, size // 32, sum_squares, jnp.zeros((8, size), jnp.float32))
    inverse = 1.0 / jnp.sqrt(jnp.sum(squares, keepdims=True))

    def scale(index, carry):
        here = pl.ds(pl.multiple_of(index * 32, 32), 32)
        block = factor[here, :] * inverse
        factor[here, :] = block
        high_a[here, :], low_a[here, :] = halves(block)
        return carry

    lax.fori_loop(0, size // 32, scale, 0)
    row = jnp.broadcast_to(row_ref[...], (8, size)) * inverse
    dot = functools.partial(jnp.dot, preferred_element_type=jnp.float32)
    operands = ((high_a, low_a), (high_b, low_b))
    for step in range(SQUARINGS):
        (high, low), (next_high, next_low) = operands[step % 2], operands[1 - step % 2]
        row = 2.0 * row - times_factor(factor, row)

        def row_tile(i, carry, high=high, low=low, next_high=next_high, next_low=next_low, step=step):
            rows = pl.ds(pl.multiple_of(i * TILE, TILE), TILE)
            left_high, left_low = high[rows, :], low[rows, :]
            for apart in range((tiles + 1) // 2):
                j = lax.rem(i + apart, tiles)
                cols = pl.ds(pl.multiple_of(j * TILE, TILE), TILE)
                right_high, right_low = high[:, cols], low[:, cols]
                square = dot(left_high, right_high) + (dot(left_high, right_low) + dot(left_low, right_high))
                fresh = 2.0 * factor[rows, cols] - square
                factor[rows, cols] = fresh
                flipped = fresh.T
                if apart:
                    factor[cols, rows] = flipped
                if step < SQUARINGS - 1:
                    next_high[rows, cols], next_low[rows, cols] = halves(fresh)
                    if apart:
                        next_high[cols, rows], next_low[cols, rows] = halves(flipped)
            return carry

        lax.fori_loop(0, tiles, row_tile, 0)

    def horner(index, value):
        return row + (value - times_factor(factor, value))

    value = lax.fori_loop(0, 2 ** (8 - SQUARINGS) - 1, horner, row)
    out_ref[...] = value[:1]


def polynomial(full, row, inv_cells):
    size = row.shape[1]
    vmem = pl.BlockSpec(memory_space=pltpu.VMEM)
    return pl.pallas_call(
        functools.partial(poly_kernel, inv_cells),
        out_shape=jax.ShapeDtypeStruct((1, size), jnp.float32),
        in_specs=[vmem, vmem],
        out_specs=vmem,
        scratch_shapes=[pltpu.VMEM((size, size), jnp.float32)] + [pltpu.VMEM((size, size), jnp.bfloat16)] * 4,
        compiler_params=pltpu.CompilerParams(vmem_limit_bytes=56 * 2**20),
    )(full, row)


def body(acts, cotangents, weight_grad):
    chans, block_x, block_y, depth_z = acts.shape
    c_out = cotangents.shape[0]
    width = 27 * chans
    n_space = lax.axis_size("space")
    n_own = lax.axis_size("own")
    col_len = width // n_space
    own_idx = lax.axis_index("own")
    space_idx = lax.axis_index("space")
    inv_cells = 1.0 / (block_x * n_space * block_y * n_own * depth_z)
    size = -(-width // TILE) * TILE
    ext = with_halo(jnp.transpose(acts, (1, 2, 0, 3)))
    full = reduced(gram_terms(ext, cotangents.reshape(c_out, -1)))
    g_total = full[slot_place(G_SLOT)] * inv_cells
    g_factor = g_total + damping * jnp.eye(c_out, dtype=jnp.float32)
    grads = lax.all_gather(weight_grad, "own", axis=1, tiled=True)
    lower = jnp.linalg.cholesky(g_factor)
    half = lax.linalg.triangular_solve(lower, grads, left_side=True, lower=True)
    solved = lax.linalg.triangular_solve(lower, half, left_side=True, lower=True, transpose_a=True)
    rows = c_out // n_own
    sharing = n_space // rows
    mine = own_idx * rows + space_idx // sharing
    row = lax.dynamic_slice_in_dim(solved, mine, 1, 0)
    row = jnp.pad(row, ((0, 0), (0, size - width)))
    done = polynomial(full, row, inv_cells)[:, :width].reshape(n_space, col_len)
    spread = lax.all_to_all(done, "space", split_axis=0, concat_axis=0, tiled=True)
    return spread.reshape(rows, sharing, col_len)[:, 0]


def solution(mesh):
    in_specs = (P(None, "space", "own", None), P(None, "space", "own", None), P(None, "own"))
    out_specs = P("own", "space")
    return jax.shard_map(body, mesh=mesh, in_specs=in_specs, out_specs=out_specs, check_vma=False)
```

```python
import functools

import jax
import jax.numpy as jnp
from jax import lax
from jax.experimental import pallas as pl
from jax.experimental.pallas import tpu as pltpu
from jax.sharding import PartitionSpec as P

SQUARINGS = 3
TILE = 256
CH = 64
NZ = 256
damping = 0.05
MESH = pl.DeviceIdType.MESH
SAME = ((0, 0), (1, 1), (2, 2))
UP = ((0, 1), (0, 2))
DOWN = ((1, 0), (2, 0))


def pair_type(first, second):
    if first == second:
        return (first, second)
    apart = second - first
    return (0, apart) if apart > 0 else (-apart, 0)


def distinct_pairs():
    pairs = []
    for x_pair in SAME + UP:
        for y_pair in SAME + UP + (DOWN if x_pair in UP else ()):
            full = x_pair in UP or y_pair in UP
            pairs.append((x_pair, y_pair, SAME + UP + (DOWN if full else ())))
    return pairs


PAIRS = distinct_pairs()
SLOTS = {}
for _x_pair, _y_pair, _z_pairs in PAIRS:
    for _z_pair in _z_pairs:
        SLOTS[(_x_pair, _y_pair, _z_pair)] = len(SLOTS)
N_SLOTS = 192
ROWS = N_SLOTS // 2 * CH


def slot_place(slot):
    return slice(slot // 2 * CH, slot // 2 * CH + CH), slice(slot % 2 * CH, slot % 2 * CH + CH)


def block_slot(row, col):
    return SLOTS[
        tuple(
            pair_type(row // unit % 3, col // unit % 3) for unit in (9, 3, 1)
        )
    ]


DIAGONAL = {block_slot(index, index) for index in range(27)}


def meet(peers):
    barrier = pltpu.get_barrier_semaphore()
    for peer in peers:
        pl.semaphore_signal(barrier, inc=1, device_id=peer, device_id_type=MESH)
    pl.semaphore_wait(barrier, len(peers))


def halo_kernel(base, ext, send_sem, recv_sem):
    space, own = lax.axis_index("space"), lax.axis_index("own")
    n_space, n_own = lax.axis_size("space"), lax.axis_size("own")
    planes, lines = base.shape[0], base.shape[1]
    ext[1 : 1 + planes, 1 : 1 + lines] = base[...]
    steps = [(dx, dy) for dx in (-1, 0, 1) for dy in (-1, 0, 1) if dx or dy]
    peers = [
        {"space": lax.rem(space + dx + n_space, n_space), "own": lax.rem(own + dy + n_own, n_own)}
        for dx, dy in steps
    ]
    meet(peers)

    def ends(step, count):
        if step == 0:
            return pl.ds(1, count), pl.ds(1, count)
        return (pl.ds(count, 1), pl.ds(0, 1)) if step > 0 else (pl.ds(1, 1), pl.ds(count + 1, 1))

    copies = []
    for index, (dx, dy) in enumerate(steps):
        from_x, to_x = ends(dx, planes)
        from_y, to_y = ends(dy, lines)
        copy = pltpu.make_async_remote_copy(
            src_ref=ext.at[from_x, from_y],
            dst_ref=ext.at[to_x, to_y],
            send_sem=send_sem.at[index],
            recv_sem=recv_sem.at[index],
            device_id=peers[index],
            device_id_type=MESH,
        )
        copy.start()
        copies.append(copy)
    for copy in copies:
        copy.wait()

    @pl.when(space == 0)
    def _():
        ext[0] = jnp.zeros_like(ext[0])

    @pl.when(space == n_space - 1)
    def _():
        ext[planes + 1] = jnp.zeros_like(ext[0])

    @pl.when(own == 0)
    def _():
        ext[:, 0] = jnp.zeros_like(ext[:, 0])

    @pl.when(own == n_own - 1)
    def _():
        ext[:, lines + 1] = jnp.zeros_like(ext[:, 0])


def with_halo(base):
    planes, lines, chans, depth = base.shape
    return pl.pallas_call(
        halo_kernel,
        out_shape=jax.ShapeDtypeStruct((planes + 2, lines + 2, chans, depth), base.dtype),
        in_specs=[pl.BlockSpec(memory_space=pltpu.VMEM)],
        out_specs=pl.BlockSpec(memory_space=pltpu.VMEM),
        scratch_shapes=[pltpu.SemaphoreType.DMA((8,)), pltpu.SemaphoreType.DMA((8,))],
        compiler_params=pltpu.CompilerParams(
            collective_id=0, has_side_effects=True, vmem_limit_bytes=32 * 2**20
        ),
    )(base)


def gram_kernel(ext, cots, out, out_g, left, right):
    planes, lines, chans, depth = ext.shape
    lane = lax.broadcasted_iota(jnp.int32, (chans, depth), 1)

    def shift_plane(xpos, carry):
        for ypos in range(lines):
            here = ext[xpos, ypos].astype(jnp.float32)
            before = jnp.where(lane == 0, 0.0, pltpu.roll(here, 1, 1))
            after = jnp.where(lane == depth - 1, 0.0, pltpu.roll(here, depth - 1, 1))
            stack = jnp.concatenate([before, here, after], axis=0)
            across = slice(ypos * depth, (ypos + 1) * depth)
            left[xpos, :, across] = stack.astype(left.dtype)
            right[xpos, across, :] = stack.T.astype(right.dtype)
        return carry

    lax.fori_loop(0, planes, shift_plane, 0)
    run = (lines - 2) * depth
    for x_pair, y_pair, z_pairs in PAIRS:
        total = None
        for xpos in range(planes - 2):
            term = jnp.dot(
                left[xpos + x_pair[0], :, y_pair[0] * depth : y_pair[0] * depth + run],
                right[xpos + x_pair[1], y_pair[1] * depth : y_pair[1] * depth + run, :],
                preferred_element_type=jnp.float32,
            )
            total = term if total is None else total + term
        for z_pair in z_pairs:
            block = total[z_pair[0] * chans : (z_pair[0] + 1) * chans, z_pair[1] * chans : (z_pair[1] + 1) * chans]
            out[slot_place(SLOTS[(x_pair, y_pair, z_pair)])] = block
    out_g[...] = jnp.zeros_like(out_g)
    out_g[:, :chans] = lax.dot_general(
        cots[...], cots[...], (((1,), (1,)), ((), ())), preferred_element_type=jnp.float32
    )
    for slot in range(len(SLOTS), N_SLOTS):
        out[slot_place(slot)] = jnp.zeros((chans, chans), jnp.float32)


def gram_terms(ext, cots):
    planes, lines, chans, depth = ext.shape
    vmem = pl.BlockSpec(memory_space=pltpu.VMEM)
    return pl.pallas_call(
        gram_kernel,
        out_shape=[
            jax.ShapeDtypeStruct((ROWS, 2 * CH), jnp.float32),
            jax.ShapeDtypeStruct((CH, 2 * CH), jnp.float32),
        ],
        in_specs=[vmem, vmem],
        out_specs=[vmem, vmem],
        scratch_shapes=[
            pltpu.VMEM((planes, 3 * chans, lines * depth), jnp.bfloat16),
            pltpu.VMEM((planes, lines * depth, 3 * chans), jnp.bfloat16),
        ],
        compiler_params=pltpu.CompilerParams(vmem_limit_bytes=48 * 2**20),
    )(ext, cots)


HALF = ROWS // 2
PART = HALF // 3
SIZES = (PART // 4, PART // 16, PART // 64)


def inverse_row(matrix, index):
    size = matrix.shape[0]
    lane = lax.broadcasted_iota(jnp.int32, (size, 128), 1)
    sub = lax.broadcasted_iota(jnp.int32, (size, 128), 0)
    work = jnp.where(lane < size, matrix, 0.0) + jnp.where((lane == size) & (sub == index), 1.0, 0.0)
    for step in range(size):
        pivot = work[step : step + 1, :] / work[step : step + 1, step : step + 1]
        work = jnp.where(sub == step, pivot, work - work[:, step : step + 1] * pivot)
    return work[:, size : size + 1]


def reduce_kernel(
    inv_cells, terms, g_part, grad, full, row_out, half, from_core, sums_1, sums_2, sums_3, came_1, came_2, came_3,
    g_sum, g_came, grads, core_send, core_recv, ring_send, ring_recv, back_send, back_recv,
    last_send, last_recv, g_send, g_recv, w_send, w_recv,
):
    space, own = lax.axis_index("space"), lax.axis_index("own")
    core, ypos, z_lo = lax.rem(space, 2), lax.rem(space // 2, 4), space // 8
    xpos, z_hi = lax.rem(own, 4), own // 4
    coords = (xpos, ypos, z_hi * 2 + z_lo)

    def peer(axis, coord):
        if axis == 0:
            return {"space": space, "own": own - xpos + coord}
        if axis == 1:
            return {"space": space + 2 * (coord - ypos), "own": own}
        return {"space": space + 8 * (lax.rem(coord, 2) - z_lo), "own": coord // 2 * 4 + xpos}

    partner = {"space": space + 1 - 2 * core, "own": own}
    ring = {
        (axis, step): peer(axis, lax.rem(coords[axis] + step, 4)) for axis in range(3) for step in (1, 2, 3)
    }
    owners = [{"space": space, "own": lax.rem(own + step, 8)} for step in range(1, 8)]
    lanes = grad.shape[1]
    grads[own, :, lanes:] = jnp.zeros((CH, grads.shape[2] - lanes), jnp.float32)
    grads[own, :, :lanes] = grad[...]
    meet([partner] + list(ring.values()) + owners)

    def rows(start, count):
        return pl.ds(pl.multiple_of(start, 8), count)

    def send(src, dst, send_sem, recv_sem, device):
        copy = pltpu.make_async_remote_copy(
            src_ref=src, dst_ref=dst, send_sem=send_sem, recv_sem=recv_sem, device_id=device, device_id_type=MESH
        )
        copy.start()
        return copy

    waiting = []
    to_core = [
        send(
            terms.at[rows((1 - core) * HALF + part * PART, PART)],
            from_core.at[rows(part * PART, PART)],
            core_send.at[part], core_recv.at[part], partner,
        )
        for part in range(3)
    ]
    waiting += to_core
    to_owners = [
        send(grads.at[own], grads.at[own], w_send.at[index], w_recv.at[index], owner)
        for index, owner in enumerate(owners)
    ]
    waiting += to_owners

    def send_g(stage, source, devices):
        copies = [
            send(source, g_came.at[stage + index], g_send.at[stage + index], g_recv.at[stage + index], device)
            for index, device in enumerate(devices)
        ]
        waiting.extend(copies)
        return copies

    def add_g(stage, value, copies, target):
        for index, copy in enumerate(copies):
            copy.wait_recv()
            value = value + g_came[stage + index]
        g_sum[target] = value

    g_copies = send_g(0, g_part, [partner])
    levels = (half, sums_1, sums_2, sums_3)
    came = (came_1, came_2, came_3)
    flights = {}

    def scatter(level, part):
        axis, count = (part + level) % 3, SIZES[level]
        for step in (1, 2, 3):
            target = lax.rem(coords[axis] + step, 4)
            slot = part * 3 + step - 1
            flights[(level, part, step)] = send(
                levels[level].at[rows(part * count * 4 + target * count, count)],
                came[level].at[rows(slot * count, count)],
                ring_send.at[level * 9 + slot], ring_recv.at[level * 9 + slot], ring[(axis, step)],
            )
            waiting.append(flights[(level, part, step)])

    def collect(level, part):
        axis, count = (part + level) % 3, SIZES[level]
        total = levels[level][rows(part * count * 4 + coords[axis] * count, count), :]
        for step in (1, 2, 3):
            flights[(level, part, step)].wait_recv()
            total = total + came[level][rows((part * 3 + step - 1) * count, count), :]
        levels[level + 1][rows(part * count, count), :] = total

    for part in range(3):
        to_core[part].wait_recv()
        here = rows(part * PART, PART)
        half[here, :] = terms[rows(core * HALF + part * PART, PART), :] + from_core[here, :]
        scatter(0, part)
    add_g(0, g_part[...], g_copies, 0)
    for level in range(3):
        stage = 1 + 3 * level
        g_copies = send_g(stage, g_sum.at[level], [ring[(level, step)] for step in (1, 2, 3)])
        for part in range(3):
            collect(level, part)
            if level < 2:
                scatter(level + 1, part)
        add_g(stage, g_sum[level], g_copies, level + 1)

    def base(level, part):
        start = core * HALF + part * PART
        for outer in range(level):
            start = start + coords[(part + outer) % 3] * SIZES[outer]
        return start

    back = {}

    def spread(level, part):
        axis, count = (part + level) % 3, SIZES[level]
        here = rows(base(level, part) + coords[axis] * count, count)
        for step in (1, 2, 3):
            slot = level * 9 + part * 3 + step - 1
            back[(level, part, step)] = send(
                full.at[here], full.at[here], back_send.at[slot], back_recv.at[slot], ring[(axis, step)]
            )
            waiting.append(back[(level, part, step)])

    for part in range(3):
        here = rows(base(3, part), SIZES[2])
        full[here, :] = sums_3[rows(part * SIZES[2], SIZES[2]), :]
        spread(2, part)
    for level in (2, 1, 0):
        if level == 0:
            diagonal = lax.broadcasted_iota(jnp.int32, (CH, 2 * CH), 0) == lax.broadcasted_iota(
                jnp.int32, (CH, 2 * CH), 1
            )
            weights = inverse_row(
                g_sum[3] * inv_cells + jnp.where(diagonal, damping, 0.0), own * 8 + space // 2
            )
            for copy in to_owners:
                copy.wait_recv()
            row_out[...] = jnp.zeros_like(row_out)
            for owner in range(8):
                piece = jnp.sum(grads[owner] * weights, axis=0, keepdims=True)
                row_out[:, owner * lanes : (owner + 1) * lanes] = piece[:, :lanes]
        for part in range(3):
            for step in (1, 2, 3):
                back[(level, part, step)].wait_recv()
            if level:
                spread(level - 1, part)
            else:
                here = rows(core * HALF + part * PART, PART)
                back[(part,)] = send(full.at[here], full.at[here], last_send.at[part], last_recv.at[part], partner)
                waiting.append(back[(part,)])
    for part in range(3):
        back[(part,)].wait_recv()
    for copy in waiting:
        copy.wait_send()


def reduced(terms, g_part, grad, inv_cells, size):
    vmem = pl.BlockSpec(memory_space=pltpu.VMEM)
    lanes = terms.shape[1]
    buffers = [HALF, HALF] + [3 * count for count in SIZES] + [9 * count for count in SIZES]
    dma = pltpu.SemaphoreType.DMA
    return pl.pallas_call(
        functools.partial(reduce_kernel, inv_cells),
        out_shape=[
            jax.ShapeDtypeStruct(terms.shape, terms.dtype),
            jax.ShapeDtypeStruct((1, size), jnp.float32),
        ],
        in_specs=[vmem] * 3,
        out_specs=[vmem] * 2,
        scratch_shapes=[pltpu.VMEM((count, lanes), terms.dtype) for count in buffers]
        + [pltpu.VMEM((count, CH, lanes), jnp.float32) for count in (4, 10)]
        + [pltpu.VMEM((8, CH, -(-grad.shape[1] // lanes) * lanes), jnp.float32)]
        + [dma((count,)) for count in (3, 3, 27, 27, 27, 27, 3, 3, 10, 10, 7, 7)],
        compiler_params=pltpu.CompilerParams(
            collective_id=1, has_side_effects=True, vmem_limit_bytes=48 * 2**20
        ),
    )(terms, g_part, grad)


def times_factor(factor, row):
    size = factor.shape[0]
    parts = []
    for base in range(0, size, 128):
        rows = factor[pl.ds(base, 128), :].reshape(16, 8, size)
        total = jnp.zeros((16, 8, 128), jnp.float32)
        for lane in range(0, size, 128):
            total = total + rows[:, :, lane : lane + 128] * row[None, :, lane : lane + 128]
        flipped = total.reshape(128, 128).T
        parts.append(jnp.broadcast_to(jnp.sum(flipped, axis=0, keepdims=True), (8, 128)))
    return jnp.concatenate(parts, axis=1)


def halves(value):
    high = value.astype(jnp.bfloat16)
    return high, (value - high.astype(jnp.float32)).astype(jnp.bfloat16)


def frobenius(full, inv_cells, eye):
    counts = {}
    for row in range(27):
        for col in range(row, 27):
            slot = block_slot(row, col)
            counts[slot] = counts.get(slot, 0) + (1 if row == col else 2)
    plain = jnp.zeros((CH, CH), jnp.float32)
    for slot, count in counts.items():
        block = full[slot_place(slot)] * inv_cells
        if slot in DIAGONAL:
            block = block + eye
        plain = plain + float(count) * (block * block)
    return jnp.sum(plain, keepdims=True)


def assemble(full, inverse, inv_cells, eye, factor, high, low):
    size = factor.shape[0]
    width = 27 * CH
    for ref in (factor, high, low):
        ref[width:, :] = jnp.zeros((size - width, size), ref.dtype)
        ref[:, width:] = jnp.zeros((size, size - width), ref.dtype)

    def put(rows, cols, value):
        factor[rows, cols] = value
        high[rows, cols], low[rows, cols] = halves(value)

    for row in range(27):
        for col in range(row, 27):
            block = full[slot_place(block_slot(row, col))] * inv_cells
            if row == col:
                block = block + eye
            block = block * inverse
            rows, cols = slice(row * CH, (row + 1) * CH), slice(col * CH, (col + 1) * CH)
            put(rows, cols, block)
            if row != col and row * CH // TILE == col * CH // TILE:
                put(cols, rows, block.T)
    tiles = size // TILE
    for row in range(tiles):
        for col in range(row + 1, tiles):
            rows, cols = slice(row * TILE, (row + 1) * TILE), slice(col * TILE, (col + 1) * TILE)
            put(cols, rows, factor[rows, cols].T)


def poly_kernel(inv_cells, full, row_ref, out_ref, factor, high_a, low_a, high_b, low_b):
    size = factor.shape[0]
    tiles = size // TILE
    eye = jnp.where(
        lax.broadcasted_iota(jnp.int32, (CH, CH), 0) == lax.broadcasted_iota(jnp.int32, (CH, CH), 1), damping, 0.0
    )
    inverse = 1.0 / jnp.sqrt(frobenius(full, inv_cells, eye))
    assemble(full, inverse, inv_cells, eye, factor, high_a, low_a)
    row = jnp.broadcast_to(row_ref[...], (8, size)) * inverse
    dot = functools.partial(jnp.dot, preferred_element_type=jnp.float32)
    operands = ((high_a, low_a), (high_b, low_b))
    for step in range(SQUARINGS):
        (high, low), (next_high, next_low) = operands[step % 2], operands[1 - step % 2]
        row = 2.0 * row - times_factor(factor, row)

        def row_tile(i, carry, high=high, low=low, next_high=next_high, next_low=next_low, step=step):
            rows = pl.ds(pl.multiple_of(i * TILE, TILE), TILE)
            left_high, left_low = high[rows, :], low[rows, :]
            for apart in range((tiles + 1) // 2):
                j = lax.rem(i + apart, tiles)
                cols = pl.ds(pl.multiple_of(j * TILE, TILE), TILE)
                right_high, right_low = high[:, cols], low[:, cols]
                square = dot(left_high, right_high) + (dot(left_high, right_low) + dot(left_low, right_high))
                fresh = 2.0 * factor[rows, cols] - square
                factor[rows, cols] = fresh
                flipped = fresh.T
                if apart:
                    factor[cols, rows] = flipped
                if step < SQUARINGS - 1:
                    next_high[rows, cols], next_low[rows, cols] = halves(fresh)
                    if apart:
                        next_high[cols, rows], next_low[cols, rows] = halves(flipped)
            return carry

        lax.fori_loop(0, tiles, row_tile, 0)

    def horner(index, value):
        return row + (value - times_factor(factor, value))

    value = lax.fori_loop(0, 2 ** (8 - SQUARINGS) - 1, horner, row)
    out_ref[...] = value[:1]


def polynomial(full, row, inv_cells):
    size = row.shape[1]
    vmem = pl.BlockSpec(memory_space=pltpu.VMEM)
    return pl.pallas_call(
        functools.partial(poly_kernel, inv_cells),
        out_shape=jax.ShapeDtypeStruct((1, size), jnp.float32),
        in_specs=[vmem, vmem],
        out_specs=vmem,
        scratch_shapes=[pltpu.VMEM((size, size), jnp.float32)] + [pltpu.VMEM((size, size), jnp.bfloat16)] * 4,
        compiler_params=pltpu.CompilerParams(vmem_limit_bytes=56 * 2**20),
    )(full, row)


def share_kernel(row, out, pieces, came, send_sem, recv_sem):
    space, own = lax.axis_index("space"), lax.axis_index("own")
    core, chip = lax.rem(space, 2), space // 2
    lanes = out.shape[1]
    peers = [{"space": lax.rem(space + 2 * step, 16), "own": own} for step in range(1, 8)]
    for index in range(16):
        piece = row[:, index * lanes : (index + 1) * lanes]
        pieces[index, :, :lanes] = jnp.broadcast_to(piece, (8, lanes))
        pieces[index, :, lanes:] = jnp.zeros((8, 128 - lanes), jnp.float32)
    meet(peers)
    copies = []
    for index, peer in enumerate(peers):
        copy = pltpu.make_async_remote_copy(
            src_ref=pieces.at[peer["space"]],
            dst_ref=came.at[chip],
            send_sem=send_sem.at[index],
            recv_sem=recv_sem.at[index],
            device_id=peer,
            device_id_type=MESH,
        )
        copy.start()
        copies.append(copy)
    came[chip] = pieces[space]
    for copy in copies:
        copy.wait()
    for index in range(8):
        out[index : index + 1, :] = came[index, :1, :lanes]


def shared(row, lanes):
    vmem = pl.BlockSpec(memory_space=pltpu.VMEM)
    return pl.pallas_call(
        share_kernel,
        out_shape=jax.ShapeDtypeStruct((8, lanes), jnp.float32),
        in_specs=[vmem],
        out_specs=vmem,
        scratch_shapes=[
            pltpu.VMEM((16, 8, 128), jnp.float32),
            pltpu.VMEM((8, 8, 128), jnp.float32),
            pltpu.SemaphoreType.DMA((7,)),
            pltpu.SemaphoreType.DMA((7,)),
        ],
        compiler_params=pltpu.CompilerParams(collective_id=2, has_side_effects=True),
    )(row)


def body(acts, cotangents, weight_grad):
    chans, block_x, block_y, depth_z = acts.shape
    c_out = cotangents.shape[0]
    width = 27 * chans
    n_space = lax.axis_size("space")
    n_own = lax.axis_size("own")
    inv_cells = 1.0 / (block_x * n_space * block_y * n_own * depth_z)
    size = -(-width // TILE) * TILE
    ext = with_halo(jnp.transpose(acts, (1, 2, 0, 3)))
    terms, g_part = gram_terms(ext, cotangents.reshape(c_out, -1))
    full, row = reduced(terms, g_part, weight_grad, inv_cells, size)
    return shared(polynomial(full, row, inv_cells), width // n_space)


def solution(mesh):
    in_specs = (P(None, "space", "own", None), P(None, "space", "own", None), P(None, "own"))
    out_specs = P("own", "space")
    return jax.shard_map(body, mesh=mesh, in_specs=in_specs, out_specs=out_specs, check_vma=False)
```

```python
import functools

import jax
import jax.numpy as jnp
from jax import lax
from jax.experimental import pallas as pl
from jax.experimental.pallas import tpu as pltpu
from jax.sharding import PartitionSpec as P

SQUARINGS = 3
TILE = 256
CH = 64
NZ = 256
damping = 0.05
MESH = pl.DeviceIdType.MESH
SAME = ((0, 0), (1, 1), (2, 2))
UP = ((0, 1), (0, 2))
DOWN = ((1, 0), (2, 0))


def pair_type(first, second):
    if first == second:
        return (first, second)
    apart = second - first
    return (0, apart) if apart > 0 else (-apart, 0)


def distinct_pairs():
    pairs = []
    for x_pair in SAME + UP:
        for y_pair in SAME + UP + (DOWN if x_pair in UP else ()):
            full = x_pair in UP or y_pair in UP
            pairs.append((x_pair, y_pair, SAME + UP + (DOWN if full else ())))
    return pairs


PAIRS = distinct_pairs()
SLOTS = {}
for _x_pair, _y_pair, _z_pairs in PAIRS:
    for _z_pair in _z_pairs:
        SLOTS[(_x_pair, _y_pair, _z_pair)] = len(SLOTS)
N_SLOTS = 192
ROWS = N_SLOTS // 2 * CH


def slot_place(slot):
    return slice(slot // 2 * CH, slot // 2 * CH + CH), slice(slot % 2 * CH, slot % 2 * CH + CH)


def block_slot(row, col):
    return SLOTS[
        tuple(
            pair_type(row // unit % 3, col // unit % 3) for unit in (9, 3, 1)
        )
    ]


DIAGONAL = {block_slot(index, index) for index in range(27)}


def meet(peers):
    barrier = pltpu.get_barrier_semaphore()
    for peer in peers:
        pl.semaphore_signal(barrier, inc=1, device_id=peer, device_id_type=MESH)
    pl.semaphore_wait(barrier, len(peers))


def halo_kernel(base, ext, send_sem, recv_sem):
    space, own = lax.axis_index("space"), lax.axis_index("own")
    n_space, n_own = lax.axis_size("space"), lax.axis_size("own")
    planes, lines = base.shape[0], base.shape[1]
    ext[1 : 1 + planes, 1 : 1 + lines] = base[...]
    steps = [(dx, dy) for dx in (-1, 0, 1) for dy in (-1, 0, 1) if dx or dy]
    peers = [
        {"space": lax.rem(space + dx + n_space, n_space), "own": lax.rem(own + dy + n_own, n_own)}
        for dx, dy in steps
    ]
    meet(peers)

    def ends(step, count):
        if step == 0:
            return pl.ds(1, count), pl.ds(1, count)
        return (pl.ds(count, 1), pl.ds(0, 1)) if step > 0 else (pl.ds(1, 1), pl.ds(count + 1, 1))

    copies = []
    for index, (dx, dy) in enumerate(steps):
        from_x, to_x = ends(dx, planes)
        from_y, to_y = ends(dy, lines)
        copy = pltpu.make_async_remote_copy(
            src_ref=ext.at[from_x, from_y],
            dst_ref=ext.at[to_x, to_y],
            send_sem=send_sem.at[index],
            recv_sem=recv_sem.at[index],
            device_id=peers[index],
            device_id_type=MESH,
        )
        copy.start()
        copies.append(copy)
    for copy in copies:
        copy.wait()

    @pl.when(space == 0)
    def _():
        ext[0] = jnp.zeros_like(ext[0])

    @pl.when(space == n_space - 1)
    def _():
        ext[planes + 1] = jnp.zeros_like(ext[0])

    @pl.when(own == 0)
    def _():
        ext[:, 0] = jnp.zeros_like(ext[:, 0])

    @pl.when(own == n_own - 1)
    def _():
        ext[:, lines + 1] = jnp.zeros_like(ext[:, 0])


def with_halo(base):
    planes, lines, chans, depth = base.shape
    return pl.pallas_call(
        halo_kernel,
        out_shape=jax.ShapeDtypeStruct((planes + 2, lines + 2, chans, depth), base.dtype),
        in_specs=[pl.BlockSpec(memory_space=pltpu.VMEM)],
        out_specs=pl.BlockSpec(memory_space=pltpu.VMEM),
        scratch_shapes=[pltpu.SemaphoreType.DMA((8,)), pltpu.SemaphoreType.DMA((8,))],
        compiler_params=pltpu.CompilerParams(
            collective_id=0, has_side_effects=True, vmem_limit_bytes=32 * 2**20
        ),
    )(base)


def gram_kernel(ext, cots, out, out_g, left, right):
    planes, lines, chans, depth = ext.shape
    lane = lax.broadcasted_iota(jnp.int32, (chans, depth), 1)

    def shift_plane(xpos, carry):
        for ypos in range(lines):
            here = ext[xpos, ypos].astype(jnp.float32)
            before = jnp.where(lane == 0, 0.0, pltpu.roll(here, 1, 1))
            after = jnp.where(lane == depth - 1, 0.0, pltpu.roll(here, depth - 1, 1))
            stack = jnp.concatenate([before, here, after], axis=0)
            across = slice(ypos * depth, (ypos + 1) * depth)
            left[xpos, :, across] = stack.astype(left.dtype)
            right[xpos, across, :] = stack.T.astype(right.dtype)
        return carry

    lax.fori_loop(0, planes, shift_plane, 0)
    run = (lines - 2) * depth
    for x_pair, y_pair, z_pairs in PAIRS:
        total = None
        for xpos in range(planes - 2):
            term = jnp.dot(
                left[xpos + x_pair[0], :, y_pair[0] * depth : y_pair[0] * depth + run],
                right[xpos + x_pair[1], y_pair[1] * depth : y_pair[1] * depth + run, :],
                preferred_element_type=jnp.float32,
            )
            total = term if total is None else total + term
        for z_pair in z_pairs:
            block = total[z_pair[0] * chans : (z_pair[0] + 1) * chans, z_pair[1] * chans : (z_pair[1] + 1) * chans]
            out[slot_place(SLOTS[(x_pair, y_pair, z_pair)])] = block
    out_g[...] = jnp.zeros_like(out_g)
    out_g[:, :chans] = lax.dot_general(
        cots[...], cots[...], (((1,), (1,)), ((), ())), preferred_element_type=jnp.float32
    )
    for slot in range(len(SLOTS), N_SLOTS):
        out[slot_place(slot)] = jnp.zeros((chans, chans), jnp.float32)


def gram_terms(ext, cots):
    planes, lines, chans, depth = ext.shape
    vmem = pl.BlockSpec(memory_space=pltpu.VMEM)
    return pl.pallas_call(
        gram_kernel,
        out_shape=[
            jax.ShapeDtypeStruct((ROWS, 2 * CH), jnp.float32),
            jax.ShapeDtypeStruct((CH, 2 * CH), jnp.float32),
        ],
        in_specs=[vmem, vmem],
        out_specs=[vmem, vmem],
        scratch_shapes=[
            pltpu.VMEM((planes, 3 * chans, lines * depth), jnp.bfloat16),
            pltpu.VMEM((planes, lines * depth, 3 * chans), jnp.bfloat16),
        ],
        compiler_params=pltpu.CompilerParams(vmem_limit_bytes=48 * 2**20),
    )(ext, cots)


HALF = ROWS // 2
PART = HALF // 3
SIZES = (PART // 4, PART // 16, PART // 64)


def inverse_row(matrix, index):
    size = matrix.shape[0]
    lane = lax.broadcasted_iota(jnp.int32, (size, 128), 1)
    sub = lax.broadcasted_iota(jnp.int32, (size, 128), 0)
    work = jnp.where(lane < size, matrix, 0.0) + jnp.where((lane == size) & (sub == index), 1.0, 0.0)
    for step in range(size):
        pivot = work[step : step + 1, :] / work[step : step + 1, step : step + 1]
        work = jnp.where(sub == step, pivot, work - work[:, step : step + 1] * pivot)
    return work[:, size : size + 1]


def reduce_kernel(
    inv_cells, terms, g_part, grad, full, row_out, half, from_core, sums_1, sums_2, sums_3, came_1, came_2, came_3,
    g_sum, g_came, grads, core_send, core_recv, ring_send, ring_recv, back_send, back_recv,
    last_send, last_recv, g_send, g_recv, w_send, w_recv,
):
    space, own = lax.axis_index("space"), lax.axis_index("own")
    core, ypos, z_lo = lax.rem(space, 2), lax.rem(space // 2, 4), space // 8
    xpos, z_hi = lax.rem(own, 4), own // 4
    coords = (xpos, ypos, z_hi * 2 + z_lo)

    def peer(axis, coord):
        if axis == 0:
            return {"space": space, "own": own - xpos + coord}
        if axis == 1:
            return {"space": space + 2 * (coord - ypos), "own": own}
        return {"space": space + 8 * (lax.rem(coord, 2) - z_lo), "own": coord // 2 * 4 + xpos}

    partner = {"space": space + 1 - 2 * core, "own": own}
    ring = {
        (axis, step): peer(axis, lax.rem(coords[axis] + step, 4)) for axis in range(3) for step in (1, 2, 3)
    }
    owners = [{"space": space, "own": lax.rem(own + step, 8)} for step in range(1, 8)]
    lanes = grad.shape[1]
    grads[own, :, lanes:] = jnp.zeros((CH, grads.shape[2] - lanes), jnp.float32)
    grads[own, :, :lanes] = grad[...]
    meet([partner] + list(ring.values()) + owners)

    def rows(start, count):
        return pl.ds(pl.multiple_of(start, 8), count)

    def send(src, dst, send_sem, recv_sem, device):
        copy = pltpu.make_async_remote_copy(
            src_ref=src, dst_ref=dst, send_sem=send_sem, recv_sem=recv_sem, device_id=device, device_id_type=MESH
        )
        copy.start()
        return copy

    waiting = []
    to_core = [
        send(
            terms.at[rows((1 - core) * HALF + part * PART, PART)],
            from_core.at[rows(part * PART, PART)],
            core_send.at[part], core_recv.at[part], partner,
        )
        for part in range(3)
    ]
    waiting += to_core
    to_owners = [
        send(grads.at[own], grads.at[own], w_send.at[index], w_recv.at[index], owner)
        for index, owner in enumerate(owners)
    ]
    waiting += to_owners

    def send_g(stage, source, devices):
        copies = [
            send(source, g_came.at[stage + index], g_send.at[stage + index], g_recv.at[stage + index], device)
            for index, device in enumerate(devices)
        ]
        waiting.extend(copies)
        return copies

    def add_g(stage, value, copies, target):
        for index, copy in enumerate(copies):
            copy.wait_recv()
            value = value + g_came[stage + index]
        g_sum[target] = value

    g_copies = send_g(0, g_part, [partner])
    levels = (half, sums_1, sums_2, sums_3)
    came = (came_1, came_2, came_3)
    flights = {}

    def scatter(level, part):
        axis, count = (part + level) % 3, SIZES[level]
        for step in (1, 2, 3):
            target = lax.rem(coords[axis] + step, 4)
            slot = part * 3 + step - 1
            flights[(level, part, step)] = send(
                levels[level].at[rows(part * count * 4 + target * count, count)],
                came[level].at[rows(slot * count, count)],
                ring_send.at[level * 9 + slot], ring_recv.at[level * 9 + slot], ring[(axis, step)],
            )
            waiting.append(flights[(level, part, step)])

    def collect(level, part):
        axis, count = (part + level) % 3, SIZES[level]
        total = levels[level][rows(part * count * 4 + coords[axis] * count, count), :]
        for step in (1, 2, 3):
            flights[(level, part, step)].wait_recv()
            total = total + came[level][rows((part * 3 + step - 1) * count, count), :]
        levels[level + 1][rows(part * count, count), :] = total

    for part in range(3):
        to_core[part].wait_recv()
        here = rows(part * PART, PART)
        half[here, :] = terms[rows(core * HALF + part * PART, PART), :] + from_core[here, :]
        scatter(0, part)
    add_g(0, g_part[...], g_copies, 0)
    for level in range(3):
        stage = 1 + 3 * level
        g_copies = send_g(stage, g_sum.at[level], [ring[(level, step)] for step in (1, 2, 3)])
        for part in range(3):
            collect(level, part)
            if level < 2:
                scatter(level + 1, part)
        add_g(stage, g_sum[level], g_copies, level + 1)

    def base(level, part):
        start = core * HALF + part * PART
        for outer in range(level):
            start = start + coords[(part + outer) % 3] * SIZES[outer]
        return start

    back = {}

    def spread(level, part):
        axis, count = (part + level) % 3, SIZES[level]
        here = rows(base(level, part) + coords[axis] * count, count)
        for step in (1, 2, 3):
            slot = level * 9 + part * 3 + step - 1
            back[(level, part, step)] = send(
                full.at[here], full.at[here], back_send.at[slot], back_recv.at[slot], ring[(axis, step)]
            )
            waiting.append(back[(level, part, step)])

    for part in range(3):
        here = rows(base(3, part), SIZES[2])
        full[here, :] = sums_3[rows(part * SIZES[2], SIZES[2]), :]
        spread(2, part)
    for level in (2, 1, 0):
        if level == 0:
            diagonal = lax.broadcasted_iota(jnp.int32, (CH, 2 * CH), 0) == lax.broadcasted_iota(
                jnp.int32, (CH, 2 * CH), 1
            )
            weights = inverse_row(
                g_sum[3] * inv_cells + jnp.where(diagonal, damping, 0.0), own * 8 + space // 2
            )
            for copy in to_owners:
                copy.wait_recv()
            row_out[...] = jnp.zeros_like(row_out)
            for owner in range(8):
                piece = jnp.sum(grads[owner] * weights, axis=0, keepdims=True)
                row_out[:, owner * lanes : (owner + 1) * lanes] = piece[:, :lanes]
        for part in range(3):
            for step in (1, 2, 3):
                back[(level, part, step)].wait_recv()
            if level:
                spread(level - 1, part)
            else:
                here = rows(core * HALF + part * PART, PART)
                back[(part,)] = send(full.at[here], full.at[here], last_send.at[part], last_recv.at[part], partner)
                waiting.append(back[(part,)])
    for part in range(3):
        back[(part,)].wait_recv()
    for copy in waiting:
        copy.wait_send()


def reduced(terms, g_part, grad, inv_cells, size):
    vmem = pl.BlockSpec(memory_space=pltpu.VMEM)
    lanes = terms.shape[1]
    buffers = [HALF, HALF] + [3 * count for count in SIZES] + [9 * count for count in SIZES]
    dma = pltpu.SemaphoreType.DMA
    return pl.pallas_call(
        functools.partial(reduce_kernel, inv_cells),
        out_shape=[
            jax.ShapeDtypeStruct(terms.shape, terms.dtype),
            jax.ShapeDtypeStruct((1, size), jnp.float32),
        ],
        in_specs=[vmem] * 3,
        out_specs=[vmem] * 2,
        scratch_shapes=[pltpu.VMEM((count, lanes), terms.dtype) for count in buffers]
        + [pltpu.VMEM((count, CH, lanes), jnp.float32) for count in (4, 10)]
        + [pltpu.VMEM((8, CH, -(-grad.shape[1] // lanes) * lanes), jnp.float32)]
        + [dma((count,)) for count in (3, 3, 27, 27, 27, 27, 3, 3, 10, 10, 7, 7)],
        compiler_params=pltpu.CompilerParams(
            collective_id=1, has_side_effects=True, vmem_limit_bytes=48 * 2**20
        ),
    )(terms, g_part, grad)


def times_factor(factor, row):
    size = factor.shape[0]
    parts = []
    for base in range(0, size, 128):
        rows = factor[pl.ds(base, 128), :].reshape(16, 8, size)
        total = jnp.zeros((16, 8, 128), jnp.float32)
        for lane in range(0, size, 128):
            total = total + rows[:, :, lane : lane + 128] * row[None, :, lane : lane + 128]
        flipped = total.reshape(128, 128).T
        parts.append(jnp.broadcast_to(jnp.sum(flipped, axis=0, keepdims=True), (8, 128)))
    return jnp.concatenate(parts, axis=1)


def halves(value):
    high = value.astype(jnp.bfloat16)
    return high, (value - high.astype(jnp.float32)).astype(jnp.bfloat16)


def frobenius(full, inv_cells, eye):
    counts = {}
    for row in range(27):
        for col in range(row, 27):
            slot = block_slot(row, col)
            counts[slot] = counts.get(slot, 0) + (1 if row == col else 2)
    plain = jnp.zeros((CH, CH), jnp.float32)
    for slot, count in counts.items():
        block = full[slot_place(slot)] * inv_cells
        if slot in DIAGONAL:
            block = block + eye
        plain = plain + float(count) * (block * block)
    return jnp.sum(plain, keepdims=True)


def assemble(full, inverse, inv_cells, eye, factor, high, low):
    size = factor.shape[0]
    width = 27 * CH
    for ref in (factor, high, low):
        ref[width:, :] = jnp.zeros((size - width, size), ref.dtype)
        ref[:, width:] = jnp.zeros((size, size - width), ref.dtype)

    def put(rows, cols, value):
        factor[rows, cols] = value
        high[rows, cols], low[rows, cols] = halves(value)

    for row in range(27):
        for col in range(row, 27):
            block = full[slot_place(block_slot(row, col))] * inv_cells
            if row == col:
                block = block + eye
            block = block * inverse
            rows, cols = slice(row * CH, (row + 1) * CH), slice(col * CH, (col + 1) * CH)
            put(rows, cols, block)
            if row != col and row * CH // TILE == col * CH // TILE:
                put(cols, rows, block.T)
    tiles = size // TILE
    for row in range(tiles):
        for col in range(row + 1, tiles):
            rows, cols = slice(row * TILE, (row + 1) * TILE), slice(col * TILE, (col + 1) * TILE)
            put(cols, rows, factor[rows, cols].T)


def poly_kernel(
    inv_cells, full, row_ref, out, factor, high_a, low_a, high_b, low_b, pieces, came,
    tile_send, tile_recv, ready, share_send, share_recv,
):
    space, own = lax.axis_index("space"), lax.axis_index("own")
    core, chip = lax.rem(space, 2), space // 2
    partner = {"space": space + 1 - 2 * core, "own": own}
    peers = [{"space": lax.rem(space + 2 * step, 16), "own": own} for step in range(1, 8)]
    meet([partner] + peers)
    size = factor.shape[0]
    tiles = size // TILE
    eye = jnp.where(
        lax.broadcasted_iota(jnp.int32, (CH, CH), 0) == lax.broadcasted_iota(jnp.int32, (CH, CH), 1), damping, 0.0
    )
    inverse = 1.0 / jnp.sqrt(frobenius(full, inv_cells, eye))
    assemble(full, inverse, inv_cells, eye, factor, high_a, low_a)
    row = jnp.broadcast_to(row_ref[...], (8, size)) * inverse
    dot = functools.partial(jnp.dot, preferred_element_type=jnp.float32)
    operands = ((high_a, low_a), (high_b, low_b))

    def place(i, half, which):
        j = lax.rem(i + 2 * half + which, tiles)
        return (
            pl.ds(pl.multiple_of(i * TILE, TILE), TILE),
            pl.ds(pl.multiple_of(j * TILE, TILE), TILE),
        )

    def tile_copy(i, which):
        here = factor.at[place(i, core, which)]
        return pltpu.make_async_remote_copy(
            src_ref=here,
            dst_ref=here,
            send_sem=tile_send.at[2 * i + which],
            recv_sem=tile_recv.at[2 * i + which],
            device_id=partner,
            device_id_type=MESH,
        )

    for step in range(SQUARINGS):
        (high, low), (next_high, next_low) = operands[step % 2], operands[1 - step % 2]
        row = 2.0 * row - times_factor(factor, row)
        pl.semaphore_signal(ready, inc=1, device_id=partner, device_id_type=MESH)

        def finish(i, half, which, fresh, step=step, next_high=next_high, next_low=next_low):
            rows, cols = place(i, half, which)
            flipped = fresh.T
            if which == 0:
                flipped = jnp.where(half == 0, fresh, flipped)
            factor[cols, rows] = flipped
            if step < SQUARINGS - 1:
                next_high[rows, cols], next_low[rows, cols] = halves(fresh)
                next_high[cols, rows], next_low[cols, rows] = halves(flipped)

        def compute(i, step=step, high=high, low=low, finish=finish):
            for which in range(2):
                rows, cols = place(i, core, which)
                square = dot(high[rows, :], high[:, cols])
                if step:
                    square = square + (dot(high[rows, :], low[:, cols]) + dot(low[rows, :], high[:, cols]))
                fresh = 2.0 * factor[rows, cols] - square
                factor[rows, cols] = fresh
                finish(i, core, which, fresh)

        def adopt(i, finish=finish):
            for which in range(2):
                finish(i, 1 - core, which, factor[place(i, 1 - core, which)])

        def next_tiles(i, carry, compute=compute, adopt=adopt):
            for which in range(2):
                tile_copy(i - 1, which).wait_recv()
            adopt(i - 1)
            compute(i)
            for which in range(2):
                tile_copy(i, which).start()
            return carry

        compute(0)
        pl.semaphore_wait(ready, 1)
        for which in range(2):
            tile_copy(0, which).start()
        lax.fori_loop(1, tiles, next_tiles, 0)
        for which in range(2):
            tile_copy(tiles - 1, which).wait_recv()
        adopt(tiles - 1)
        for index in range(2 * tiles):
            tile_copy(index // 2, index % 2).wait_send()

    def horner(index, value):
        return row + (value - times_factor(factor, value))

    value = lax.fori_loop(0, 2 ** (8 - SQUARINGS) - 1, horner, row)

    lanes = out.shape[1]
    for index in range(16):
        pieces[index, :, :lanes] = value[:, index * lanes : (index + 1) * lanes]
        pieces[index, :, lanes:] = jnp.zeros((8, 128 - lanes), jnp.float32)
    copies = []
    for index, peer in enumerate(peers):
        copy = pltpu.make_async_remote_copy(
            src_ref=pieces.at[peer["space"]],
            dst_ref=came.at[chip],
            send_sem=share_send.at[index],
            recv_sem=share_recv.at[index],
            device_id=peer,
            device_id_type=MESH,
        )
        copy.start()
        copies.append(copy)
    came[chip] = pieces[space]
    for copy in copies:
        copy.wait()
    for index in range(8):
        out[index : index + 1, :] = came[index, :1, :lanes]


def polynomial(full, row, inv_cells, lanes):
    size = row.shape[1]
    tiles = size // TILE
    vmem = pl.BlockSpec(memory_space=pltpu.VMEM)
    dma = pltpu.SemaphoreType.DMA
    return pl.pallas_call(
        functools.partial(poly_kernel, inv_cells),
        out_shape=jax.ShapeDtypeStruct((8, lanes), jnp.float32),
        in_specs=[vmem, vmem],
        out_specs=vmem,
        scratch_shapes=[pltpu.VMEM((size, size), jnp.float32)]
        + [pltpu.VMEM((size, size), jnp.bfloat16)] * 4
        + [pltpu.VMEM((16, 8, 128), jnp.float32), pltpu.VMEM((8, 8, 128), jnp.float32)]
        + [dma((2 * tiles,)), dma((2 * tiles,)), pltpu.SemaphoreType.REGULAR, dma((7,)), dma((7,))],
        compiler_params=pltpu.CompilerParams(
            collective_id=2, has_side_effects=True, vmem_limit_bytes=56 * 2**20
        ),
    )(full, row)


def body(acts, cotangents, weight_grad):
    chans, block_x, block_y, depth_z = acts.shape
    c_out = cotangents.shape[0]
    width = 27 * chans
    n_space = lax.axis_size("space")
    n_own = lax.axis_size("own")
    inv_cells = 1.0 / (block_x * n_space * block_y * n_own * depth_z)
    size = -(-width // TILE) * TILE
    ext = with_halo(jnp.transpose(acts, (1, 2, 0, 3)))
    terms, g_part = gram_terms(ext, cotangents.reshape(c_out, -1))
    full, row = reduced(terms, g_part, weight_grad, inv_cells, size)
    return polynomial(full, row, inv_cells, width // n_space)


def solution(mesh):
    in_specs = (P(None, "space", "own", None), P(None, "space", "own", None), P(None, "own"))
    out_specs = P("own", "space")
    return jax.shard_map(body, mesh=mesh, in_specs=in_specs, out_specs=out_specs, check_vma=False)
```

```python
import functools

import jax
import jax.numpy as jnp
from jax import lax
from jax.experimental import pallas as pl
from jax.experimental.pallas import tpu as pltpu
from jax.sharding import PartitionSpec as P

SQUARINGS = 3
TILE = 256
LAG = 3
CH = 64
NZ = 256
damping = 0.05
MESH = pl.DeviceIdType.MESH
SAME = ((0, 0), (1, 1), (2, 2))
UP = ((0, 1), (0, 2))
DOWN = ((1, 0), (2, 0))


def pair_type(first, second):
    if first == second:
        return (first, second)
    apart = second - first
    return (0, apart) if apart > 0 else (-apart, 0)


def distinct_pairs():
    pairs = []
    for x_pair in SAME + UP:
        for y_pair in SAME + UP + (DOWN if x_pair in UP else ()):
            full = x_pair in UP or y_pair in UP
            pairs.append((x_pair, y_pair, SAME + UP + (DOWN if full else ())))
    return pairs


PAIRS = distinct_pairs()
SLOTS = {}
for _x_pair, _y_pair, _z_pairs in PAIRS:
    for _z_pair in _z_pairs:
        SLOTS[(_x_pair, _y_pair, _z_pair)] = len(SLOTS)
N_SLOTS = 192
ROWS = N_SLOTS // 2 * CH


def slot_place(slot):
    return slice(slot // 2 * CH, slot // 2 * CH + CH), slice(slot % 2 * CH, slot % 2 * CH + CH)


def block_slot(row, col):
    return SLOTS[
        tuple(
            pair_type(row // unit % 3, col // unit % 3) for unit in (9, 3, 1)
        )
    ]


DIAGONAL = {block_slot(index, index) for index in range(27)}


def meet(peers):
    barrier = pltpu.get_barrier_semaphore()
    for peer in peers:
        pl.semaphore_signal(barrier, inc=1, device_id=peer, device_id_type=MESH)
    pl.semaphore_wait(barrier, len(peers))


def inverse_row(matrix, index):
    size = matrix.shape[0]
    lane = lax.broadcasted_iota(jnp.int32, (size, 128), 1)
    sub = lax.broadcasted_iota(jnp.int32, (size, 128), 0)
    work = jnp.where(lane < size, matrix, 0.0) + jnp.where((lane == size) & (sub == index), 1.0, 0.0)
    for step in range(size):
        pivot = work[step : step + 1, :] / work[step : step + 1, step : step + 1]
        work = jnp.where(sub == step, pivot, work - work[:, step : step + 1] * pivot)
    return work[:, size : size + 1]


HALF = ROWS // 2
PART = HALF // 3
SLOTS_PER_PART = N_SLOTS // 3
SIZES = (PART // 4, PART // 16, PART // 64)


def front_kernel(
    inv_cells, base, cots, grad, full, row_out,
    ext, left, right, terms, half, from_core, sums_1, sums_2, sums_3, came_1, came_2, came_3, g_sum, g_came, grads,
    halo_send, halo_recv, core_send, core_recv, ring_send, ring_recv, back_send, back_recv,
    last_send, last_recv, g_send, g_recv, w_send, w_recv,
):
    space, own = lax.axis_index("space"), lax.axis_index("own")
    n_space, n_own = lax.axis_size("space"), lax.axis_size("own")
    core, ypos, z_lo = lax.rem(space, 2), lax.rem(space // 2, 4), space // 8
    xpos, z_hi = lax.rem(own, 4), own // 4
    coords = (xpos, ypos, z_hi * 2 + z_lo)
    planes, lines, chans, depth = base.shape
    lanes = grad.shape[1]

    def peer(axis, coord):
        if axis == 0:
            return {"space": space, "own": own - xpos + coord}
        if axis == 1:
            return {"space": space + 2 * (coord - ypos), "own": own}
        return {"space": space + 8 * (lax.rem(coord, 2) - z_lo), "own": coord // 2 * 4 + xpos}

    partner = {"space": space + 1 - 2 * core, "own": own}
    ring = {
        (axis, step): peer(axis, lax.rem(coords[axis] + step, 4)) for axis in range(3) for step in (1, 2, 3)
    }
    owners = [{"space": space, "own": lax.rem(own + step, n_own)} for step in range(1, n_own)]
    steps = [(dx, dy) for dx in (-1, 0, 1) for dy in (-1, 0, 1) if dx or dy]
    around = [
        {"space": lax.rem(space + dx + n_space, n_space), "own": lax.rem(own + dy + n_own, n_own)}
        for dx, dy in steps
    ]
    ext[1 : 1 + planes, 1 : 1 + lines] = base[...]
    grads[own, :, lanes:] = jnp.zeros((CH, grads.shape[2] - lanes), jnp.float32)
    grads[own, :, :lanes] = grad[...]
    meet([partner] + list(ring.values()) + owners + around)

    def rows(start, count):
        return pl.ds(pl.multiple_of(start, 8), count)

    waiting = []

    def send(src, dst, send_sem, recv_sem, device):
        copy = pltpu.make_async_remote_copy(
            src_ref=src, dst_ref=dst, send_sem=send_sem, recv_sem=recv_sem, device_id=device, device_id_type=MESH
        )
        copy.start()
        waiting.append(copy)
        return copy

    def ends(step, count):
        if step == 0:
            return pl.ds(1, count), pl.ds(1, count)
        return (pl.ds(count, 1), pl.ds(0, 1)) if step > 0 else (pl.ds(1, 1), pl.ds(count + 1, 1))

    halo = []
    for index, (dx, dy) in enumerate(steps):
        (from_x, to_x), (from_y, to_y) = ends(dx, planes), ends(dy, lines)
        halo.append(
            send(ext.at[from_x, from_y], ext.at[to_x, to_y], halo_send.at[index], halo_recv.at[index], around[index])
        )
    to_owners = [
        send(grads.at[own], grads.at[own], w_send.at[index], w_recv.at[index], owner)
        for index, owner in enumerate(owners)
    ]

    lane = lax.broadcasted_iota(jnp.int32, (chans, depth), 1)

    def shift_line(x, y):
        here = ext[x, y].astype(jnp.float32)
        before = jnp.where(lane == 0, 0.0, pltpu.roll(here, 1, 1))
        after = jnp.where(lane == depth - 1, 0.0, pltpu.roll(here, depth - 1, 1))
        stack = jnp.concatenate([before, here, after], axis=0)
        across = slice(y * depth, (y + 1) * depth)
        left[x, :, across] = stack.astype(left.dtype)
        right[x, across, :] = stack.T.astype(right.dtype)

    def shift_lines(x, ys):
        for y in ys:
            shift_line(x, y)

    def inner_plane(x, carry):
        shift_lines(x, range(1, lines + 1))
        return carry

    def edge_lines(x, carry):
        shift_lines(x, (0, lines + 1))
        return carry

    def outer_plane(index, carry):
        shift_lines(index * (planes + 1), range(lines + 2))
        return carry

    g_sum[0] = jnp.zeros_like(g_sum[0])
    g_sum[0, :, :chans] = lax.dot_general(
        cots[...], cots[...], (((1,), (1,)), ((), ())), preferred_element_type=jnp.float32
    )
    g_copies = [send(g_sum.at[0], g_came.at[0], g_send.at[0], g_recv.at[0], partner)]
    lax.fori_loop(1, planes + 1, inner_plane, 0)
    for copy in halo:
        copy.wait()
    del waiting[: len(halo)]

    @pl.when(space == 0)
    def _():
        ext[0] = jnp.zeros_like(ext[0])

    @pl.when(space == n_space - 1)
    def _():
        ext[planes + 1] = jnp.zeros_like(ext[0])

    @pl.when(own == 0)
    def _():
        ext[:, 0] = jnp.zeros_like(ext[:, 0])

    @pl.when(own == n_own - 1)
    def _():
        ext[:, lines + 1] = jnp.zeros_like(ext[:, 0])

    lax.fori_loop(1, planes + 1, edge_lines, 0)
    lax.fori_loop(0, 2, outer_plane, 0)

    levels = (half, sums_1, sums_2, sums_3)
    came = (came_1, came_2, came_3)
    flights, back, to_core = {}, {}, {}

    def exchange(part):
        to_core[part] = send(
            terms.at[rows(part * 2 * PART + (1 - core) * PART, PART)],
            from_core.at[rows(part * PART, PART)],
            core_send.at[part], core_recv.at[part], partner,
        )

    def scatter(level, part):
        axis, count = (part + level) % 3, SIZES[level]
        for step in (1, 2, 3):
            target = lax.rem(coords[axis] + step, 4)
            slot = part * 3 + step - 1
            flights[(level, part, step)] = send(
                levels[level].at[rows(part * count * 4 + target * count, count)],
                came[level].at[rows(slot * count, count)],
                ring_send.at[level * 9 + slot], ring_recv.at[level * 9 + slot], ring[(axis, step)],
            )

    def merge(part):
        to_core[part].wait_recv()
        here = rows(part * PART, PART)
        half[here, :] = terms[rows(part * 2 * PART + core * PART, PART), :] + from_core[here, :]
        scatter(0, part)

    def collect(level, part):
        axis, count = (part + level) % 3, SIZES[level]
        total = levels[level][rows(part * count * 4 + coords[axis] * count, count), :]
        for step in (1, 2, 3):
            flights[(level, part, step)].wait_recv()
            total = total + came[level][rows((part * 3 + step - 1) * count, count), :]
        levels[level + 1][rows(part * count, count), :] = total
        if level < 2:
            scatter(level + 1, part)

    def send_g(stage, source, devices):
        return [
            send(source, g_came.at[stage + index], g_send.at[stage + index], g_recv.at[stage + index], device)
            for index, device in enumerate(devices)
        ]

    def add_g(stage, value, copies, target):
        for index, copy in enumerate(copies):
            copy.wait_recv()
            value = value + g_came[stage + index]
        g_sum[target] = value

    run = lines * depth
    done = 0
    started = 0
    for x_pair, y_pair, z_pairs in PAIRS:
        total = None
        for x in range(planes):
            term = jnp.dot(
                left[x + x_pair[0], :, y_pair[0] * depth : y_pair[0] * depth + run],
                right[x + x_pair[1], y_pair[1] * depth : y_pair[1] * depth + run, :],
                preferred_element_type=jnp.float32,
            )
            total = term if total is None else total + term
        for z_pair in z_pairs:
            block = total[z_pair[0] * chans : (z_pair[0] + 1) * chans, z_pair[1] * chans : (z_pair[1] + 1) * chans]
            terms[slot_place(SLOTS[(x_pair, y_pair, z_pair)])] = block
            done += 1
        if done >= (started + 1) * SLOTS_PER_PART:
            exchange(started)
            if started:
                merge(started - 1)
            started += 1
    for slot in range(done, N_SLOTS):
        terms[slot_place(slot)] = jnp.zeros((chans, chans), jnp.float32)
    exchange(2)
    merge(1)
    add_g(0, g_sum[0], g_copies, 1)
    g_copies = send_g(1, g_sum.at[1], [ring[(0, step)] for step in (1, 2, 3)])
    collect(0, 0)
    merge(2)
    collect(0, 1)
    add_g(1, g_sum[1], g_copies, 2)
    g_copies = send_g(4, g_sum.at[2], [ring[(1, step)] for step in (1, 2, 3)])
    collect(1, 0)
    collect(0, 2)
    collect(1, 1)
    add_g(4, g_sum[2], g_copies, 3)
    g_copies = send_g(7, g_sum.at[3], [ring[(2, step)] for step in (1, 2, 3)])

    def start(level, part):
        first = part * 2 * PART + core * PART
        for outer in range(level):
            first = first + coords[(part + outer) % 3] * SIZES[outer]
        return first

    def forward(part, index, coord):
        here = rows(start(0, part) + coord * SIZES[0], SIZES[0])
        slot = part * 4 + index
        back[(part, index)] = send(full.at[here], full.at[here], last_send.at[slot], last_recv.at[slot], partner)

    def spread(level, part):
        axis, count = (part + level) % 3, SIZES[level]
        here = rows(start(level, part) + coords[axis] * count, count)
        for step in (1, 2, 3):
            slot = level * 9 + part * 3 + step - 1
            back[(level, part, step)] = send(
                full.at[here], full.at[here], back_send.at[slot], back_recv.at[slot], ring[(axis, step)]
            )
        if level == 0:
            forward(part, 0, coords[axis])

    def gathered(level, part):
        axis = (part + level) % 3
        for step in (1, 2, 3):
            back[(level, part, step)].wait_recv()
            if level == 0:
                forward(part, step, lax.rem(coords[axis] + 4 - step, 4))
        if level:
            spread(level - 1, part)

    def turn(part):
        collect(2, part)
        here = rows(start(3, part), SIZES[2])
        full[here, :] = sums_3[rows(part * SIZES[2], SIZES[2]), :]
        spread(2, part)

    turn(0)
    collect(1, 2)
    turn(1)
    gathered(2, 0)
    turn(2)
    gathered(2, 1)
    gathered(1, 0)
    gathered(2, 2)
    gathered(1, 1)
    add_g(7, g_sum[3], g_copies, 4)
    gathered(1, 2)
    diagonal = lax.broadcasted_iota(jnp.int32, (CH, 2 * CH), 0) == lax.broadcasted_iota(jnp.int32, (CH, 2 * CH), 1)
    weights = inverse_row(g_sum[4] * inv_cells + jnp.where(diagonal, damping, 0.0), own * 8 + space // 2)
    for copy in to_owners:
        copy.wait_recv()
    row_out[...] = jnp.zeros_like(row_out)
    for owner in range(n_own):
        piece = jnp.sum(grads[owner] * weights, axis=0, keepdims=True)
        row_out[:, owner * lanes : (owner + 1) * lanes] = piece[:, :lanes]
    for part in range(3):
        gathered(0, part)
    for part in range(3):
        for index in range(4):
            back[(part, index)].wait_recv()
    for copy in waiting:
        copy.wait_send()


def front(base, cots, grad, inv_cells, size):
    planes, lines, chans, depth = base.shape
    vmem = pl.BlockSpec(memory_space=pltpu.VMEM)
    lanes = 2 * CH
    dma = pltpu.SemaphoreType.DMA
    counts = [HALF, HALF] + [3 * count for count in SIZES] + [9 * count for count in SIZES]
    return pl.pallas_call(
        functools.partial(front_kernel, inv_cells),
        out_shape=[
            jax.ShapeDtypeStruct((ROWS, lanes), jnp.float32),
            jax.ShapeDtypeStruct((1, size), jnp.float32),
        ],
        in_specs=[vmem] * 3,
        out_specs=[vmem] * 2,
        scratch_shapes=[
            pltpu.VMEM((planes + 2, lines + 2, chans, depth), jnp.bfloat16),
            pltpu.VMEM((planes + 2, 3 * chans, (lines + 2) * depth), jnp.bfloat16),
            pltpu.VMEM((planes + 2, (lines + 2) * depth, 3 * chans), jnp.bfloat16),
            pltpu.VMEM((ROWS, lanes), jnp.float32),
        ]
        + [pltpu.VMEM((count, lanes), jnp.float32) for count in counts]
        + [pltpu.VMEM((count, CH, lanes), jnp.float32) for count in (5, 10)]
        + [pltpu.VMEM((8, CH, -(-grad.shape[1] // lanes) * lanes), jnp.float32)]
        + [dma((count,)) for count in (8, 8, 3, 3, 27, 27, 27, 27, 12, 12, 10, 10, 7, 7)],
        compiler_params=pltpu.CompilerParams(
            collective_id=1, has_side_effects=True, vmem_limit_bytes=48 * 2**20
        ),
    )(base, cots, grad)


def times_factor(factor, row):
    size = factor.shape[0]
    parts = []
    for base in range(0, size, 128):
        rows = factor[pl.ds(base, 128), :].reshape(16, 8, size)
        total = jnp.zeros((16, 8, 128), jnp.float32)
        for lane in range(0, size, 128):
            total = total + rows[:, :, lane : lane + 128] * row[None, :, lane : lane + 128]
        flipped = total.reshape(128, 128).T
        parts.append(jnp.broadcast_to(jnp.sum(flipped, axis=0, keepdims=True), (8, 128)))
    return jnp.concatenate(parts, axis=1)


def halves(value):
    high = value.astype(jnp.bfloat16)
    return high, (value - high.astype(jnp.float32)).astype(jnp.bfloat16)


def frobenius(full, inv_cells, eye):
    counts = {}
    for row in range(27):
        for col in range(row, 27):
            slot = block_slot(row, col)
            counts[slot] = counts.get(slot, 0) + (1 if row == col else 2)
    plain = jnp.zeros((CH, CH), jnp.float32)
    for slot, count in counts.items():
        block = full[slot_place(slot)] * inv_cells
        if slot in DIAGONAL:
            block = block + eye
        plain = plain + float(count) * (block * block)
    return jnp.sum(plain, keepdims=True)


def assemble(full, inverse, inv_cells, eye, factor, high, low):
    size = factor.shape[0]
    width = 27 * CH
    for ref in (factor, high, low):
        ref[width:, :] = jnp.zeros((size - width, size), ref.dtype)
        ref[:, width:] = jnp.zeros((size, size - width), ref.dtype)

    def put(rows, cols, value):
        factor[rows, cols] = value
        high[rows, cols], low[rows, cols] = halves(value)

    for row in range(27):
        for col in range(row, 27):
            block = full[slot_place(block_slot(row, col))] * inv_cells
            if row == col:
                block = block + eye
            block = block * inverse
            rows, cols = slice(row * CH, (row + 1) * CH), slice(col * CH, (col + 1) * CH)
            put(rows, cols, block)
            if row != col and row * CH // TILE == col * CH // TILE:
                put(cols, rows, block.T)
    tiles = size // TILE
    for row in range(tiles):
        for col in range(row + 1, tiles):
            rows, cols = slice(row * TILE, (row + 1) * TILE), slice(col * TILE, (col + 1) * TILE)
            put(cols, rows, factor[rows, cols].T)


def poly_kernel(
    inv_cells, full, row_ref, out, factor, high_a, low_a, high_b, low_b, pieces, came,
    tile_send, tile_recv, ready, share_send, share_recv,
):
    space, own = lax.axis_index("space"), lax.axis_index("own")
    core, chip = lax.rem(space, 2), space // 2
    partner = {"space": space + 1 - 2 * core, "own": own}
    peers = [{"space": lax.rem(space + 2 * step, 16), "own": own} for step in range(1, 8)]
    meet([partner] + peers)
    size = factor.shape[0]
    tiles = size // TILE
    eye = jnp.where(
        lax.broadcasted_iota(jnp.int32, (CH, CH), 0) == lax.broadcasted_iota(jnp.int32, (CH, CH), 1), damping, 0.0
    )
    inverse = 1.0 / jnp.sqrt(frobenius(full, inv_cells, eye))
    assemble(full, inverse, inv_cells, eye, factor, high_a, low_a)
    row = jnp.broadcast_to(row_ref[...], (8, size)) * inverse
    dot = functools.partial(jnp.dot, preferred_element_type=jnp.float32)
    operands = ((high_a, low_a), (high_b, low_b))

    def place(i, half, which):
        j = lax.rem(i + 2 * half + which, tiles)
        return (
            pl.ds(pl.multiple_of(i * TILE, TILE), TILE),
            pl.ds(pl.multiple_of(j * TILE, TILE), TILE),
        )

    def tile_copy(i, which):
        here = factor.at[place(i, core, which)]
        return pltpu.make_async_remote_copy(
            src_ref=here,
            dst_ref=here,
            send_sem=tile_send.at[2 * i + which],
            recv_sem=tile_recv.at[2 * i + which],
            device_id=partner,
            device_id_type=MESH,
        )

    for step in range(SQUARINGS):
        (high, low), (next_high, next_low) = operands[step % 2], operands[1 - step % 2]
        row = 2.0 * row - times_factor(factor, row)
        pl.semaphore_signal(ready, inc=1, device_id=partner, device_id_type=MESH)

        def finish(i, half, which, fresh, step=step, next_high=next_high, next_low=next_low):
            rows, cols = place(i, half, which)
            flipped = fresh.T
            if which == 0:
                flipped = jnp.where(half == 0, fresh, flipped)
            factor[cols, rows] = flipped
            if step < SQUARINGS - 1:
                next_high[rows, cols], next_low[rows, cols] = halves(fresh)
                next_high[cols, rows], next_low[cols, rows] = halves(flipped)

        def compute(i, step=step, high=high, low=low, finish=finish):
            for which in range(2):
                rows, cols = place(i, core, which)
                square = dot(high[rows, :], high[:, cols])
                if step:
                    square = square + (dot(high[rows, :], low[:, cols]) + dot(low[rows, :], high[:, cols]))
                fresh = 2.0 * factor[rows, cols] - square
                factor[rows, cols] = fresh
                finish(i, core, which, fresh)

        def adopt(i, finish=finish):
            for which in range(2):
                finish(i, 1 - core, which, factor[place(i, 1 - core, which)])

        def send_tiles(i):
            for which in range(2):
                tile_copy(i, which).start()

        def first_tiles(i, carry, compute=compute):
            compute(i)

            @pl.when(i == 0)
            def _():
                pl.semaphore_wait(ready, 1)

            send_tiles(i)
            return carry

        def next_tiles(i, carry, compute=compute, adopt=adopt):
            for which in range(2):
                tile_copy(i - LAG, which).wait_recv()
            adopt(i - LAG)
            compute(i)
            send_tiles(i)
            return carry

        def last_tiles(i, carry, adopt=adopt):
            for which in range(2):
                tile_copy(i, which).wait_recv()
            adopt(i)
            return carry

        lax.fori_loop(0, LAG, first_tiles, 0)
        lax.fori_loop(LAG, tiles, next_tiles, 0)
        lax.fori_loop(tiles - LAG, tiles, last_tiles, 0)
        for index in range(2 * tiles):
            tile_copy(index // 2, index % 2).wait_send()

    def horner(index, value):
        return row + (value - times_factor(factor, value))

    value = lax.fori_loop(0, 2 ** (8 - SQUARINGS) - 1, horner, row)

    lanes = out.shape[1]
    for index in range(16):
        pieces[index, :, :lanes] = value[:, index * lanes : (index + 1) * lanes]
        pieces[index, :, lanes:] = jnp.zeros((8, 128 - lanes), jnp.float32)
    copies = []
    for index, peer in enumerate(peers):
        copy = pltpu.make_async_remote_copy(
            src_ref=pieces.at[peer["space"]],
            dst_ref=came.at[chip],
            send_sem=share_send.at[index],
            recv_sem=share_recv.at[index],
            device_id=peer,
            device_id_type=MESH,
        )
        copy.start()
        copies.append(copy)
    came[chip] = pieces[space]
    for copy in copies:
        copy.wait()
    for index in range(8):
        out[index : index + 1, :] = came[index, :1, :lanes]


def polynomial(full, row, inv_cells, lanes):
    size = row.shape[1]
    tiles = size // TILE
    vmem = pl.BlockSpec(memory_space=pltpu.VMEM)
    dma = pltpu.SemaphoreType.DMA
    return pl.pallas_call(
        functools.partial(poly_kernel, inv_cells),
        out_shape=jax.ShapeDtypeStruct((8, lanes), jnp.float32),
        in_specs=[vmem, vmem],
        out_specs=vmem,
        scratch_shapes=[pltpu.VMEM((size, size), jnp.float32)]
        + [pltpu.VMEM((size, size), jnp.bfloat16)] * 4
        + [pltpu.VMEM((16, 8, 128), jnp.float32), pltpu.VMEM((8, 8, 128), jnp.float32)]
        + [dma((2 * tiles,)), dma((2 * tiles,)), pltpu.SemaphoreType.REGULAR, dma((7,)), dma((7,))],
        compiler_params=pltpu.CompilerParams(
            collective_id=2, has_side_effects=True, vmem_limit_bytes=56 * 2**20
        ),
    )(full, row)


def body(acts, cotangents, weight_grad):
    chans, block_x, block_y, depth_z = acts.shape
    c_out = cotangents.shape[0]
    width = 27 * chans
    n_space = lax.axis_size("space")
    n_own = lax.axis_size("own")
    inv_cells = 1.0 / (block_x * n_space * block_y * n_own * depth_z)
    size = -(-width // TILE) * TILE
    base = jnp.transpose(acts, (1, 2, 0, 3))
    full, row = front(base, cotangents.reshape(c_out, -1), weight_grad, inv_cells, size)
    return polynomial(full, row, inv_cells, width // n_space)


def solution(mesh):
    in_specs = (P(None, "space", "own", None), P(None, "space", "own", None), P(None, "own"))
    out_specs = P("own", "space")
    return jax.shard_map(body, mesh=mesh, in_specs=in_specs, out_specs=out_specs, check_vma=False)
```

```python
import functools

import jax
import jax.numpy as jnp
from jax import lax
from jax.experimental import pallas as pl
from jax.experimental.pallas import tpu as pltpu
from jax.sharding import PartitionSpec as P

SQUARINGS = 3
TILE = 256
LAG = 3
CH = 64
NZ = 256
damping = 0.05
MESH = pl.DeviceIdType.MESH
SAME = ((0, 0), (1, 1), (2, 2))
UP = ((0, 1), (0, 2))
DOWN = ((1, 0), (2, 0))


def pair_type(first, second):
    if first == second:
        return (first, second)
    apart = second - first
    return (0, apart) if apart > 0 else (-apart, 0)


def distinct_pairs():
    pairs = []
    for x_pair in SAME + UP:
        for y_pair in SAME + UP + (DOWN if x_pair in UP else ()):
            full = x_pair in UP or y_pair in UP
            pairs.append((x_pair, y_pair, SAME + UP + (DOWN if full else ())))
    return pairs


PAIRS = distinct_pairs()
SLOTS = {}
for _x_pair, _y_pair, _z_pairs in PAIRS:
    for _z_pair in _z_pairs:
        SLOTS[(_x_pair, _y_pair, _z_pair)] = len(SLOTS)
N_SLOTS = 192
ROWS = N_SLOTS // 2 * CH


def slot_place(slot):
    return slice(slot // 2 * CH, slot // 2 * CH + CH), slice(slot % 2 * CH, slot % 2 * CH + CH)


def block_slot(row, col):
    return SLOTS[
        tuple(
            pair_type(row // unit % 3, col // unit % 3) for unit in (9, 3, 1)
        )
    ]


DIAGONAL = {block_slot(index, index) for index in range(27)}


def meet(peers):
    barrier = pltpu.get_barrier_semaphore()
    for peer in peers:
        pl.semaphore_signal(barrier, inc=1, device_id=peer, device_id_type=MESH)
    pl.semaphore_wait(barrier, len(peers))


def inverse_columns(matrix, first, apart):
    size = matrix.shape[0]
    lane = lax.broadcasted_iota(jnp.int32, (size, 128), 1)
    sub = lax.broadcasted_iota(jnp.int32, (size, 128), 0)
    wanted = (lane >= size) & (lane < size + 8) & (sub == first + apart * (lane - size))
    work = jnp.where(lane < size, matrix, jnp.where(wanted, 1.0, 0.0))
    for step in range(size):
        pivot = work[step : step + 1, :] / work[step : step + 1, step : step + 1]
        work = jnp.where(sub == step, pivot, work - work[:, step : step + 1] * pivot)
    return [work[:, size + index : size + index + 1] for index in range(8)]


HALF = ROWS // 2
PART = HALF // 3
SLOTS_PER_PART = N_SLOTS // 3
SIZES = (PART // 4, PART // 16)


def front_kernel(
    inv_cells, base, cots, grad, full, row_out,
    ext, left, right, terms, half, from_core, sums_1, sums_2, came_0, came_1, came_2, g_sum, g_came, products, shares,
    halo_send, halo_recv, core_send, core_recv, ring_send, ring_recv, back_send, back_recv,
    last_send, last_recv, g_send, g_recv, w_send, w_recv,
):
    space, own = lax.axis_index("space"), lax.axis_index("own")
    n_space, n_own = lax.axis_size("space"), lax.axis_size("own")
    core, ypos, z_lo = lax.rem(space, 2), lax.rem(space // 2, 4), space // 8
    xpos, z_hi = lax.rem(own, 4), own // 4
    coords = (xpos, ypos, z_hi * 2 + z_lo)
    planes, lines, chans, depth = base.shape
    lanes = grad.shape[1]

    def peer(axis, coord):
        if axis == 0:
            return {"space": space, "own": own - xpos + coord}
        if axis == 1:
            return {"space": space + 2 * (coord - ypos), "own": own}
        return {"space": space + 8 * (lax.rem(coord, 2) - z_lo), "own": coord // 2 * 4 + xpos}

    partner = {"space": space + 1 - 2 * core, "own": own}
    ring = {
        (axis, step): peer(axis, lax.rem(coords[axis] + step, 4)) for axis in range(3) for step in (1, 2, 3)
    }
    owners = [{"space": space, "own": lax.rem(own + step, n_own)} for step in range(1, n_own)]
    steps = [(dx, dy) for dx in (-1, 0, 1) for dy in (-1, 0, 1) if dx or dy]
    around = [
        {"space": lax.rem(space + dx + n_space, n_space), "own": lax.rem(own + dy + n_own, n_own)}
        for dx, dy in steps
    ]
    ext[1 : 1 + planes, 1 : 1 + lines] = base[...]
    products[...] = jnp.zeros_like(products)
    meet([partner] + list(ring.values()) + owners + around)

    def rows(start, count):
        return pl.ds(pl.multiple_of(start, 8), count)

    waiting = []

    def send(src, dst, send_sem, recv_sem, device):
        copy = pltpu.make_async_remote_copy(
            src_ref=src, dst_ref=dst, send_sem=send_sem, recv_sem=recv_sem, device_id=device, device_id_type=MESH
        )
        copy.start()
        waiting.append(copy)
        return copy

    def ends(step, count):
        if step == 0:
            return pl.ds(1, count), pl.ds(1, count)
        return (pl.ds(count, 1), pl.ds(0, 1)) if step > 0 else (pl.ds(1, 1), pl.ds(count + 1, 1))

    halo = []
    for index, (dx, dy) in enumerate(steps):
        (from_x, to_x), (from_y, to_y) = ends(dx, planes), ends(dy, lines)
        halo.append(
            send(ext.at[from_x, from_y], ext.at[to_x, to_y], halo_send.at[index], halo_recv.at[index], around[index])
        )

    lane = lax.broadcasted_iota(jnp.int32, (chans, depth), 1)

    def shift_line(x, y):
        here = ext[x, y].astype(jnp.float32)
        before = jnp.where(lane == 0, 0.0, pltpu.roll(here, 1, 1))
        after = jnp.where(lane == depth - 1, 0.0, pltpu.roll(here, depth - 1, 1))
        stack = jnp.concatenate([before, here, after], axis=0)
        across = slice(y * depth, (y + 1) * depth)
        left[x, :, across] = stack.astype(left.dtype)
        right[x, across, :] = stack.T.astype(right.dtype)

    def shift_lines(x, ys):
        for y in ys:
            shift_line(x, y)

    def inner_plane(x, carry):
        shift_lines(x, range(1, lines + 1))
        return carry

    def edge_lines(x, carry):
        shift_lines(x, (0, lines + 1))
        return carry

    def outer_plane(index, carry):
        shift_lines(index * (planes + 1), range(lines + 2))
        return carry

    g_sum[0] = jnp.zeros_like(g_sum[0])
    g_sum[0, :, :chans] = lax.dot_general(
        cots[...], cots[...], (((1,), (1,)), ((), ())), preferred_element_type=jnp.float32
    )
    g_copies = [send(g_sum.at[0], g_came.at[0], g_send.at[0], g_recv.at[0], partner)]
    lax.fori_loop(1, planes + 1, inner_plane, 0)
    for copy in halo:
        copy.wait()
    del waiting[: len(halo)]

    @pl.when(space == 0)
    def _():
        ext[0] = jnp.zeros_like(ext[0])

    @pl.when(space == n_space - 1)
    def _():
        ext[planes + 1] = jnp.zeros_like(ext[0])

    @pl.when(own == 0)
    def _():
        ext[:, 0] = jnp.zeros_like(ext[:, 0])

    @pl.when(own == n_own - 1)
    def _():
        ext[:, lines + 1] = jnp.zeros_like(ext[:, 0])

    lax.fori_loop(1, planes + 1, edge_lines, 0)
    lax.fori_loop(0, 2, outer_plane, 0)

    levels = (half, sums_1, sums_2)
    came = (came_0, came_1)
    flights, back, to_core = {}, {}, {}

    def exchange(part):
        to_core[part] = send(
            terms.at[rows(part * 2 * PART + (1 - core) * PART, PART)],
            from_core.at[rows(part * PART, PART)],
            core_send.at[part], core_recv.at[part], partner,
        )

    def scatter(level, part):
        axis, count = (part + level) % 3, SIZES[level]
        for step in (1, 2, 3):
            target = lax.rem(coords[axis] + step, 4)
            slot = part * 3 + step - 1
            flights[(level, part, step)] = send(
                levels[level].at[rows(part * count * 4 + target * count, count)],
                came[level].at[rows(slot * count, count)],
                ring_send.at[level * 9 + slot], ring_recv.at[level * 9 + slot], ring[(axis, step)],
            )

    def merge(part):
        to_core[part].wait_recv()
        here = rows(part * PART, PART)
        half[here, :] = terms[rows(part * 2 * PART + core * PART, PART), :] + from_core[here, :]
        scatter(0, part)

    def collect(level, part):
        axis, count = (part + level) % 3, SIZES[level]
        total = levels[level][rows(part * count * 4 + coords[axis] * count, count), :]
        for step in (1, 2, 3):
            flights[(level, part, step)].wait_recv()
            total = total + came[level][rows((part * 3 + step - 1) * count, count), :]
        levels[level + 1][rows(part * count, count), :] = total
        if level == 0:
            scatter(1, part)
        else:
            swap(part)

    def swap(part):
        axis, count = (part + 2) % 3, SIZES[1]
        mine = rows((part * 4 + coords[axis]) * count, count)
        for step in (1, 2, 3):
            slot = 18 + part * 3 + step - 1
            flights[(2, part, step)] = send(
                sums_2.at[rows(part * count, count)], came_2.at[mine], ring_send.at[slot], ring_recv.at[slot],
                ring[(axis, step)],
            )
        came_2[mine, :] = sums_2[rows(part * count, count), :]

    def settle(part):
        count = SIZES[1]
        for step in (1, 2, 3):
            flights[(2, part, step)].wait_recv()
        total = came_2[rows(part * 4 * count, count), :]
        for coord in (1, 2, 3):
            total = total + came_2[rows((part * 4 + coord) * count, count), :]
        full[rows(start(2, part), count), :] = total
        spread(1, part)

    def send_g(stage, source, devices):
        return [
            send(source, g_came.at[stage + index], g_send.at[stage + index], g_recv.at[stage + index], device)
            for index, device in enumerate(devices)
        ]

    def add_g(stage, value, copies, target):
        for index, copy in enumerate(copies):
            copy.wait_recv()
            value = value + g_came[stage + index]
        g_sum[target] = value

    run = lines * depth
    done = 0
    started = 0
    for x_pair, y_pair, z_pairs in PAIRS:
        total = None
        for x in range(planes):
            term = jnp.dot(
                left[x + x_pair[0], :, y_pair[0] * depth : y_pair[0] * depth + run],
                right[x + x_pair[1], y_pair[1] * depth : y_pair[1] * depth + run, :],
                preferred_element_type=jnp.float32,
            )
            total = term if total is None else total + term
        for z_pair in z_pairs:
            block = total[z_pair[0] * chans : (z_pair[0] + 1) * chans, z_pair[1] * chans : (z_pair[1] + 1) * chans]
            terms[slot_place(SLOTS[(x_pair, y_pair, z_pair)])] = block
            done += 1
        if done >= (started + 1) * SLOTS_PER_PART:
            exchange(started)
            if started:
                merge(started - 1)
            started += 1
    for slot in range(done, N_SLOTS):
        terms[slot_place(slot)] = jnp.zeros((chans, chans), jnp.float32)
    exchange(2)
    merge(1)
    merge(2)
    add_g(0, g_sum[0], g_copies, 1)
    g_copies = send_g(1, g_sum.at[1], [ring[(0, step)] for step in (1, 2, 3)])
    collect(0, 0)
    collect(0, 1)
    collect(0, 2)
    add_g(1, g_sum[1], g_copies, 2)
    g_copies = send_g(4, g_sum.at[2], [ring[(1, step)] for step in (1, 2, 3)])
    collect(1, 0)
    collect(1, 1)
    collect(1, 2)
    add_g(4, g_sum[2], g_copies, 3)
    g_copies = send_g(7, g_sum.at[3], [ring[(2, step)] for step in (1, 2, 3)])

    def start(level, part):
        first = part * 2 * PART + core * PART
        for outer in range(level):
            first = first + coords[(part + outer) % 3] * SIZES[outer]
        return first

    def forward(part, index, coord):
        here = rows(start(0, part) + coord * SIZES[0], SIZES[0])
        slot = part * 4 + index
        back[(part, index)] = send(full.at[here], full.at[here], last_send.at[slot], last_recv.at[slot], partner)

    def spread(level, part):
        axis, count = (part + level) % 3, SIZES[level]
        here = rows(start(level, part) + coords[axis] * count, count)
        for step in (1, 2, 3):
            slot = level * 9 + part * 3 + step - 1
            back[(level, part, step)] = send(
                full.at[here], full.at[here], back_send.at[slot], back_recv.at[slot], ring[(axis, step)]
            )
        if level == 0:
            forward(part, 0, coords[axis])

    def gathered(level, part):
        axis = (part + level) % 3
        for step in (1, 2, 3):
            back[(level, part, step)].wait_recv()
            if level == 0:
                forward(part, step, lax.rem(coords[axis] + 4 - step, 4))
        if level:
            spread(level - 1, part)

    for part in range(3):
        settle(part)
    add_g(7, g_sum[3], g_copies, 4)
    diagonal = lax.broadcasted_iota(jnp.int32, (CH, 2 * CH), 0) == lax.broadcasted_iota(jnp.int32, (CH, 2 * CH), 1)
    g_factor = g_sum[4] * inv_cells + jnp.where(diagonal, damping, 0.0)
    for owner, weights in enumerate(inverse_columns(g_factor, space // 2, 8)):
        products[owner, :1, :lanes] = jnp.sum(grad[...] * weights, axis=0, keepdims=True)
    to_owners = [
        send(products.at[owner["own"]], shares.at[own], w_send.at[index], w_recv.at[index], owner)
        for index, owner in enumerate(owners)
    ]
    shares[own] = products[own]
    for part in range(3):
        gathered(1, part)
    for part in range(3):
        gathered(0, part)
    for copy in to_owners:
        copy.wait_recv()
    row_out[...] = jnp.zeros_like(row_out)
    for owner in range(n_own):
        row_out[:, owner * lanes : (owner + 1) * lanes] = shares[owner, :1, :lanes]
    for part in range(3):
        for index in range(4):
            back[(part, index)].wait_recv()
    for copy in waiting:
        copy.wait_send()


def front(base, cots, grad, inv_cells, size):
    planes, lines, chans, depth = base.shape
    vmem = pl.BlockSpec(memory_space=pltpu.VMEM)
    lanes = 2 * CH
    dma = pltpu.SemaphoreType.DMA
    counts = [HALF, HALF, 3 * SIZES[0], 3 * SIZES[1], 9 * SIZES[0], 9 * SIZES[1], 12 * SIZES[1]]
    return pl.pallas_call(
        functools.partial(front_kernel, inv_cells),
        out_shape=[
            jax.ShapeDtypeStruct((ROWS, lanes), jnp.float32),
            jax.ShapeDtypeStruct((1, size), jnp.float32),
        ],
        in_specs=[vmem] * 3,
        out_specs=[vmem] * 2,
        scratch_shapes=[
            pltpu.VMEM((planes + 2, lines + 2, chans, depth), jnp.bfloat16),
            pltpu.VMEM((planes + 2, 3 * chans, (lines + 2) * depth), jnp.bfloat16),
            pltpu.VMEM((planes + 2, (lines + 2) * depth, 3 * chans), jnp.bfloat16),
            pltpu.VMEM((ROWS, lanes), jnp.float32),
        ]
        + [pltpu.VMEM((count, lanes), jnp.float32) for count in counts]
        + [pltpu.VMEM((count, CH, lanes), jnp.float32) for count in (5, 10)]
        + [pltpu.VMEM((8, 8, -(-grad.shape[1] // lanes) * lanes), jnp.float32)] * 2
        + [dma((count,)) for count in (8, 8, 3, 3, 27, 27, 18, 18, 12, 12, 10, 10, 7, 7)],
        compiler_params=pltpu.CompilerParams(
            collective_id=1, has_side_effects=True, vmem_limit_bytes=48 * 2**20
        ),
    )(base, cots, grad)


def times_factor(factor, row):
    size = factor.shape[0]
    parts = []
    for base in range(0, size, 128):
        rows = factor[pl.ds(base, 128), :].reshape(16, 8, size)
        total = jnp.zeros((16, 8, 128), jnp.float32)
        for lane in range(0, size, 128):
            total = total + rows[:, :, lane : lane + 128] * row[None, :, lane : lane + 128]
        flipped = total.reshape(128, 128).T
        parts.append(jnp.broadcast_to(jnp.sum(flipped, axis=0, keepdims=True), (8, 128)))
    return jnp.concatenate(parts, axis=1)


def halves(value):
    high = value.astype(jnp.bfloat16)
    return high, (value - high.astype(jnp.float32)).astype(jnp.bfloat16)


def frobenius(full, inv_cells, eye):
    counts = {}
    for row in range(27):
        for col in range(row, 27):
            slot = block_slot(row, col)
            counts[slot] = counts.get(slot, 0) + (1 if row == col else 2)
    plain = jnp.zeros((CH, CH), jnp.float32)
    for slot, count in counts.items():
        block = full[slot_place(slot)] * inv_cells
        if slot in DIAGONAL:
            block = block + eye
        plain = plain + float(count) * (block * block)
    return jnp.sum(plain, keepdims=True)


def assemble(full, inverse, inv_cells, eye, factor, high, low):
    size = factor.shape[0]
    width = 27 * CH
    for ref in (factor, high, low):
        ref[width:, :] = jnp.zeros((size - width, size), ref.dtype)
        ref[:, width:] = jnp.zeros((size, size - width), ref.dtype)

    def put(rows, cols, value):
        factor[rows, cols] = value
        high[rows, cols], low[rows, cols] = halves(value)

    for row in range(27):
        for col in range(row, 27):
            block = full[slot_place(block_slot(row, col))] * inv_cells
            if row == col:
                block = block + eye
            block = block * inverse
            rows, cols = slice(row * CH, (row + 1) * CH), slice(col * CH, (col + 1) * CH)
            put(rows, cols, block)
            if row != col and row * CH // TILE == col * CH // TILE:
                put(cols, rows, block.T)
    tiles = size // TILE
    for row in range(tiles):
        for col in range(row + 1, tiles):
            rows, cols = slice(row * TILE, (row + 1) * TILE), slice(col * TILE, (col + 1) * TILE)
            put(cols, rows, factor[rows, cols].T)


def poly_kernel(
    inv_cells, full, row_ref, out, factor, high_a, low_a, high_b, low_b, pieces, came,
    tile_send, tile_recv, ready, share_send, share_recv,
):
    space, own = lax.axis_index("space"), lax.axis_index("own")
    core, chip = lax.rem(space, 2), space // 2
    partner = {"space": space + 1 - 2 * core, "own": own}
    peers = [{"space": lax.rem(space + 2 * step, 16), "own": own} for step in range(1, 8)]
    meet([partner] + peers)
    size = factor.shape[0]
    tiles = size // TILE
    eye = jnp.where(
        lax.broadcasted_iota(jnp.int32, (CH, CH), 0) == lax.broadcasted_iota(jnp.int32, (CH, CH), 1), damping, 0.0
    )
    inverse = 1.0 / jnp.sqrt(frobenius(full, inv_cells, eye))
    assemble(full, inverse, inv_cells, eye, factor, high_a, low_a)
    row = jnp.broadcast_to(row_ref[...], (8, size)) * inverse
    dot = functools.partial(jnp.dot, preferred_element_type=jnp.float32)
    operands = ((high_a, low_a), (high_b, low_b))

    def place(i, half, which):
        j = lax.rem(i + 2 * half + which, tiles)
        return (
            pl.ds(pl.multiple_of(i * TILE, TILE), TILE),
            pl.ds(pl.multiple_of(j * TILE, TILE), TILE),
        )

    def tile_copy(i, which):
        here = factor.at[place(i, core, which)]
        return pltpu.make_async_remote_copy(
            src_ref=here,
            dst_ref=here,
            send_sem=tile_send.at[2 * i + which],
            recv_sem=tile_recv.at[2 * i + which],
            device_id=partner,
            device_id_type=MESH,
        )

    for step in range(SQUARINGS):
        (high, low), (next_high, next_low) = operands[step % 2], operands[1 - step % 2]
        row = 2.0 * row - times_factor(factor, row)
        pl.semaphore_signal(ready, inc=1, device_id=partner, device_id_type=MESH)

        def finish(i, half, which, fresh, step=step, next_high=next_high, next_low=next_low):
            rows, cols = place(i, half, which)
            flipped = fresh.T
            if which == 0:
                flipped = jnp.where(half == 0, fresh, flipped)
            factor[cols, rows] = flipped
            if step < SQUARINGS - 1:
                next_high[rows, cols], next_low[rows, cols] = halves(fresh)
                next_high[cols, rows], next_low[cols, rows] = halves(flipped)

        def compute(i, step=step, high=high, low=low, finish=finish):
            for which in range(2):
                rows, cols = place(i, core, which)
                square = dot(high[rows, :], high[:, cols])
                if step:
                    square = square + (dot(high[rows, :], low[:, cols]) + dot(low[rows, :], high[:, cols]))
                fresh = 2.0 * factor[rows, cols] - square
                factor[rows, cols] = fresh
                finish(i, core, which, fresh)

        def adopt(i, finish=finish):
            for which in range(2):
                finish(i, 1 - core, which, factor[place(i, 1 - core, which)])

        def send_tiles(i):
            for which in range(2):
                tile_copy(i, which).start()

        def first_tiles(i, carry, compute=compute):
            compute(i)

            @pl.when(i == 0)
            def _():
                pl.semaphore_wait(ready, 1)

            send_tiles(i)
            return carry

        def next_tiles(i, carry, compute=compute, adopt=adopt):
            for which in range(2):
                tile_copy(i - LAG, which).wait_recv()
            adopt(i - LAG)
            compute(i)
            send_tiles(i)
            return carry

        def last_tiles(i, carry, adopt=adopt):
            for which in range(2):
                tile_copy(i, which).wait_recv()
            adopt(i)
            return carry

        lax.fori_loop(0, LAG, first_tiles, 0)
        lax.fori_loop(LAG, tiles, next_tiles, 0)
        lax.fori_loop(tiles - LAG, tiles, last_tiles, 0)
        for index in range(2 * tiles):
            tile_copy(index // 2, index % 2).wait_send()

    def horner(index, value):
        return row + (value - times_factor(factor, value))

    value = lax.fori_loop(0, 2 ** (8 - SQUARINGS) - 1, horner, row)

    lanes = out.shape[1]
    for index in range(16):
        pieces[index, :, :lanes] = value[:, index * lanes : (index + 1) * lanes]
        pieces[index, :, lanes:] = jnp.zeros((8, 128 - lanes), jnp.float32)
    copies = []
    for index, peer in enumerate(peers):
        copy = pltpu.make_async_remote_copy(
            src_ref=pieces.at[peer["space"]],
            dst_ref=came.at[chip],
            send_sem=share_send.at[index],
            recv_sem=share_recv.at[index],
            device_id=peer,
            device_id_type=MESH,
        )
        copy.start()
        copies.append(copy)
    came[chip] = pieces[space]
    for copy in copies:
        copy.wait()
    for index in range(8):
        out[index : index + 1, :] = came[index, :1, :lanes]


def polynomial(full, row, inv_cells, lanes):
    size = row.shape[1]
    tiles = size // TILE
    vmem = pl.BlockSpec(memory_space=pltpu.VMEM)
    dma = pltpu.SemaphoreType.DMA
    return pl.pallas_call(
        functools.partial(poly_kernel, inv_cells),
        out_shape=jax.ShapeDtypeStruct((8, lanes), jnp.float32),
        in_specs=[vmem, vmem],
        out_specs=vmem,
        scratch_shapes=[pltpu.VMEM((size, size), jnp.float32)]
        + [pltpu.VMEM((size, size), jnp.bfloat16)] * 4
        + [pltpu.VMEM((16, 8, 128), jnp.float32), pltpu.VMEM((8, 8, 128), jnp.float32)]
        + [dma((2 * tiles,)), dma((2 * tiles,)), pltpu.SemaphoreType.REGULAR, dma((7,)), dma((7,))],
        compiler_params=pltpu.CompilerParams(
            collective_id=2, has_side_effects=True, vmem_limit_bytes=56 * 2**20
        ),
    )(full, row)


def body(acts, cotangents, weight_grad):
    chans, block_x, block_y, depth_z = acts.shape
    c_out = cotangents.shape[0]
    width = 27 * chans
    n_space = lax.axis_size("space")
    n_own = lax.axis_size("own")
    inv_cells = 1.0 / (block_x * n_space * block_y * n_own * depth_z)
    size = -(-width // TILE) * TILE
    base = jnp.transpose(acts, (1, 2, 0, 3))
    full, row = front(base, cotangents.reshape(c_out, -1), weight_grad, inv_cells, size)
    return polynomial(full, row, inv_cells, width // n_space)


def solution(mesh):
    in_specs = (P(None, "space", "own", None), P(None, "space", "own", None), P(None, "own"))
    out_specs = P("own", "space")
    return jax.shard_map(body, mesh=mesh, in_specs=in_specs, out_specs=out_specs, check_vma=False)
```

```python
import functools

import jax
import jax.numpy as jnp
from jax import lax
from jax.experimental import pallas as pl
from jax.experimental.pallas import tpu as pltpu
from jax.sharding import PartitionSpec as P

SQUARINGS = 3
TILE = 256
LAG = 3
CH = 64
NZ = 256
damping = 0.05
MESH = pl.DeviceIdType.MESH
SAME = ((0, 0), (1, 1), (2, 2))
UP = ((0, 1), (0, 2))
DOWN = ((1, 0), (2, 0))


def pair_type(first, second):
    if first == second:
        return (first, second)
    apart = second - first
    return (0, apart) if apart > 0 else (-apart, 0)


def distinct_pairs():
    pairs = []
    for x_pair in SAME + UP:
        for y_pair in SAME + UP + (DOWN if x_pair in UP else ()):
            full = x_pair in UP or y_pair in UP
            pairs.append((x_pair, y_pair, SAME + UP + (DOWN if full else ())))
    return pairs


PAIRS = distinct_pairs()
SLOTS = {}
for _x_pair, _y_pair, _z_pairs in PAIRS:
    for _z_pair in _z_pairs:
        SLOTS[(_x_pair, _y_pair, _z_pair)] = len(SLOTS)
N_SLOTS = 192
ROWS = N_SLOTS // 2 * CH


def slot_place(slot):
    return slice(slot // 2 * CH, slot // 2 * CH + CH), slice(slot % 2 * CH, slot % 2 * CH + CH)


def block_slot(row, col):
    return SLOTS[
        tuple(
            pair_type(row // unit % 3, col // unit % 3) for unit in (9, 3, 1)
        )
    ]


DIAGONAL = {block_slot(index, index) for index in range(27)}


def row_peers(space, own):
    return [{"space": lax.rem(space + 2 * step, 16), "own": own} for step in range(1, 8)]


def meet(peers):
    barrier = pltpu.get_barrier_semaphore()
    for peer in peers:
        pl.semaphore_signal(barrier, inc=1, device_id=peer, device_id_type=MESH)
    pl.semaphore_wait(barrier, len(peers))


def inverse_columns(matrix, first, apart):
    size = matrix.shape[0]
    lane = lax.broadcasted_iota(jnp.int32, (size, 128), 1)
    sub = lax.broadcasted_iota(jnp.int32, (size, 128), 0)
    wanted = (lane >= size) & (lane < size + 8) & (sub == first + apart * (lane - size))
    work = jnp.where(lane < size, matrix, jnp.where(wanted, 1.0, 0.0))
    for step in range(size):
        pivot = work[step : step + 1, :] / work[step : step + 1, step : step + 1]
        work = jnp.where(sub == step, pivot, work - work[:, step : step + 1] * pivot)
    return [work[:, size + index : size + index + 1] for index in range(8)]


HALF = ROWS // 2
PART = HALF // 3
SLOTS_PER_PART = N_SLOTS // 3
SIZES = (PART // 4, PART // 16)


def front_part(
    inv_cells, base, cots, grad, factor, high, low, full, row_out,
    ext, left, right, terms, half, from_core, sums_1, sums_2, came_0, came_1, came_2, g_sum, g_came, products, shares,
    halo_send, halo_recv, core_send, core_recv, ring_send, ring_recv, back_send, back_recv,
    last_send, last_recv, g_send, g_recv, w_send, w_recv,
):
    space, own = lax.axis_index("space"), lax.axis_index("own")
    n_space, n_own = lax.axis_size("space"), lax.axis_size("own")
    core, ypos, z_lo = lax.rem(space, 2), lax.rem(space // 2, 4), space // 8
    xpos, z_hi = lax.rem(own, 4), own // 4
    coords = (xpos, ypos, z_hi * 2 + z_lo)
    planes, lines, chans, depth = base.shape
    lanes = grad.shape[1]

    def peer(axis, coord):
        if axis == 0:
            return {"space": space, "own": own - xpos + coord}
        if axis == 1:
            return {"space": space + 2 * (coord - ypos), "own": own}
        return {"space": space + 8 * (lax.rem(coord, 2) - z_lo), "own": coord // 2 * 4 + xpos}

    partner = {"space": space + 1 - 2 * core, "own": own}
    ring = {
        (axis, step): peer(axis, lax.rem(coords[axis] + step, 4)) for axis in range(3) for step in (1, 2, 3)
    }
    owners = [{"space": space, "own": lax.rem(own + step, n_own)} for step in range(1, n_own)]
    steps = [(dx, dy) for dx in (-1, 0, 1) for dy in (-1, 0, 1) if dx or dy]
    around = [
        {"space": lax.rem(space + dx + n_space, n_space), "own": lax.rem(own + dy + n_own, n_own)}
        for dx, dy in steps
    ]
    ext[1 : 1 + planes, 1 : 1 + lines] = base[...]
    products[...] = jnp.zeros_like(products)
    meet([partner] + list(ring.values()) + owners + around + row_peers(space, own))

    def rows(start, count):
        return pl.ds(pl.multiple_of(start, 8), count)

    waiting = []

    def send(src, dst, send_sem, recv_sem, device):
        copy = pltpu.make_async_remote_copy(
            src_ref=src, dst_ref=dst, send_sem=send_sem, recv_sem=recv_sem, device_id=device, device_id_type=MESH
        )
        copy.start()
        waiting.append(copy)
        return copy

    def ends(step, count):
        if step == 0:
            return pl.ds(1, count), pl.ds(1, count)
        return (pl.ds(count, 1), pl.ds(0, 1)) if step > 0 else (pl.ds(1, 1), pl.ds(count + 1, 1))

    halo = []
    for index, (dx, dy) in enumerate(steps):
        (from_x, to_x), (from_y, to_y) = ends(dx, planes), ends(dy, lines)
        halo.append(
            send(ext.at[from_x, from_y], ext.at[to_x, to_y], halo_send.at[index], halo_recv.at[index], around[index])
        )

    lane = lax.broadcasted_iota(jnp.int32, (chans, depth), 1)

    def shift_line(x, y):
        here = ext[x, y].astype(jnp.float32)
        before = jnp.where(lane == 0, 0.0, pltpu.roll(here, 1, 1))
        after = jnp.where(lane == depth - 1, 0.0, pltpu.roll(here, depth - 1, 1))
        stack = jnp.concatenate([before, here, after], axis=0)
        across = slice(y * depth, (y + 1) * depth)
        left[x, :, across] = stack.astype(left.dtype)
        right[x, across, :] = stack.T.astype(right.dtype)

    def shift_lines(x, ys):
        for y in ys:
            shift_line(x, y)

    def inner_plane(x, carry):
        shift_lines(x, range(1, lines + 1))
        return carry

    def edge_lines(x, carry):
        shift_lines(x, (0, lines + 1))
        return carry

    def outer_plane(index, carry):
        shift_lines(index * (planes + 1), range(lines + 2))
        return carry

    g_sum[0] = jnp.zeros_like(g_sum[0])
    g_sum[0, :, :chans] = lax.dot_general(
        cots[...], cots[...], (((1,), (1,)), ((), ())), preferred_element_type=jnp.float32
    )
    g_copies = [send(g_sum.at[0], g_came.at[0], g_send.at[0], g_recv.at[0], partner)]
    lax.fori_loop(1, planes + 1, inner_plane, 0)
    for copy in halo:
        copy.wait()
    del waiting[: len(halo)]

    @pl.when(space == 0)
    def _():
        ext[0] = jnp.zeros_like(ext[0])

    @pl.when(space == n_space - 1)
    def _():
        ext[planes + 1] = jnp.zeros_like(ext[0])

    @pl.when(own == 0)
    def _():
        ext[:, 0] = jnp.zeros_like(ext[:, 0])

    @pl.when(own == n_own - 1)
    def _():
        ext[:, lines + 1] = jnp.zeros_like(ext[:, 0])

    lax.fori_loop(1, planes + 1, edge_lines, 0)
    lax.fori_loop(0, 2, outer_plane, 0)

    levels = (half, sums_1, sums_2)
    came = (came_0, came_1)
    flights, back, to_core = {}, {}, {}

    def exchange(part):
        to_core[part] = send(
            terms.at[rows(part * 2 * PART + (1 - core) * PART, PART)],
            from_core.at[rows(part * PART, PART)],
            core_send.at[part], core_recv.at[part], partner,
        )

    def scatter(level, part):
        axis, count = (part + level) % 3, SIZES[level]
        for step in (1, 2, 3):
            target = lax.rem(coords[axis] + step, 4)
            slot = part * 3 + step - 1
            flights[(level, part, step)] = send(
                levels[level].at[rows(part * count * 4 + target * count, count)],
                came[level].at[rows(slot * count, count)],
                ring_send.at[level * 9 + slot], ring_recv.at[level * 9 + slot], ring[(axis, step)],
            )

    def merge(part):
        to_core[part].wait_recv()
        here = rows(part * PART, PART)
        half[here, :] = terms[rows(part * 2 * PART + core * PART, PART), :] + from_core[here, :]
        scatter(0, part)

    def collect(level, part):
        axis, count = (part + level) % 3, SIZES[level]
        total = levels[level][rows(part * count * 4 + coords[axis] * count, count), :]
        for step in (1, 2, 3):
            flights[(level, part, step)].wait_recv()
            total = total + came[level][rows((part * 3 + step - 1) * count, count), :]
        levels[level + 1][rows(part * count, count), :] = total
        if level == 0:
            scatter(1, part)
        else:
            swap(part)

    def swap(part):
        axis, count = (part + 2) % 3, SIZES[1]
        mine = rows((part * 4 + coords[axis]) * count, count)
        for step in (1, 2, 3):
            slot = 18 + part * 3 + step - 1
            flights[(2, part, step)] = send(
                sums_2.at[rows(part * count, count)], came_2.at[mine], ring_send.at[slot], ring_recv.at[slot],
                ring[(axis, step)],
            )
        came_2[mine, :] = sums_2[rows(part * count, count), :]

    def settle(part):
        count = SIZES[1]
        for step in (1, 2, 3):
            flights[(2, part, step)].wait_recv()
        total = came_2[rows(part * 4 * count, count), :]
        for coord in (1, 2, 3):
            total = total + came_2[rows((part * 4 + coord) * count, count), :]
        full[rows(start(2, part), count), :] = total
        spread(1, part)

    def send_g(stage, source, devices):
        return [
            send(source, g_came.at[stage + index], g_send.at[stage + index], g_recv.at[stage + index], device)
            for index, device in enumerate(devices)
        ]

    def add_g(stage, value, copies, target):
        for index, copy in enumerate(copies):
            copy.wait_recv()
            value = value + g_came[stage + index]
        g_sum[target] = value

    run = lines * depth
    done = 0
    started = 0
    for x_pair, y_pair, z_pairs in PAIRS:
        total = None
        for x in range(planes):
            term = jnp.dot(
                left[x + x_pair[0], :, y_pair[0] * depth : y_pair[0] * depth + run],
                right[x + x_pair[1], y_pair[1] * depth : y_pair[1] * depth + run, :],
                preferred_element_type=jnp.float32,
            )
            total = term if total is None else total + term
        for z_pair in z_pairs:
            block = total[z_pair[0] * chans : (z_pair[0] + 1) * chans, z_pair[1] * chans : (z_pair[1] + 1) * chans]
            terms[slot_place(SLOTS[(x_pair, y_pair, z_pair)])] = block
            done += 1
        if done >= (started + 1) * SLOTS_PER_PART:
            exchange(started)
            if started:
                merge(started - 1)
            started += 1
    for slot in range(done, N_SLOTS):
        terms[slot_place(slot)] = jnp.zeros((chans, chans), jnp.float32)
    exchange(2)
    merge(1)
    merge(2)
    add_g(0, g_sum[0], g_copies, 1)
    g_copies = send_g(1, g_sum.at[1], [ring[(0, step)] for step in (1, 2, 3)])
    collect(0, 0)
    collect(0, 1)
    collect(0, 2)
    add_g(1, g_sum[1], g_copies, 2)
    g_copies = send_g(4, g_sum.at[2], [ring[(1, step)] for step in (1, 2, 3)])
    collect(1, 0)
    collect(1, 1)
    collect(1, 2)
    add_g(4, g_sum[2], g_copies, 3)
    g_copies = send_g(7, g_sum.at[3], [ring[(2, step)] for step in (1, 2, 3)])

    def start(level, part):
        first = part * 2 * PART + core * PART
        for outer in range(level):
            first = first + coords[(part + outer) % 3] * SIZES[outer]
        return first

    def forward(part, index, coord):
        here = rows(start(0, part) + coord * SIZES[0], SIZES[0])
        slot = part * 4 + index
        back[(part, index)] = send(full.at[here], full.at[here], last_send.at[slot], last_recv.at[slot], partner)

    def spread(level, part):
        axis, count = (part + level) % 3, SIZES[level]
        here = rows(start(level, part) + coords[axis] * count, count)
        for step in (1, 2, 3):
            slot = level * 9 + part * 3 + step - 1
            back[(level, part, step)] = send(
                full.at[here], full.at[here], back_send.at[slot], back_recv.at[slot], ring[(axis, step)]
            )
        if level == 0:
            forward(part, 0, coords[axis])

    def gathered(level, part):
        axis = (part + level) % 3
        for step in (1, 2, 3):
            back[(level, part, step)].wait_recv()
            if level == 0:
                forward(part, step, lax.rem(coords[axis] + 4 - step, 4))
        if level:
            spread(level - 1, part)

    for part in range(3):
        settle(part)
    add_g(7, g_sum[3], g_copies, 4)
    diagonal = lax.broadcasted_iota(jnp.int32, (CH, 2 * CH), 0) == lax.broadcasted_iota(jnp.int32, (CH, 2 * CH), 1)
    g_factor = g_sum[4] * inv_cells + jnp.where(diagonal, damping, 0.0)
    for owner, weights in enumerate(inverse_columns(g_factor, space // 2, 8)):
        products[owner, :1, :lanes] = jnp.sum(grad[...] * weights, axis=0, keepdims=True)
    to_owners = [
        send(products.at[owner["own"]], shares.at[own], w_send.at[index], w_recv.at[index], owner)
        for index, owner in enumerate(owners)
    ]
    shares[own] = products[own]
    for part in range(3):
        gathered(1, part)
    for part in range(3):
        gathered(0, part)
    eye = jnp.where(
        lax.broadcasted_iota(jnp.int32, (CH, CH), 0) == lax.broadcasted_iota(jnp.int32, (CH, CH), 1), damping, 0.0
    )
    clear_margin(factor, high, low)
    squares = jnp.zeros((CH, CH), jnp.float32)
    for part in range(3):
        for index in range(4):
            back[(part, index)].wait_recv()
        squares = squares + assemble(part, full, inv_cells, eye, factor, high, low)
    mirror(factor, high, low)
    for copy in to_owners:
        copy.wait_recv()
    row_out[...] = jnp.zeros_like(row_out)
    for owner in range(n_own):
        row_out[:, owner * lanes : (owner + 1) * lanes] = shares[owner, :1, :lanes]
    for copy in waiting:
        copy.wait_send()
    return 1.0 / jnp.sqrt(jnp.sum(squares, keepdims=True))


def times_factor(factor, row):
    size = factor.shape[0]
    parts = []
    for base in range(0, size, 128):
        rows = factor[pl.ds(base, 128), :].reshape(16, 8, size)
        total = jnp.zeros((16, 8, 128), jnp.float32)
        for lane in range(0, size, 128):
            total = total + rows[:, :, lane : lane + 128] * row[None, :, lane : lane + 128]
        flipped = total.reshape(128, 128).T
        parts.append(jnp.broadcast_to(jnp.sum(flipped, axis=0, keepdims=True), (8, 128)))
    return jnp.concatenate(parts, axis=1)


def halves(value):
    high = value.astype(jnp.bfloat16)
    return high, (value - high.astype(jnp.float32)).astype(jnp.bfloat16)


def put(rows, cols, value, factor, high, low):
    factor[rows, cols] = value
    high[rows, cols], low[rows, cols] = halves(value)


def clear_margin(*refs):
    size, width = refs[0].shape[0], 27 * CH
    for ref in refs:
        ref[width:, :] = jnp.zeros((size - width, size), ref.dtype)
        ref[:, width:] = jnp.zeros((size, size - width), ref.dtype)


def assemble(part, full, inv_cells, eye, *refs):
    places = {}
    for row in range(27):
        for col in range(row, 27):
            slot = block_slot(row, col)
            if slot // SLOTS_PER_PART == part:
                places.setdefault(slot, []).append((row, col))
    squares = jnp.zeros((CH, CH), jnp.float32)
    for slot, pairs in places.items():
        block = full[slot_place(slot)] * inv_cells
        if slot in DIAGONAL:
            block = block + eye
        squares = squares + float(sum(1 if row == col else 2 for row, col in pairs)) * (block * block)
        for row, col in pairs:
            rows, cols = slice(row * CH, (row + 1) * CH), slice(col * CH, (col + 1) * CH)
            put(rows, cols, block, *refs)
            if row != col and row * CH // TILE == col * CH // TILE:
                put(cols, rows, block.T, *refs)
    return squares


def mirror(factor, *refs):
    tiles = factor.shape[0] // TILE
    for row in range(tiles):
        for col in range(row + 1, tiles):
            rows, cols = slice(row * TILE, (row + 1) * TILE), slice(col * TILE, (col + 1) * TILE)
            put(cols, rows, factor[rows, cols].T, factor, *refs)


def poly_part(
    inverse, row_ref, out, factor, high_a, low_a, high_b, low_b, pieces, came,
    tile_send, tile_recv, ready, share_send, share_recv,
):
    space, own = lax.axis_index("space"), lax.axis_index("own")
    core, chip = lax.rem(space, 2), space // 2
    partner = {"space": space + 1 - 2 * core, "own": own}
    peers = row_peers(space, own)
    size = factor.shape[0]
    tiles = size // TILE
    row = jnp.broadcast_to(row_ref[...], (8, size)) * inverse
    dot = functools.partial(jnp.dot, preferred_element_type=jnp.float32)
    operands = ((high_a, low_a), (high_b, low_b))

    def place(i, half, which):
        j = lax.rem(i + 2 * half + which, tiles)
        return (
            pl.ds(pl.multiple_of(i * TILE, TILE), TILE),
            pl.ds(pl.multiple_of(j * TILE, TILE), TILE),
        )

    def tile_copy(i, which):
        here = factor.at[place(i, core, which)]
        return pltpu.make_async_remote_copy(
            src_ref=here,
            dst_ref=here,
            send_sem=tile_send.at[2 * i + which],
            recv_sem=tile_recv.at[2 * i + which],
            device_id=partner,
            device_id_type=MESH,
        )

    for step in range(SQUARINGS):
        (high, low), (next_high, next_low) = operands[step % 2], operands[1 - step % 2]
        applied = times_factor(factor, row)
        row = 2.0 * row - (applied if step else applied * inverse)
        pl.semaphore_signal(ready, inc=1, device_id=partner, device_id_type=MESH)

        def finish(i, half, which, fresh, step=step, next_high=next_high, next_low=next_low):
            rows, cols = place(i, half, which)
            flipped = fresh.T
            if which == 0:
                flipped = jnp.where(half == 0, fresh, flipped)
            factor[cols, rows] = flipped
            if step < SQUARINGS - 1:
                next_high[rows, cols], next_low[rows, cols] = halves(fresh)
                next_high[cols, rows], next_low[cols, rows] = halves(flipped)

        def compute(i, step=step, high=high, low=low, finish=finish):
            for which in range(2):
                rows, cols = place(i, core, which)
                square = dot(high[rows, :], high[:, cols])
                if step:
                    square = square + (dot(high[rows, :], low[:, cols]) + dot(low[rows, :], high[:, cols]))
                if step:
                    fresh = 2.0 * factor[rows, cols] - square
                else:
                    fresh = (2.0 * inverse) * factor[rows, cols] - (inverse * inverse) * square
                factor[rows, cols] = fresh
                finish(i, core, which, fresh)

        def adopt(i, finish=finish):
            for which in range(2):
                finish(i, 1 - core, which, factor[place(i, 1 - core, which)])

        def send_tiles(i):
            for which in range(2):
                tile_copy(i, which).start()

        def first_tiles(i, carry, compute=compute):
            compute(i)

            @pl.when(i == 0)
            def _():
                pl.semaphore_wait(ready, 1)

            send_tiles(i)
            return carry

        def next_tiles(i, carry, compute=compute, adopt=adopt):
            for which in range(2):
                tile_copy(i - LAG, which).wait_recv()
            adopt(i - LAG)
            compute(i)
            send_tiles(i)
            return carry

        def last_tiles(i, carry, adopt=adopt):
            for which in range(2):
                tile_copy(i, which).wait_recv()
            adopt(i)
            return carry

        lax.fori_loop(0, LAG, first_tiles, 0)
        lax.fori_loop(LAG, tiles, next_tiles, 0)
        lax.fori_loop(tiles - LAG, tiles, last_tiles, 0)
        for index in range(2 * tiles):
            tile_copy(index // 2, index % 2).wait_send()

    def horner(index, value):
        return row + (value - times_factor(factor, value))

    value = lax.fori_loop(0, 2 ** (8 - SQUARINGS) - 1, horner, row)

    lanes = out.shape[1]
    for index in range(16):
        pieces[index, :, :lanes] = value[:, index * lanes : (index + 1) * lanes]
        pieces[index, :, lanes:] = jnp.zeros((8, 128 - lanes), jnp.float32)
    copies = []
    for index, peer in enumerate(peers):
        copy = pltpu.make_async_remote_copy(
            src_ref=pieces.at[peer["space"]],
            dst_ref=came.at[chip],
            send_sem=share_send.at[index],
            recv_sem=share_recv.at[index],
            device_id=peer,
            device_id_type=MESH,
        )
        copy.start()
        copies.append(copy)
    came[chip] = pieces[space]
    for copy in copies:
        copy.wait()
    for index in range(8):
        out[index : index + 1, :] = came[index, :1, :lanes]


N_FRONT = 31


def whole_kernel(inv_cells, base, cots, grad, out, factor, high_a, low_a, high_b, low_b, *refs):
    shared, rest = refs[:N_FRONT], refs[N_FRONT:]
    inverse = front_part(inv_cells, base, cots, grad, factor, high_a, low_a, *shared)
    poly_part(inverse, shared[1], out, factor, high_a, low_a, high_b, low_b, *rest)


def whole(base, cots, grad, inv_cells, size):
    planes, lines, chans, depth = base.shape
    vmem = pl.BlockSpec(memory_space=pltpu.VMEM)
    lanes = 2 * CH
    tiles = size // TILE
    dma = pltpu.SemaphoreType.DMA
    counts = [HALF, HALF, 3 * SIZES[0], 3 * SIZES[1], 9 * SIZES[0], 9 * SIZES[1], 12 * SIZES[1]]
    front_refs = (
        [
            pltpu.VMEM((ROWS, lanes), jnp.float32),
            pltpu.VMEM((1, size), jnp.float32),
            pltpu.VMEM((planes + 2, lines + 2, chans, depth), jnp.bfloat16),
            pltpu.VMEM((planes + 2, 3 * chans, (lines + 2) * depth), jnp.bfloat16),
            pltpu.VMEM((planes + 2, (lines + 2) * depth, 3 * chans), jnp.bfloat16),
            pltpu.VMEM((ROWS, lanes), jnp.float32),
        ]
        + [pltpu.VMEM((count, lanes), jnp.float32) for count in counts]
        + [pltpu.VMEM((count, CH, lanes), jnp.float32) for count in (5, 10)]
        + [pltpu.VMEM((8, 8, -(-grad.shape[1] // lanes) * lanes), jnp.float32)] * 2
        + [dma((count,)) for count in (8, 8, 3, 3, 27, 27, 18, 18, 12, 12, 10, 10, 7, 7)]
    )
    return pl.pallas_call(
        functools.partial(whole_kernel, inv_cells),
        out_shape=jax.ShapeDtypeStruct((8, grad.shape[1] // 2), jnp.float32),
        in_specs=[vmem] * 3,
        out_specs=vmem,
        scratch_shapes=[pltpu.VMEM((size, size), jnp.float32)]
        + [pltpu.VMEM((size, size), jnp.bfloat16)] * 4
        + front_refs
        + [pltpu.VMEM((16, 8, 128), jnp.float32), pltpu.VMEM((8, 8, 128), jnp.float32)]
        + [dma((2 * tiles,)), dma((2 * tiles,)), pltpu.SemaphoreType.REGULAR, dma((7,)), dma((7,))],
        compiler_params=pltpu.CompilerParams(
            collective_id=1, has_side_effects=True, vmem_limit_bytes=60 * 2**20
        ),
    )(base, cots, grad)


def body(acts, cotangents, weight_grad):
    chans, block_x, block_y, depth_z = acts.shape
    c_out = cotangents.shape[0]
    width = 27 * chans
    n_space = lax.axis_size("space")
    n_own = lax.axis_size("own")
    inv_cells = 1.0 / (block_x * n_space * block_y * n_own * depth_z)
    size = -(-width // TILE) * TILE
    base = jnp.transpose(acts, (1, 2, 0, 3))
    return whole(base, cotangents.reshape(c_out, -1), weight_grad, inv_cells, size)


def solution(mesh):
    in_specs = (P(None, "space", "own", None), P(None, "space", "own", None), P(None, "own"))
    out_specs = P("own", "space")
    return jax.shard_map(body, mesh=mesh, in_specs=in_specs, out_specs=out_specs, check_vma=False)
```

```python
import functools

import jax
import jax.numpy as jnp
from jax import lax
from jax.experimental import pallas as pl
from jax.experimental.pallas import tpu as pltpu
from jax.sharding import PartitionSpec as P

SQUARINGS = 4
TILE = 256
EIGHT = jnp.float8_e4m3fn
COARSE = 2.0**8
FINE = 2.0**17
LAG = 3
CH = 64
NZ = 256
damping = 0.05
MESH = pl.DeviceIdType.MESH
SAME = ((0, 0), (1, 1), (2, 2))
UP = ((0, 1), (0, 2))
DOWN = ((1, 0), (2, 0))


def pair_type(first, second):
    if first == second:
        return (first, second)
    apart = second - first
    return (0, apart) if apart > 0 else (-apart, 0)


def distinct_pairs():
    pairs = []
    for x_pair in SAME + UP:
        for y_pair in SAME + UP + (DOWN if x_pair in UP else ()):
            full = x_pair in UP or y_pair in UP
            pairs.append((x_pair, y_pair, SAME + UP + (DOWN if full else ())))
    return pairs


PAIRS = distinct_pairs()
SLOTS = {}
for _x_pair, _y_pair, _z_pairs in PAIRS:
    for _z_pair in _z_pairs:
        SLOTS[(_x_pair, _y_pair, _z_pair)] = len(SLOTS)
N_SLOTS = 192
ROWS = N_SLOTS // 2 * CH


def slot_place(slot):
    return slice(slot // 2 * CH, slot // 2 * CH + CH), slice(slot % 2 * CH, slot % 2 * CH + CH)


def block_slot(row, col):
    return SLOTS[
        tuple(
            pair_type(row // unit % 3, col // unit % 3) for unit in (9, 3, 1)
        )
    ]


DIAGONAL = {block_slot(index, index) for index in range(27)}


def row_peers(space, own):
    return [{"space": lax.rem(space + 2 * step, 16), "own": own} for step in range(1, 8)]


def meet(peers):
    barrier = pltpu.get_barrier_semaphore()
    for peer in peers:
        pl.semaphore_signal(barrier, inc=1, device_id=peer, device_id_type=MESH)
    pl.semaphore_wait(barrier, len(peers))


def inverse_columns(matrix, first, apart):
    size = matrix.shape[0]
    lane = lax.broadcasted_iota(jnp.int32, (size, 128), 1)
    sub = lax.broadcasted_iota(jnp.int32, (size, 128), 0)
    wanted = (lane >= size) & (lane < size + 8) & (sub == first + apart * (lane - size))
    work = jnp.where(lane < size, matrix, jnp.where(wanted, 1.0, 0.0))
    for step in range(size):
        pivot = work[step : step + 1, :] / work[step : step + 1, step : step + 1]
        work = jnp.where(sub == step, pivot, work - work[:, step : step + 1] * pivot)
    return [work[:, size + index : size + index + 1] for index in range(8)]


HALF = ROWS // 2
PART = HALF // 3
SLOTS_PER_PART = N_SLOTS // 3
SIZES = (PART // 4, PART // 16)


def front_part(
    inv_cells, base, cots, grad, factor, high, full, row_out,
    ext, left, right, terms, half, from_core, sums_1, sums_2, came_0, came_1, came_2, g_sum, g_came, products, shares,
    halo_send, halo_recv, core_send, core_recv, ring_send, ring_recv, back_send, back_recv,
    last_send, last_recv, g_send, g_recv, w_send, w_recv,
):
    space, own = lax.axis_index("space"), lax.axis_index("own")
    n_space, n_own = lax.axis_size("space"), lax.axis_size("own")
    core, ypos, z_lo = lax.rem(space, 2), lax.rem(space // 2, 4), space // 8
    xpos, z_hi = lax.rem(own, 4), own // 4
    coords = (xpos, ypos, z_hi * 2 + z_lo)
    planes, lines, chans, depth = base.shape
    lanes = grad.shape[1]

    def peer(axis, coord):
        if axis == 0:
            return {"space": space, "own": own - xpos + coord}
        if axis == 1:
            return {"space": space + 2 * (coord - ypos), "own": own}
        return {"space": space + 8 * (lax.rem(coord, 2) - z_lo), "own": coord // 2 * 4 + xpos}

    partner = {"space": space + 1 - 2 * core, "own": own}
    ring = {
        (axis, step): peer(axis, lax.rem(coords[axis] + step, 4)) for axis in range(3) for step in (1, 2, 3)
    }
    owners = [{"space": space, "own": lax.rem(own + step, n_own)} for step in range(1, n_own)]
    steps = [(dx, dy) for dx in (-1, 0, 1) for dy in (-1, 0, 1) if dx or dy]
    around = [
        {"space": lax.rem(space + dx + n_space, n_space), "own": lax.rem(own + dy + n_own, n_own)}
        for dx, dy in steps
    ]
    ext[1 : 1 + planes, 1 : 1 + lines] = base[...]
    products[...] = jnp.zeros_like(products)
    meet([partner] + list(ring.values()) + owners + around + row_peers(space, own))

    def rows(start, count):
        return pl.ds(pl.multiple_of(start, 8), count)

    waiting = []

    def send(src, dst, send_sem, recv_sem, device):
        copy = pltpu.make_async_remote_copy(
            src_ref=src, dst_ref=dst, send_sem=send_sem, recv_sem=recv_sem, device_id=device, device_id_type=MESH
        )
        copy.start()
        waiting.append(copy)
        return copy

    def ends(step, count):
        if step == 0:
            return pl.ds(1, count), pl.ds(1, count)
        return (pl.ds(count, 1), pl.ds(0, 1)) if step > 0 else (pl.ds(1, 1), pl.ds(count + 1, 1))

    halo = []
    for index, (dx, dy) in enumerate(steps):
        (from_x, to_x), (from_y, to_y) = ends(dx, planes), ends(dy, lines)
        halo.append(
            send(ext.at[from_x, from_y], ext.at[to_x, to_y], halo_send.at[index], halo_recv.at[index], around[index])
        )

    lane = lax.broadcasted_iota(jnp.int32, (chans, depth), 1)

    def shift_line(x, y):
        here = ext[x, y].astype(jnp.float32)
        before = jnp.where(lane == 0, 0.0, pltpu.roll(here, 1, 1))
        after = jnp.where(lane == depth - 1, 0.0, pltpu.roll(here, depth - 1, 1))
        stack = jnp.concatenate([before, here, after], axis=0)
        across = slice(y * depth, (y + 1) * depth)
        left[x, :, across] = stack.astype(left.dtype)
        right[x, across, :] = stack.T.astype(right.dtype)

    def shift_lines(x, ys):
        for y in ys:
            shift_line(x, y)

    def inner_plane(x, carry):
        shift_lines(x, range(1, lines + 1))
        return carry

    def edge_lines(x, carry):
        shift_lines(x, (0, lines + 1))
        return carry

    def outer_plane(index, carry):
        shift_lines(index * (planes + 1), range(lines + 2))
        return carry

    g_sum[0] = jnp.zeros_like(g_sum[0])
    g_sum[0, :, :chans] = lax.dot_general(
        cots[...], cots[...], (((1,), (1,)), ((), ())), preferred_element_type=jnp.float32
    )
    g_copies = [send(g_sum.at[0], g_came.at[0], g_send.at[0], g_recv.at[0], partner)]
    lax.fori_loop(1, planes + 1, inner_plane, 0)
    for copy in halo:
        copy.wait()
    del waiting[: len(halo)]

    @pl.when(space == 0)
    def _():
        ext[0] = jnp.zeros_like(ext[0])

    @pl.when(space == n_space - 1)
    def _():
        ext[planes + 1] = jnp.zeros_like(ext[0])

    @pl.when(own == 0)
    def _():
        ext[:, 0] = jnp.zeros_like(ext[:, 0])

    @pl.when(own == n_own - 1)
    def _():
        ext[:, lines + 1] = jnp.zeros_like(ext[:, 0])

    lax.fori_loop(1, planes + 1, edge_lines, 0)
    lax.fori_loop(0, 2, outer_plane, 0)

    levels = (half, sums_1, sums_2)
    came = (came_0, came_1)
    flights, back, to_core = {}, {}, {}

    def exchange(part):
        to_core[part] = send(
            terms.at[rows(part * 2 * PART + (1 - core) * PART, PART)],
            from_core.at[rows(part * PART, PART)],
            core_send.at[part], core_recv.at[part], partner,
        )

    def scatter(level, part):
        axis, count = (part + level) % 3, SIZES[level]
        for step in (1, 2, 3):
            target = lax.rem(coords[axis] + step, 4)
            slot = part * 3 + step - 1
            flights[(level, part, step)] = send(
                levels[level].at[rows(part * count * 4 + target * count, count)],
                came[level].at[rows(slot * count, count)],
                ring_send.at[level * 9 + slot], ring_recv.at[level * 9 + slot], ring[(axis, step)],
            )

    def merge(part):
        to_core[part].wait_recv()
        here = rows(part * PART, PART)
        half[here, :] = terms[rows(part * 2 * PART + core * PART, PART), :] + from_core[here, :]
        scatter(0, part)

    def collect(level, part):
        axis, count = (part + level) % 3, SIZES[level]
        total = levels[level][rows(part * count * 4 + coords[axis] * count, count), :]
        for step in (1, 2, 3):
            flights[(level, part, step)].wait_recv()
            total = total + came[level][rows((part * 3 + step - 1) * count, count), :]
        levels[level + 1][rows(part * count, count), :] = total
        if level == 0:
            scatter(1, part)
        else:
            swap(part)

    def swap(part):
        axis, count = (part + 2) % 3, SIZES[1]
        mine = rows((part * 4 + coords[axis]) * count, count)
        for step in (1, 2, 3):
            slot = 18 + part * 3 + step - 1
            flights[(2, part, step)] = send(
                sums_2.at[rows(part * count, count)], came_2.at[mine], ring_send.at[slot], ring_recv.at[slot],
                ring[(axis, step)],
            )
        came_2[mine, :] = sums_2[rows(part * count, count), :]

    def settle(part):
        count = SIZES[1]
        for step in (1, 2, 3):
            flights[(2, part, step)].wait_recv()
        total = came_2[rows(part * 4 * count, count), :]
        for coord in (1, 2, 3):
            total = total + came_2[rows((part * 4 + coord) * count, count), :]
        full[rows(start(2, part), count), :] = total
        spread(1, part)

    def send_g(stage, source, devices):
        return [
            send(source, g_came.at[stage + index], g_send.at[stage + index], g_recv.at[stage + index], device)
            for index, device in enumerate(devices)
        ]

    def add_g(stage, value, copies, target):
        for index, copy in enumerate(copies):
            copy.wait_recv()
            value = value + g_came[stage + index]
        g_sum[target] = value

    run = lines * depth
    done = 0
    started = 0
    for x_pair, y_pair, z_pairs in PAIRS:
        total = None
        for x in range(planes):
            term = jnp.dot(
                left[x + x_pair[0], :, y_pair[0] * depth : y_pair[0] * depth + run],
                right[x + x_pair[1], y_pair[1] * depth : y_pair[1] * depth + run, :],
                preferred_element_type=jnp.float32,
            )
            total = term if total is None else total + term
        for z_pair in z_pairs:
            block = total[z_pair[0] * chans : (z_pair[0] + 1) * chans, z_pair[1] * chans : (z_pair[1] + 1) * chans]
            terms[slot_place(SLOTS[(x_pair, y_pair, z_pair)])] = block
            done += 1
        if done >= (started + 1) * SLOTS_PER_PART:
            exchange(started)
            if started:
                merge(started - 1)
            started += 1
    for slot in range(done, N_SLOTS):
        terms[slot_place(slot)] = jnp.zeros((chans, chans), jnp.float32)
    exchange(2)
    merge(1)
    merge(2)
    add_g(0, g_sum[0], g_copies, 1)
    g_copies = send_g(1, g_sum.at[1], [ring[(0, step)] for step in (1, 2, 3)])
    collect(0, 0)
    collect(0, 1)
    collect(0, 2)
    add_g(1, g_sum[1], g_copies, 2)
    g_copies = send_g(4, g_sum.at[2], [ring[(1, step)] for step in (1, 2, 3)])
    collect(1, 0)
    collect(1, 1)
    collect(1, 2)
    add_g(4, g_sum[2], g_copies, 3)
    g_copies = send_g(7, g_sum.at[3], [ring[(2, step)] for step in (1, 2, 3)])

    def start(level, part):
        first = part * 2 * PART + core * PART
        for outer in range(level):
            first = first + coords[(part + outer) % 3] * SIZES[outer]
        return first

    def forward(part, index, coord):
        here = rows(start(0, part) + coord * SIZES[0], SIZES[0])
        slot = part * 4 + index
        back[(part, index)] = send(full.at[here], full.at[here], last_send.at[slot], last_recv.at[slot], partner)

    def spread(level, part):
        axis, count = (part + level) % 3, SIZES[level]
        here = rows(start(level, part) + coords[axis] * count, count)
        for step in (1, 2, 3):
            slot = level * 9 + part * 3 + step - 1
            back[(level, part, step)] = send(
                full.at[here], full.at[here], back_send.at[slot], back_recv.at[slot], ring[(axis, step)]
            )
        if level == 0:
            forward(part, 0, coords[axis])

    def gathered(level, part):
        axis = (part + level) % 3
        for step in (1, 2, 3):
            back[(level, part, step)].wait_recv()
            if level == 0:
                forward(part, step, lax.rem(coords[axis] + 4 - step, 4))
        if level:
            spread(level - 1, part)

    for part in range(3):
        settle(part)
    add_g(7, g_sum[3], g_copies, 4)
    diagonal = lax.broadcasted_iota(jnp.int32, (CH, 2 * CH), 0) == lax.broadcasted_iota(jnp.int32, (CH, 2 * CH), 1)
    g_factor = g_sum[4] * inv_cells + jnp.where(diagonal, damping, 0.0)
    for owner, weights in enumerate(inverse_columns(g_factor, space // 2, 8)):
        products[owner, :1, :lanes] = jnp.sum(grad[...] * weights, axis=0, keepdims=True)
    to_owners = [
        send(products.at[owner["own"]], shares.at[own], w_send.at[index], w_recv.at[index], owner)
        for index, owner in enumerate(owners)
    ]
    shares[own] = products[own]
    for part in range(3):
        gathered(1, part)
    for part in range(3):
        gathered(0, part)
    eye = jnp.where(
        lax.broadcasted_iota(jnp.int32, (CH, CH), 0) == lax.broadcasted_iota(jnp.int32, (CH, CH), 1), damping, 0.0
    )
    clear_margin(factor, high)
    squares = jnp.zeros((CH, CH), jnp.float32)
    for part in range(3):
        for index in range(4):
            back[(part, index)].wait_recv()
        squares = squares + assemble(part, full, inv_cells, eye, factor, high)
    mirror(factor, high)
    for copy in to_owners:
        copy.wait_recv()
    row_out[...] = jnp.zeros_like(row_out)
    for owner in range(n_own):
        row_out[:, owner * lanes : (owner + 1) * lanes] = shares[owner, :1, :lanes]
    for copy in waiting:
        copy.wait_send()
    return 1.0 / jnp.sqrt(jnp.sum(squares, keepdims=True))


def times_block(rows, row):
    size = rows.shape[1]
    rows = rows.reshape(16, 8, size)
    total = jnp.zeros((16, 8, 128), jnp.float32)
    for lane in range(0, size, 128):
        total = total + rows[:, :, lane : lane + 128] * row[None, :, lane : lane + 128]
    flipped = total.reshape(128, 128).T
    return jnp.broadcast_to(jnp.sum(flipped, axis=0, keepdims=True), (8, 128))


def times_factor(factor, row):
    size = factor.shape[0]
    return jnp.concatenate([times_block(factor[pl.ds(base, 128), :], row) for base in range(0, size, 128)], axis=1)


def store_split(here, value, high, coarse, fine):
    top = value.astype(high.dtype)
    high[here] = top
    top = top.astype(jnp.float32)
    coarse[here] = (top * COARSE).astype(coarse.dtype)
    fine[here] = ((value - top) * FINE).astype(fine.dtype)


def put(rows, cols, value, factor, high):
    factor[rows, cols] = value
    high[rows, cols] = value.astype(high.dtype)


def clear_margin(*refs):
    size, width = refs[0].shape[0], 27 * CH
    for ref in refs:
        ref[width:, :] = jnp.zeros((size - width, size), ref.dtype)
        ref[:, width:] = jnp.zeros((size, size - width), ref.dtype)


def assemble(part, full, inv_cells, eye, *refs):
    places = {}
    for row in range(27):
        for col in range(row, 27):
            slot = block_slot(row, col)
            if slot // SLOTS_PER_PART == part:
                places.setdefault(slot, []).append((row, col))
    squares = jnp.zeros((CH, CH), jnp.float32)
    for slot, pairs in places.items():
        block = full[slot_place(slot)] * inv_cells
        if slot in DIAGONAL:
            block = block + eye
        squares = squares + float(sum(1 if row == col else 2 for row, col in pairs)) * (block * block)
        for row, col in pairs:
            rows, cols = slice(row * CH, (row + 1) * CH), slice(col * CH, (col + 1) * CH)
            put(rows, cols, block, *refs)
            if row != col and row * CH // TILE == col * CH // TILE:
                put(cols, rows, block.T, *refs)
    return squares


def mirror(factor, *refs):
    tiles = factor.shape[0] // TILE
    for row in range(tiles):
        for col in range(row + 1, tiles):
            rows, cols = slice(row * TILE, (row + 1) * TILE), slice(col * TILE, (col + 1) * TILE)
            put(cols, rows, factor[rows, cols].T, factor, *refs)


def poly_part(
    inverse, row_ref, out, factor, high_a, high_b, coarse_a, fine_a, coarse_b, fine_b, pieces, came,
    tile_send, tile_recv, ready, share_send, share_recv,
):
    space, own = lax.axis_index("space"), lax.axis_index("own")
    core, chip = lax.rem(space, 2), space // 2
    partner = {"space": space + 1 - 2 * core, "own": own}
    peers = row_peers(space, own)
    size = factor.shape[0]
    tiles = size // TILE
    row = jnp.broadcast_to(row_ref[...], (8, size)) * inverse
    dot = functools.partial(jnp.dot, preferred_element_type=jnp.float32)
    operands = ((high_a, coarse_a, fine_a), (high_b, coarse_b, fine_b))

    def place(i, half, which):
        first = lax.rem(i + tiles - 1, tiles)
        j = lax.rem(first + 2 * half + 1, tiles)
        return (
            pl.ds(pl.multiple_of(lax.rem(first + which, tiles) * TILE, TILE), TILE),
            pl.ds(pl.multiple_of(j * TILE, TILE), TILE),
        )

    def tile_copy(i, which):
        here = factor.at[place(i, core, which)]
        return pltpu.make_async_remote_copy(
            src_ref=here,
            dst_ref=here,
            send_sem=tile_send.at[2 * i + which],
            recv_sem=tile_recv.at[2 * i + which],
            device_id=partner,
            device_id_type=MESH,
        )

    for step in range(SQUARINGS):
        now, later = operands[step % 2], operands[1 - step % 2]
        applied = times_factor(factor, row)
        row = 2.0 * row - (applied if step else applied * inverse)
        pl.semaphore_signal(ready, inc=1, device_id=partner, device_id_type=MESH)

        def finish(i, half, which, fresh, step=step, later=later):
            rows, cols = place(i, half, which)
            flipped = fresh.T
            if which == 1:
                flipped = jnp.where(half == 0, fresh, flipped)
            factor[cols, rows] = flipped
            if step < SQUARINGS - 1:
                store_split((rows, cols), fresh, *later)
                store_split((cols, rows), flipped, *later)

        def product(rows, cols, step=step, now=now):
            high, coarse, fine = now
            square = dot(high[rows, :], high[:, cols])
            if step:
                cross = dot(coarse[rows, :], fine[:, cols]) + dot(fine[rows, :], coarse[:, cols])
                square = square + cross * (1.0 / (COARSE * FINE))
            return square

        def renew(i, which, square, step=step, finish=finish):
            here = place(i, core, which)
            if step:
                fresh = 2.0 * factor[here] - square
            else:
                fresh = (2.0 * inverse) * factor[here] - (inverse * inverse) * square
            factor[here] = fresh
            finish(i, core, which, fresh)

        def compute(i, product=product, renew=renew):
            cols = place(i, core, 0)[1]
            square = product(pl.ds(pl.multiple_of((i - 1) * TILE, TILE), 2 * TILE), cols)
            renew(i, 0, square[:TILE])
            renew(i, 1, square[TILE:])

        def adopt(i, finish=finish):
            for which in range(2):
                finish(i, 1 - core, which, factor[place(i, 1 - core, which)])

        def send_tiles(i):
            for which in range(2):
                tile_copy(i, which).start()

        def first_tiles(i, carry, compute=compute):
            compute(i)
            send_tiles(i)
            return carry

        def next_tiles(i, carry, compute=compute, adopt=adopt):
            for which in range(2):
                tile_copy(i - LAG, which).wait_recv()
            adopt(i - LAG)
            compute(i)
            send_tiles(i)
            return carry

        def last_tiles(i, carry, adopt=adopt):
            for which in range(2):
                tile_copy(i, which).wait_recv()
            adopt(i)
            return carry

        for which in range(2):
            renew(0, which, product(*place(0, core, which)))
        pl.semaphore_wait(ready, 1)
        send_tiles(0)
        lax.fori_loop(1, LAG, first_tiles, 0)
        lax.fori_loop(LAG, tiles, next_tiles, 0)
        lax.fori_loop(tiles - LAG, tiles, last_tiles, 0)
        for index in range(2 * tiles):
            tile_copy(index // 2, index % 2).wait_send()

    def horner(index, value):
        return row + (value - times_factor(factor, value))

    value = lax.fori_loop(0, 2 ** (8 - SQUARINGS) - 1, horner, row)

    lanes = out.shape[1]
    for index in range(16):
        pieces[index, :, :lanes] = value[:, index * lanes : (index + 1) * lanes]
        pieces[index, :, lanes:] = jnp.zeros((8, 128 - lanes), jnp.float32)
    copies = []
    for index, peer in enumerate(peers):
        copy = pltpu.make_async_remote_copy(
            src_ref=pieces.at[peer["space"]],
            dst_ref=came.at[chip],
            send_sem=share_send.at[index],
            recv_sem=share_recv.at[index],
            device_id=peer,
            device_id_type=MESH,
        )
        copy.start()
        copies.append(copy)
    came[chip] = pieces[space]
    for copy in copies:
        copy.wait()
    for index in range(8):
        out[index : index + 1, :] = came[index, :1, :lanes]


N_FRONT = 31


def whole_kernel(inv_cells, base, cots, grad, out, factor, *refs):
    operands, shared, rest = refs[:6], refs[6 : 6 + N_FRONT], refs[6 + N_FRONT :]
    inverse = front_part(inv_cells, base, cots, grad, factor, operands[0], *shared)
    poly_part(inverse, shared[1], out, factor, *operands, *rest)


def whole(base, cots, grad, inv_cells, size):
    planes, lines, chans, depth = base.shape
    vmem = pl.BlockSpec(memory_space=pltpu.VMEM)
    lanes = 2 * CH
    tiles = size // TILE
    dma = pltpu.SemaphoreType.DMA
    counts = [HALF, HALF, 3 * SIZES[0], 3 * SIZES[1], 9 * SIZES[0], 9 * SIZES[1], 12 * SIZES[1]]
    front_refs = (
        [
            pltpu.VMEM((ROWS, lanes), jnp.float32),
            pltpu.VMEM((1, size), jnp.float32),
            pltpu.VMEM((planes + 2, lines + 2, chans, depth), jnp.bfloat16),
            pltpu.VMEM((planes + 2, 3 * chans, (lines + 2) * depth), jnp.bfloat16),
            pltpu.VMEM((planes + 2, (lines + 2) * depth, 3 * chans), jnp.bfloat16),
            pltpu.VMEM((ROWS, lanes), jnp.float32),
        ]
        + [pltpu.VMEM((count, lanes), jnp.float32) for count in counts]
        + [pltpu.VMEM((count, CH, lanes), jnp.float32) for count in (5, 10)]
        + [pltpu.VMEM((8, 8, -(-grad.shape[1] // lanes) * lanes), jnp.float32)] * 2
        + [dma((count,)) for count in (8, 8, 3, 3, 27, 27, 18, 18, 12, 12, 10, 10, 7, 7)]
    )
    return pl.pallas_call(
        functools.partial(whole_kernel, inv_cells),
        out_shape=jax.ShapeDtypeStruct((8, grad.shape[1] // 2), jnp.float32),
        in_specs=[vmem] * 3,
        out_specs=vmem,
        scratch_shapes=[pltpu.VMEM((size, size), jnp.float32)]
        + [pltpu.VMEM((size, size), jnp.bfloat16)] * 2
        + [pltpu.VMEM((size, size), EIGHT)] * 4
        + front_refs
        + [pltpu.VMEM((16, 8, 128), jnp.float32), pltpu.VMEM((8, 8, 128), jnp.float32)]
        + [dma((2 * tiles,)), dma((2 * tiles,)), pltpu.SemaphoreType.REGULAR, dma((7,)), dma((7,))],
        compiler_params=pltpu.CompilerParams(
            collective_id=1, has_side_effects=True, vmem_limit_bytes=60 * 2**20
        ),
    )(base, cots, grad)


def body(acts, cotangents, weight_grad):
    chans, block_x, block_y, depth_z = acts.shape
    c_out = cotangents.shape[0]
    width = 27 * chans
    n_space = lax.axis_size("space")
    n_own = lax.axis_size("own")
    inv_cells = 1.0 / (block_x * n_space * block_y * n_own * depth_z)
    size = -(-width // TILE) * TILE
    base = jnp.transpose(acts, (1, 2, 0, 3))
    return whole(base, cotangents.reshape(c_out, -1), weight_grad, inv_cells, size)


def solution(mesh):
    in_specs = (P(None, "space", "own", None), P(None, "space", "own", None), P(None, "own"))
    out_specs = P("own", "space")
    return jax.shard_map(body, mesh=mesh, in_specs=in_specs, out_specs=out_specs, check_vma=False)
```

```python
import functools

import jax
import jax.numpy as jnp
from jax import lax
from jax.experimental import pallas as pl
from jax.experimental.pallas import tpu as pltpu
from jax.sharding import PartitionSpec as P

SQUARINGS = 4
TILE = 256
EIGHT = jnp.float8_e4m3fn
COARSE = 2.0**8
FINE = 2.0**17
LAG = 4
CH = 64
NZ = 256
damping = 0.05
MESH = pl.DeviceIdType.MESH
SAME = ((0, 0), (1, 1), (2, 2))
UP = ((0, 1), (0, 2))
DOWN = ((1, 0), (2, 0))


def pair_type(first, second):
    if first == second:
        return (first, second)
    apart = second - first
    return (0, apart) if apart > 0 else (-apart, 0)


def distinct_pairs():
    pairs = []
    for x_pair in SAME + UP:
        for y_pair in SAME + UP + (DOWN if x_pair in UP else ()):
            full = x_pair in UP or y_pair in UP
            pairs.append((x_pair, y_pair, SAME + UP + (DOWN if full else ())))
    return pairs


PAIRS = distinct_pairs()
SLOTS = {}
for _x_pair, _y_pair, _z_pairs in PAIRS:
    for _z_pair in _z_pairs:
        SLOTS[(_x_pair, _y_pair, _z_pair)] = len(SLOTS)
N_SLOTS = 192
ROWS = N_SLOTS // 2 * CH


def slot_place(slot):
    return slice(slot // 2 * CH, slot // 2 * CH + CH), slice(slot % 2 * CH, slot % 2 * CH + CH)


def block_slot(row, col):
    return SLOTS[
        tuple(
            pair_type(row // unit % 3, col // unit % 3) for unit in (9, 3, 1)
        )
    ]


DIAGONAL = {block_slot(index, index) for index in range(27)}


def row_peers(space, own):
    return [{"space": lax.rem(space + 2 * step, 16), "own": own} for step in range(1, 8)]


def meet(peers):
    barrier = pltpu.get_barrier_semaphore()
    for peer in peers:
        pl.semaphore_signal(barrier, inc=1, device_id=peer, device_id_type=MESH)
    pl.semaphore_wait(barrier, len(peers))


def inverse_columns(matrix, first, apart):
    size = matrix.shape[0]
    lane = lax.broadcasted_iota(jnp.int32, (size, 128), 1)
    sub = lax.broadcasted_iota(jnp.int32, (size, 128), 0)
    wanted = (lane >= size) & (lane < size + 8) & (sub == first + apart * (lane - size))
    work = jnp.where(lane < size, matrix, jnp.where(wanted, 1.0, 0.0))
    for step in range(size):
        pivot = work[step : step + 1, :] / work[step : step + 1, step : step + 1]
        work = jnp.where(sub == step, pivot, work - work[:, step : step + 1] * pivot)
    return [work[:, size + index : size + index + 1] for index in range(8)]


HALF = ROWS // 2
PART = HALF // 3
SLOTS_PER_PART = N_SLOTS // 3
SIZES = (PART // 4, PART // 16)


def front_part(
    inv_cells, base, cots, grad, factor, high, full, row_out,
    ext, left, right, terms, half, from_core, sums_1, sums_2, came_0, came_1, came_2, g_sum, g_came, products, shares,
    halo_send, halo_recv, core_send, core_recv, ring_send, ring_recv, back_send, back_recv,
    last_send, last_recv, g_send, g_recv, w_send, w_recv,
):
    space, own = lax.axis_index("space"), lax.axis_index("own")
    n_space, n_own = lax.axis_size("space"), lax.axis_size("own")
    core, ypos, z_lo = lax.rem(space, 2), lax.rem(space // 2, 4), space // 8
    xpos, z_hi = lax.rem(own, 4), own // 4
    coords = (xpos, ypos, z_hi * 2 + z_lo)
    planes, lines, chans, depth = base.shape
    lanes = grad.shape[1]

    def peer(axis, coord):
        if axis == 0:
            return {"space": space, "own": own - xpos + coord}
        if axis == 1:
            return {"space": space + 2 * (coord - ypos), "own": own}
        return {"space": space + 8 * (lax.rem(coord, 2) - z_lo), "own": coord // 2 * 4 + xpos}

    partner = {"space": space + 1 - 2 * core, "own": own}
    ring = {
        (axis, step): peer(axis, lax.rem(coords[axis] + step, 4)) for axis in range(3) for step in (1, 2, 3)
    }
    owners = [{"space": space, "own": lax.rem(own + step, n_own)} for step in range(1, n_own)]
    steps = [(dx, dy) for dx in (-1, 0, 1) for dy in (-1, 0, 1) if dx or dy]
    around = [
        {"space": lax.rem(space + dx + n_space, n_space), "own": lax.rem(own + dy + n_own, n_own)}
        for dx, dy in steps
    ]
    ext[1 : 1 + planes, 1 : 1 + lines] = base[...]
    products[...] = jnp.zeros_like(products)
    meet([partner] + list(ring.values()) + owners + around + row_peers(space, own))

    def rows(start, count):
        return pl.ds(pl.multiple_of(start, 8), count)

    waiting = []

    def send(src, dst, send_sem, recv_sem, device):
        copy = pltpu.make_async_remote_copy(
            src_ref=src, dst_ref=dst, send_sem=send_sem, recv_sem=recv_sem, device_id=device, device_id_type=MESH
        )
        copy.start()
        waiting.append(copy)
        return copy

    def ends(step, count):
        if step == 0:
            return pl.ds(1, count), pl.ds(1, count)
        return (pl.ds(count, 1), pl.ds(0, 1)) if step > 0 else (pl.ds(1, 1), pl.ds(count + 1, 1))

    halo = []
    for index, (dx, dy) in enumerate(steps):
        (from_x, to_x), (from_y, to_y) = ends(dx, planes), ends(dy, lines)
        halo.append(
            send(ext.at[from_x, from_y], ext.at[to_x, to_y], halo_send.at[index], halo_recv.at[index], around[index])
        )

    lane = lax.broadcasted_iota(jnp.int32, (chans, depth), 1)

    def shift_line(x, y):
        here = ext[x, y].astype(jnp.float32)
        before = jnp.where(lane == 0, 0.0, pltpu.roll(here, 1, 1))
        after = jnp.where(lane == depth - 1, 0.0, pltpu.roll(here, depth - 1, 1))
        stack = jnp.concatenate([before, here, after], axis=0)
        across = slice(y * depth, (y + 1) * depth)
        left[x, :, across] = stack.astype(left.dtype)
        right[x, across, :] = stack.T.astype(right.dtype)

    def shift_lines(x, ys):
        for y in ys:
            shift_line(x, y)

    def inner_plane(x, carry):
        shift_lines(x, range(1, lines + 1))
        return carry

    def edge_lines(x, carry):
        shift_lines(x, (0, lines + 1))
        return carry

    def outer_plane(index, carry):
        shift_lines(index * (planes + 1), range(lines + 2))
        return carry

    g_sum[0] = jnp.zeros_like(g_sum[0])
    g_sum[0, :, :chans] = lax.dot_general(
        cots[...], cots[...], (((1,), (1,)), ((), ())), preferred_element_type=jnp.float32
    )
    g_copies = [send(g_sum.at[0], g_came.at[0], g_send.at[0], g_recv.at[0], partner)]
    lax.fori_loop(1, planes + 1, inner_plane, 0)
    for copy in halo:
        copy.wait()
    del waiting[: len(halo)]

    @pl.when(space == 0)
    def _():
        ext[0] = jnp.zeros_like(ext[0])

    @pl.when(space == n_space - 1)
    def _():
        ext[planes + 1] = jnp.zeros_like(ext[0])

    @pl.when(own == 0)
    def _():
        ext[:, 0] = jnp.zeros_like(ext[:, 0])

    @pl.when(own == n_own - 1)
    def _():
        ext[:, lines + 1] = jnp.zeros_like(ext[:, 0])

    lax.fori_loop(1, planes + 1, edge_lines, 0)
    lax.fori_loop(0, 2, outer_plane, 0)

    levels = (half, sums_1, sums_2)
    came = (came_0, came_1)
    flights, back, to_core = {}, {}, {}

    def exchange(part):
        to_core[part] = send(
            terms.at[rows(part * 2 * PART + (1 - core) * PART, PART)],
            from_core.at[rows(part * PART, PART)],
            core_send.at[part], core_recv.at[part], partner,
        )

    def scatter(level, part):
        axis, count = (part + level) % 3, SIZES[level]
        for step in (1, 2, 3):
            target = lax.rem(coords[axis] + step, 4)
            slot = part * 3 + step - 1
            flights[(level, part, step)] = send(
                levels[level].at[rows(part * count * 4 + target * count, count)],
                came[level].at[rows(slot * count, count)],
                ring_send.at[level * 9 + slot], ring_recv.at[level * 9 + slot], ring[(axis, step)],
            )

    def merge(part):
        to_core[part].wait_recv()
        here = rows(part * PART, PART)
        half[here, :] = terms[rows(part * 2 * PART + core * PART, PART), :] + from_core[here, :]
        scatter(0, part)

    def collect(level, part):
        axis, count = (part + level) % 3, SIZES[level]
        total = levels[level][rows(part * count * 4 + coords[axis] * count, count), :]
        for step in (1, 2, 3):
            flights[(level, part, step)].wait_recv()
            total = total + came[level][rows((part * 3 + step - 1) * count, count), :]
        levels[level + 1][rows(part * count, count), :] = total
        if level == 0:
            scatter(1, part)
        else:
            swap(part)

    def swap(part):
        axis, count = (part + 2) % 3, SIZES[1]
        mine = rows((part * 4 + coords[axis]) * count, count)
        for step in (1, 2, 3):
            slot = 18 + part * 3 + step - 1
            flights[(2, part, step)] = send(
                sums_2.at[rows(part * count, count)], came_2.at[mine], ring_send.at[slot], ring_recv.at[slot],
                ring[(axis, step)],
            )
        came_2[mine, :] = sums_2[rows(part * count, count), :]

    def settle(part):
        count = SIZES[1]
        for step in (1, 2, 3):
            flights[(2, part, step)].wait_recv()
        total = came_2[rows(part * 4 * count, count), :]
        for coord in (1, 2, 3):
            total = total + came_2[rows((part * 4 + coord) * count, count), :]
        full[rows(start(2, part), count), :] = total
        spread(1, part)

    def send_g(stage, source, devices):
        return [
            send(source, g_came.at[stage + index], g_send.at[stage + index], g_recv.at[stage + index], device)
            for index, device in enumerate(devices)
        ]

    def add_g(stage, value, copies, target):
        for index, copy in enumerate(copies):
            copy.wait_recv()
            value = value + g_came[stage + index]
        g_sum[target] = value

    run = lines * depth
    done = 0
    started = 0
    for x_pair, y_pair, z_pairs in PAIRS:
        total = None
        for x in range(planes):
            term = jnp.dot(
                left[x + x_pair[0], :, y_pair[0] * depth : y_pair[0] * depth + run],
                right[x + x_pair[1], y_pair[1] * depth : y_pair[1] * depth + run, :],
                preferred_element_type=jnp.float32,
            )
            total = term if total is None else total + term
        for z_pair in z_pairs:
            block = total[z_pair[0] * chans : (z_pair[0] + 1) * chans, z_pair[1] * chans : (z_pair[1] + 1) * chans]
            terms[slot_place(SLOTS[(x_pair, y_pair, z_pair)])] = block
            done += 1
        if done >= (started + 1) * SLOTS_PER_PART:
            exchange(started)
            if started:
                merge(started - 1)
            started += 1
    for slot in range(done, N_SLOTS):
        terms[slot_place(slot)] = jnp.zeros((chans, chans), jnp.float32)
    exchange(2)
    merge(1)
    merge(2)
    add_g(0, g_sum[0], g_copies, 1)
    g_copies = send_g(1, g_sum.at[1], [ring[(0, step)] for step in (1, 2, 3)])
    collect(0, 0)
    collect(0, 1)
    collect(0, 2)
    add_g(1, g_sum[1], g_copies, 2)
    g_copies = send_g(4, g_sum.at[2], [ring[(1, step)] for step in (1, 2, 3)])
    collect(1, 0)
    collect(1, 1)
    collect(1, 2)
    add_g(4, g_sum[2], g_copies, 3)
    g_copies = send_g(7, g_sum.at[3], [ring[(2, step)] for step in (1, 2, 3)])

    def start(level, part):
        first = part * 2 * PART + core * PART
        for outer in range(level):
            first = first + coords[(part + outer) % 3] * SIZES[outer]
        return first

    def forward(part, index, coord):
        here = rows(start(0, part) + coord * SIZES[0], SIZES[0])
        slot = part * 4 + index
        back[(part, index)] = send(full.at[here], full.at[here], last_send.at[slot], last_recv.at[slot], partner)

    def spread(level, part):
        axis, count = (part + level) % 3, SIZES[level]
        here = rows(start(level, part) + coords[axis] * count, count)
        for step in (1, 2, 3):
            slot = level * 9 + part * 3 + step - 1
            back[(level, part, step)] = send(
                full.at[here], full.at[here], back_send.at[slot], back_recv.at[slot], ring[(axis, step)]
            )
        if level == 0:
            forward(part, 0, coords[axis])

    def gathered(level, part):
        axis = (part + level) % 3
        for step in (1, 2, 3):
            back[(level, part, step)].wait_recv()
            if level == 0:
                forward(part, step, lax.rem(coords[axis] + 4 - step, 4))
        if level:
            spread(level - 1, part)

    for part in range(3):
        settle(part)
    add_g(7, g_sum[3], g_copies, 4)
    diagonal = lax.broadcasted_iota(jnp.int32, (CH, 2 * CH), 0) == lax.broadcasted_iota(jnp.int32, (CH, 2 * CH), 1)
    g_factor = g_sum[4] * inv_cells + jnp.where(diagonal, damping, 0.0)
    for owner, weights in enumerate(inverse_columns(g_factor, space // 2, 8)):
        products[owner, :1, :lanes] = jnp.sum(grad[...] * weights, axis=0, keepdims=True)
    to_owners = [
        send(products.at[owner["own"]], shares.at[own], w_send.at[index], w_recv.at[index], owner)
        for index, owner in enumerate(owners)
    ]
    shares[own] = products[own]
    for part in range(3):
        gathered(1, part)
    for part in range(3):
        gathered(0, part)
    eye = jnp.where(
        lax.broadcasted_iota(jnp.int32, (CH, CH), 0) == lax.broadcasted_iota(jnp.int32, (CH, CH), 1), damping, 0.0
    )
    clear_margin(factor, high)
    squares = jnp.zeros((CH, CH), jnp.float32)
    for part in range(3):
        for index in range(4):
            back[(part, index)].wait_recv()
        squares = squares + assemble(part, full, inv_cells, eye, factor, high)
    mirror(factor, high)
    for copy in to_owners:
        copy.wait_recv()
    row_out[...] = jnp.zeros_like(row_out)
    for owner in range(n_own):
        row_out[:, owner * lanes : (owner + 1) * lanes] = shares[owner, :1, :lanes]
    for copy in waiting:
        copy.wait_send()
    return 1.0 / jnp.sqrt(jnp.sum(squares, keepdims=True))


def times_block(rows, row):
    count, size = rows.shape
    rows = rows.reshape(count // 8, 8, size)
    total = jnp.zeros((count // 8, 8, 128), jnp.float32)
    for lane in range(0, size, 128):
        total = total + rows[:, :, lane : lane + 128] * row[None, :, lane : lane + 128]
    flipped = total.reshape(count, 128).T
    return jnp.broadcast_to(jnp.sum(flipped, axis=0, keepdims=True), (8, count))


def times_factor(factor, row):
    size, width = factor.shape[0], 27 * CH
    parts = [
        times_block(factor[pl.ds(base, min(128, width - base)), :], row) for base in range(0, width, 128)
    ]
    return jnp.concatenate(parts + [jnp.zeros((8, size - width), jnp.float32)], axis=1)


def store_split(here, value, high, coarse, fine):
    top = value.astype(high.dtype)
    high[here] = top
    top = top.astype(jnp.float32)
    coarse[here] = (top * COARSE).astype(coarse.dtype)
    fine[here] = ((value - top) * FINE).astype(fine.dtype)


def put(rows, cols, value, factor, high):
    factor[rows, cols] = value
    high[rows, cols] = value.astype(high.dtype)


def clear_margin(*refs):
    size, width = refs[0].shape[0], 27 * CH
    for ref in refs:
        ref[width:, :] = jnp.zeros((size - width, size), ref.dtype)
        ref[:, width:] = jnp.zeros((size, size - width), ref.dtype)


def assemble(part, full, inv_cells, eye, *refs):
    places = {}
    for row in range(27):
        for col in range(row, 27):
            slot = block_slot(row, col)
            if slot // SLOTS_PER_PART == part:
                places.setdefault(slot, []).append((row, col))
    squares = jnp.zeros((CH, CH), jnp.float32)
    for slot, pairs in places.items():
        block = full[slot_place(slot)] * inv_cells
        if slot in DIAGONAL:
            block = block + eye
        squares = squares + float(sum(1 if row == col else 2 for row, col in pairs)) * (block * block)
        for row, col in pairs:
            rows, cols = slice(row * CH, (row + 1) * CH), slice(col * CH, (col + 1) * CH)
            put(rows, cols, block, *refs)
            if row != col and row * CH // TILE == col * CH // TILE:
                put(cols, rows, block.T, *refs)
    return squares


def mirror(factor, *refs):
    tiles = factor.shape[0] // TILE
    for row in range(tiles):
        for col in range(row + 1, tiles):
            rows, cols = slice(row * TILE, (row + 1) * TILE), slice(col * TILE, (col + 1) * TILE)
            put(cols, rows, factor[rows, cols].T, factor, *refs)


def poly_part(
    lanes, inverse, row_ref, out, factor, high_a, high_b, coarse_a, fine_a, coarse_b, fine_b, pieces, came,
    tile_send, tile_recv, ready, share_send, share_recv,
):
    space, own = lax.axis_index("space"), lax.axis_index("own")
    core, chip = lax.rem(space, 2), space // 2
    partner = {"space": space + 1 - 2 * core, "own": own}
    peers = row_peers(space, own)
    size = factor.shape[0]
    tiles = size // TILE
    row = jnp.broadcast_to(row_ref[...], (8, size)) * inverse
    dot = functools.partial(jnp.dot, preferred_element_type=jnp.float32)
    operands = ((high_a, coarse_a, fine_a), (high_b, coarse_b, fine_b))

    def place(i, half, which):
        first = lax.rem(i + tiles - 1, tiles)
        j = lax.rem(first + 2 * half + 1, tiles)
        return (
            pl.ds(pl.multiple_of(lax.rem(first + which, tiles) * TILE, TILE), TILE),
            pl.ds(pl.multiple_of(j * TILE, TILE), TILE),
        )

    def tile_copy(i, which):
        here = factor.at[place(i, core, which)]
        return pltpu.make_async_remote_copy(
            src_ref=here,
            dst_ref=here,
            send_sem=tile_send.at[2 * i + which],
            recv_sem=tile_recv.at[2 * i + which],
            device_id=partner,
            device_id_type=MESH,
        )

    for step in range(SQUARINGS):
        now, later = operands[step % 2], operands[1 - step % 2]
        applied = times_factor(factor, row)
        row = 2.0 * row - (applied if step else applied * inverse)
        pl.semaphore_signal(ready, inc=1, device_id=partner, device_id_type=MESH)

        def finish(i, half, which, fresh, step=step, later=later):
            rows, cols = place(i, half, which)
            flipped = fresh.T
            if which == 1:
                flipped = jnp.where(half == 0, fresh, flipped)
            factor[cols, rows] = flipped
            if step < SQUARINGS - 1:
                store_split((rows, cols), fresh, *later)
                store_split((cols, rows), flipped, *later)

        def product(rows, cols, step=step, now=now):
            high, coarse, fine = now
            square = dot(high[rows, :], high[:, cols])
            if step:
                cross = dot(coarse[rows, :], fine[:, cols]) + dot(fine[rows, :], coarse[:, cols])
                square = square + cross * (1.0 / (COARSE * FINE))
            return square

        def renew(i, which, square, step=step, finish=finish):
            here = place(i, core, which)
            if step:
                fresh = 2.0 * factor[here] - square
            else:
                fresh = (2.0 * inverse) * factor[here] - (inverse * inverse) * square
            factor[here] = fresh
            finish(i, core, which, fresh)

        def compute(i, product=product, renew=renew):
            cols = place(i, core, 0)[1]
            square = product(pl.ds(pl.multiple_of((i - 1) * TILE, TILE), 2 * TILE), cols)
            renew(i, 0, square[:TILE])
            renew(i, 1, square[TILE:])

        def adopt(i, finish=finish):
            for which in range(2):
                finish(i, 1 - core, which, factor[place(i, 1 - core, which)])

        def send_tiles(i):
            for which in range(2):
                tile_copy(i, which).start()

        def first_tiles(i, carry, compute=compute):
            compute(i)
            send_tiles(i)
            return carry

        def next_tiles(i, carry, compute=compute, adopt=adopt):
            for which in range(2):
                tile_copy(i - LAG, which).wait_recv()
            adopt(i - LAG)
            compute(i)
            send_tiles(i)
            return carry

        def last_tiles(i, carry, adopt=adopt):
            for which in range(2):
                tile_copy(i, which).wait_recv()
            adopt(i)
            return carry

        for which in range(2):
            renew(0, which, product(*place(0, core, which)))
        pl.semaphore_wait(ready, 1)
        send_tiles(0)
        lax.fori_loop(1, LAG, first_tiles, 0)
        lax.fori_loop(LAG, tiles, next_tiles, 0)
        lax.fori_loop(tiles - LAG, tiles, last_tiles, 0)
        for index in range(2 * tiles):
            tile_copy(index // 2, index % 2).wait_send()

    def horner(index, value):
        return row + (value - times_factor(factor, value))

    value = lax.fori_loop(0, 2 ** (8 - SQUARINGS) - 1, horner, row)

    for index in range(16):
        pieces[index, :, :lanes] = value[:, index * lanes : (index + 1) * lanes]
        pieces[index, :, lanes:] = jnp.zeros((8, 128 - lanes), jnp.float32)
    copies = []
    for index, peer in enumerate(peers):
        copy = pltpu.make_async_remote_copy(
            src_ref=pieces.at[peer["space"]],
            dst_ref=came.at[chip],
            send_sem=share_send.at[index],
            recv_sem=share_recv.at[index],
            device_id=peer,
            device_id_type=MESH,
        )
        copy.start()
        copies.append(copy)
    came[chip] = pieces[space]
    for copy in copies:
        copy.wait()
    for index in range(8):
        out[index : index + 1, :] = came[index, :1, :]


N_FRONT = 31


def whole_kernel(inv_cells, base, cots, grad, out, factor, *refs):
    operands, shared, rest = refs[:6], refs[6 : 6 + N_FRONT], refs[6 + N_FRONT :]
    inverse = front_part(inv_cells, base, cots, grad, factor, operands[0], *shared)
    poly_part(grad.shape[1] // 2, inverse, shared[1], out, factor, *operands, *rest)


def whole(base, cots, grad, inv_cells, size):
    planes, lines, chans, depth = base.shape
    vmem = pl.BlockSpec(memory_space=pltpu.VMEM)
    lanes = 2 * CH
    tiles = size // TILE
    dma = pltpu.SemaphoreType.DMA
    counts = [HALF, HALF, 3 * SIZES[0], 3 * SIZES[1], 9 * SIZES[0], 9 * SIZES[1], 12 * SIZES[1]]
    front_refs = (
        [
            pltpu.VMEM((ROWS, lanes), jnp.float32),
            pltpu.VMEM((1, size), jnp.float32),
            pltpu.VMEM((planes + 2, lines + 2, chans, depth), jnp.bfloat16),
            pltpu.VMEM((planes + 2, 3 * chans, (lines + 2) * depth), jnp.bfloat16),
            pltpu.VMEM((planes + 2, (lines + 2) * depth, 3 * chans), jnp.bfloat16),
            pltpu.VMEM((ROWS, lanes), jnp.float32),
        ]
        + [pltpu.VMEM((count, lanes), jnp.float32) for count in counts]
        + [pltpu.VMEM((count, CH, lanes), jnp.float32) for count in (5, 10)]
        + [pltpu.VMEM((8, 8, -(-grad.shape[1] // lanes) * lanes), jnp.float32)] * 2
        + [dma((count,)) for count in (8, 8, 3, 3, 27, 27, 18, 18, 12, 12, 10, 10, 7, 7)]
    )
    return pl.pallas_call(
        functools.partial(whole_kernel, inv_cells),
        out_shape=jax.ShapeDtypeStruct((8, lanes), jnp.float32),
        in_specs=[vmem] * 3,
        out_specs=vmem,
        scratch_shapes=[pltpu.VMEM((size, size), jnp.float32)]
        + [pltpu.VMEM((size, size), jnp.bfloat16)] * 2
        + [pltpu.VMEM((size, size), EIGHT)] * 4
        + front_refs
        + [pltpu.VMEM((16, 8, 128), jnp.float32), pltpu.VMEM((8, 8, 128), jnp.float32)]
        + [dma((2 * tiles,)), dma((2 * tiles,)), pltpu.SemaphoreType.REGULAR, dma((7,)), dma((7,))],
        compiler_params=pltpu.CompilerParams(
            collective_id=1, has_side_effects=True, vmem_limit_bytes=60 * 2**20
        ),
    )(base, cots, grad)


def body(acts, cotangents, weight_grad):
    chans, block_x, block_y, depth_z = acts.shape
    c_out = cotangents.shape[0]
    width = 27 * chans
    n_space = lax.axis_size("space")
    n_own = lax.axis_size("own")
    inv_cells = 1.0 / (block_x * n_space * block_y * n_own * depth_z)
    size = -(-width // TILE) * TILE
    base = jnp.transpose(acts, (1, 2, 0, 3))
    return whole(base, cotangents.reshape(c_out, -1), weight_grad, inv_cells, size)[:, : weight_grad.shape[1] // 2]


def solution(mesh):
    in_specs = (P(None, "space", "own", None), P(None, "space", "own", None), P(None, "own"))
    out_specs = P("own", "space")
    return jax.shard_map(body, mesh=mesh, in_specs=in_specs, out_specs=out_specs, check_vma=False)
```
